32 devices in a mesh: dp: 8 (over z, y), layer: 4 (over x, core).
Axes of the slice: x: 2, y: 2, z: 4, core: 2. Of those that a mesh axis runs over, the one named last changes fastest.
Arguments:
- inputs: bfloat16 [32768, 640], P(('dp', 'layer')), may hold values from -6 to 6
- encoder_out: bfloat16 [4, 32768, 640], P('layer', 'dp'), may hold values from -6 to 6
- query_self: bfloat16 [640, 640], replicated, may hold values from -0.25 to 0.25
- key_self: bfloat16 [640, 640], replicated, may hold values from -0.25 to 0.25
- value_self: bfloat16 [640, 640], replicated, may hold values from -0.25 to 0.25
- out_self: bfloat16 [640, 640], replicated, may hold values from -0.5 to 0.5
- query_cross: bfloat16 [640, 640], replicated, may hold values from -0.25 to 0.25
- key_cross: bfloat16 [640, 640], replicated, may hold values from -0.25 to 0.25
- value_cross: bfloat16 [640, 640], replicated, may hold values from -0.25 to 0.25
- out_cross: bfloat16 [640, 640], replicated, may hold values from -0.5 to 0.5
- feed_up: bfloat16 [640, 3072], replicated, may hold values from -0.25 to 0.25
- feed_down: bfloat16 [3072, 640], replicated, may hold values from -0.15625 to 0.15625
- gain_self: float32 [640], replicated, may hold values from 0.25 to 1.75
- gain_cross: float32 [640], replicated, may hold values from 0.25 to 1.75
- gain_feed: float32 [640], replicated, may hold values from 0.25 to 1.75
- seg_target: int32 [128, 256], P(('dp', 'layer')), may hold values from 0 to 7, never falling along the last dimension, each value on 1 to 64 neighbouring positions
- seg_source: int32 [128, 256], P(('dp', 'layer')), may hold values from 0 to 7, never falling along the last dimension, each value on 1 to 64 neighbouring positions
- subnet_of_row: int32 [128], P('dp'), may hold values from 0 to 5
- chosen_layers: int32 [6, 2], replicated, may hold values from 0 to 3, all different within a row
- out_grad: bfloat16 [32768, 640], P(('dp', 'layer')), may hold values from -6 to 6
Outputs:
- layer_out: bfloat16 [32768, 640], P(('dp', 'layer'))
- input_grad: bfloat16 [32768, 640], P(('dp', 'layer'))
- encoder_grad: float32 [4, 32768, 640], P('layer', 'dp')
- grad_query_self: float32 [640, 640], P('dp')
- grad_key_self: float32 [640, 640], P('dp')
- grad_value_self: float32 [640, 640], P('dp')
- grad_out_self: float32 [640, 640], P('dp')
- grad_query_cross: float32 [640, 640], P('dp')
- grad_key_cross: float32 [640, 640], P('dp')
- grad_value_cross: float32 [640, 640], P('dp')
- grad_out_cross: float32 [640, 640], P('dp')
- grad_feed_up: float32 [640, 3072], P('dp')
- grad_feed_down: float32 [3072, 640], P('dp')
- grad_gain_self: float32 [640], P('dp')
- grad_gain_cross: float32 [640], P('dp')
- grad_gain_feed: float32 [640], P('dp')
The draws below stay inside these ranges and needn't reach their ends.
Inputs may be any that keep to these rules, and one draw needn't show every extreme that they name: `seg_target`: each row holds 8 sentences numbered in order, each of 1 to 64 tokens, one of exactly 64. `seg_source`: each row holds 8 sentences numbered in order, each of 1 to 64 tokens, one of exactly 64. `chosen_layers`: each sub-net names 2 different encoder layers; every layer is named by some sub-net.
All inputs are finite; a program needn't handle non-finite values.
Results may differ from the reference program's by a relative error of at most 0.018.
Values may be sent and summed in bfloat16 or wider, within the bound.
No kernel may reach another device: no remote copies, remote signals or barrier semaphores. Data moves between devices by JAX's collectives and lax.ppermute only.
A program may use at most 192 MiB of HBM per device.

```python
import math
import jax
import jax.numpy as jnp
import numpy as np
from jax import lax

D = 640
HEADS = 8
HEAD = 80
FF = 3072
ROW_LEN = 256
SEGS = 8
SEG_MOST = 64
SUBNETS = 6
PICK = 2
ENC = 4
TOKENS = 32768
ROWS = 128


def plant(values, rng, least, largest):
    place = [jax.random.randint(jax.random.fold_in(rng, axis), (), 0, length) for axis, length in enumerate(values.shape)]
    main_axis = values.shape.index(max(values.shape))
    neighbour = place[:main_axis] + [(place[main_axis] + 1) % values.shape[main_axis]] + place[main_axis + 1:]
    return values.at[tuple(place)].set(least).at[tuple(neighbour)].set(largest)


def spiked(drawn, key, source, target, parts, factor):
    owner, partner = [(jnp.arange(drawn.shape[axis_at]) // (drawn.shape[axis_at] // parts)).reshape([-1 if axis == axis_at else 1 for axis in range(drawn.ndim)]) for axis_at in (source, target)]
    chosen = jax.random.permutation(key, parts)[partner]
    strong = (owner == chosen) | (owner == (partner + parts // 2) % parts)
    return jnp.where(strong, factor * drawn, drawn)


def block_scale(key, shape, cuts, least, largest):
    level, own = 1.0, jax.random.fold_in(key, 6)
    for position, shards_of in cuts:
        heights = jnp.exp(jax.random.uniform(jax.random.fold_in(own, position), (shards_of,), jnp.float32, least / len(cuts), largest / len(cuts)))
        level = level * jnp.repeat(heights, shape[position] // shards_of).reshape([-1 if axis == position else 1 for axis in range(len(shape))])
    return level


def choose_distinct(own_key, rows, amount, top, lift):
    sequence = jax.random.permutation(jax.random.fold_in(own_key, 1), amount)
    boost = sequence
    for power in range(3):
        boost = boost * boost // amount
    boost = boost * lift // amount
    lots = jax.random.randint(jax.random.fold_in(own_key, 2), (rows, amount), 0, 4096) + boost
    sure = jax.random.permutation(jax.random.fold_in(own_key, 3), rows)[jnp.arange(amount) % rows]
    lots = jnp.where(jnp.arange(rows)[:, None] == sure[None, :], 1 << 14, lots)
    merit = lots * amount + jnp.arange(amount)
    return lax.top_k(merit.astype(jnp.int32), top)[1].astype(jnp.int32)


def length_profile(amount, total, bound, slope):
    loads = [(1 << 20) // math.isqrt(rank ** slope) + 1 for rank in range(2, amount + 1)]
    rest, holding = total - bound - (amount - 1), [1] * (amount - 1)
    while rest > 0:
        movable = [i for i in range(amount - 1) if holding[i] < bound]
        mass, remaining = sum([loads[i] for i in movable]), rest
        for i in movable:
            more = min(bound - holding[i], max(1, remaining * loads[i] // mass), rest)
            holding[i] = holding[i] + more
            rest = rest - more
    return np.array([bound] + holding)


def uneven(own_key, count, total, most, lean):
    if count == 2:
        one = jax.random.randint(own_key, (), max(1, total - most), min(most, total - 1) + 1)
        return jnp.stack([one, total - one])
    sizes = jnp.asarray(length_profile(count, total, most, lean), jnp.int32)
    couples = (count - 1) // 2
    giver, sink = sizes[1:1 + 2 * couples:2], sizes[2:2 + 2 * couples:2]
    room = jnp.minimum(giver - 1, most - sink)
    moved = jax.random.randint(jax.random.fold_in(own_key, 1), (couples,), 0, 1 << 20) % (room + 1)
    sizes = sizes.at[1:1 + 2 * couples:2].set(giver - moved).at[2:2 + 2 * couples:2].set(sink + moved)
    return sizes[jax.random.permutation(jax.random.fold_in(own_key, 2), count)]


def normal_values(rng, extent, scale, most, split=(), dtype=jnp.bfloat16):
    values = jax.random.normal(rng, extent, jnp.float32) * scale
    if len(split) > 0:
        values = block_scale(rng, extent, split, -0.22, 0.18) * values
    return jnp.clip(values, min=-most, max=most).astype(dtype)


def gaussian_with(own_key, extent, scale, bound, cuts, heavy, kind=jnp.bfloat16):
    entries = scale * jax.random.normal(own_key, extent, jnp.float32)
    if cuts:
        entries = entries * block_scale(own_key, extent, cuts, -0.22, 0.18)
    return jnp.clip(spiked(entries, jax.random.fold_in(own_key, 3), *heavy), -bound, bound).astype(kind)


def setup_inputs(seed: int = 0) -> dict:
    key_of = jax.random.split(jax.random.key(seed), 21)
    return {
        "inputs": gaussian_with(key_of[0], (TOKENS, D), 1.0, 6.0, ((0, 32),), (0, 1, 32, 2.75)),
        "encoder_out": normal_values(key_of[1], (ENC, TOKENS, D), 1.0, 6.0, ((0, 4), (1, 8))),
        "query_self": normal_values(key_of[2], (D, D), D ** -0.5, 0.25),
        "key_self": normal_values(key_of[3], (D, D), D ** -0.5, 0.25),
        "value_self": normal_values(key_of[4], (D, D), D ** -0.5, 0.25),
        "out_self": normal_values(key_of[5], (D, D), (D // 4) ** -0.5, 0.5),
        "query_cross": normal_values(key_of[6], (D, D), D ** -0.5, 0.25),
        "key_cross": normal_values(key_of[7], (D, D), D ** -0.5, 0.25),
        "value_cross": normal_values(key_of[8], (D, D), D ** -0.5, 0.25),
        "out_cross": normal_values(key_of[9], (D, D), (D // 5) ** -0.5, 0.5),
        "feed_up": normal_values(key_of[10], (D, FF), D ** -0.5, 0.25),
        "feed_down": normal_values(key_of[11], (FF, D), (FF // 2) ** -0.5, 0.15625),
        "gain_self": jnp.clip(1.0 + 0.15 * jax.random.normal(key_of[12], (D,), jnp.float32), 0.25, 1.75),
        "gain_cross": jnp.clip(1.0 + 0.15 * jax.random.normal(key_of[13], (D,), jnp.float32), 0.25, 1.75),
        "gain_feed": jnp.clip(1.0 + 0.15 * jax.random.normal(key_of[14], (D,), jnp.float32), 0.25, 1.75),
        "seg_target": jax.vmap(lambda own: jnp.searchsorted(jnp.cumsum(uneven(own, SEGS, ROW_LEN, SEG_MOST, 1)), jnp.arange(ROW_LEN), side="right"))(jax.random.split(key_of[15], ROWS)).reshape((ROWS, ROW_LEN)).astype(jnp.int32),
        "seg_source": jax.vmap(lambda own: jnp.searchsorted(jnp.cumsum(uneven(own, SEGS, ROW_LEN, SEG_MOST, 1)), jnp.arange(ROW_LEN), side="right"))(jax.random.split(key_of[16], ROWS)).reshape((ROWS, ROW_LEN)).astype(jnp.int32),
        "subnet_of_row": plant(jax.random.randint(key_of[17], (ROWS,), 0, SUBNETS), jax.random.fold_in(key_of[17], 1), 0, SUBNETS - 1).astype(jnp.int32),
        "chosen_layers": choose_distinct(key_of[18], SUBNETS, ENC, PICK, 4096),
        "out_grad": gaussian_with(key_of[19], (TOKENS, D), 1.0, 6.0, ((0, 32),), (0, 1, 32, 2.75)),
    }


@jax.custom_vjp
def low(v):
    return lax.optimization_barrier(v.astype(jnp.bfloat16)).astype(jnp.float32)

@jax.custom_vjp
def low_back(v):
    return v

def low_keep(v):
    return (low(v), None)

def low_pass(kept, grad):
    return (grad,)

def back_keep(v):
    return (v, None)

def back_low(kept, grad):
    return (low(grad),)
low.defvjp(low_keep, low_pass)
low_back.defvjp(back_keep, back_low)

def matmul(left, right):
    return jnp.dot(left, right, precision=lax.Precision.HIGHEST, preferred_element_type=jnp.float32)

def layer_norm(value, gain):
    centred = value - lax.optimization_barrier(jnp.mean(value, axis=-1, keepdims=True))
    spread = lax.optimization_barrier(jnp.mean(centred * centred, axis=-1, keepdims=True))
    return centred * lax.rsqrt(spread + 1e-05) * gain

def attend(queries, key_block, value_block, allowed):
    scale_factor = 1.0 / math.sqrt(HEAD)
    scores = low_back(jnp.einsum('rqhe,rkhe->rhqk', queries, key_block, precision=lax.Precision.HIGHEST) * scale_factor)
    scores = jnp.where(allowed[:, None], scores, -1000000000.0)
    row_peak = lax.optimization_barrier(jnp.max(scores, axis=-1, keepdims=True))
    raised = jnp.exp(scores - row_peak)
    weights = low(raised / lax.optimization_barrier(jnp.sum(raised, axis=-1, keepdims=True)))
    return low(low_back(jnp.einsum('rhqk,rkhe->rqhe', weights, value_block, precision=lax.Precision.HIGHEST)))

def grouped(queries, key_block, value_block, allowed):
    row_count = queries.shape[0]
    group_size = math.gcd(row_count, 16)

    def to_groups(array):
        return array.reshape((row_count // group_size, group_size) + array.shape[1:])
    block_fn = jax.checkpoint(lambda pieces: attend(pieces[0], pieces[1], pieces[2], pieces[3]))
    result = lax.map(block_fn, (to_groups(queries), to_groups(key_block), to_groups(value_block), to_groups(allowed)))
    return result.reshape(queries.shape)

def reference(inputs, encoder_out, query_self, key_self, value_self, out_self, query_cross, key_cross, value_cross, out_cross, feed_up, feed_down, gain_self, gain_cross, gain_feed, seg_target, seg_source, subnet_of_row, chosen_layers, out_grad):
    row_count = seg_target.shape[0]
    width = inputs.shape[1]
    positions = jnp.arange(ROW_LEN)
    causal = positions[:, None] >= positions[None, :]
    self_mask = (seg_target[:, :, None] == seg_target[:, None, :]) & causal[None]
    cross_mask = seg_target[:, :, None] == seg_source[:, None, :]
    layer_ids = jnp.arange(encoder_out.shape[0])
    picked = lax.optimization_barrier(jnp.sum((chosen_layers[:, :, None] == layer_ids[None, None, :]).astype(jnp.float32), axis=1))
    row_pick = (subnet_of_row[:, None] == jnp.arange(chosen_layers.shape[0])[None, :]).astype(jnp.float32)
    row_weight = matmul(row_pick, picked)
    token_weight = 0.5 * jnp.repeat(row_weight, ROW_LEN, axis=0)

    def split_heads(flat):
        return flat.reshape(row_count, ROW_LEN, HEADS, HEAD)

    def forward(tokens, encoder, w_query_self, w_key_self, w_value_self, w_out_self, w_query_cross, w_key_cross, w_value_cross, w_out_cross, w_feed_up, w_feed_down, g_self, g_cross, g_feed):
        normed_self = low(layer_norm(tokens, g_self))
        queries_self = low(low_back(matmul(normed_self, w_query_self)))
        keys_self = low(low_back(matmul(normed_self, w_key_self)))
        values_self = low(low_back(matmul(normed_self, w_value_self)))
        attn_self = grouped(split_heads(queries_self), split_heads(keys_self), split_heads(values_self), self_mask).reshape(-1, width)
        after_self = tokens + low_back(matmul(attn_self, w_out_self))
        normed_cross = low(layer_norm(after_self, g_cross))
        memory = low(low_back(jnp.einsum('te,etd->td', token_weight, encoder, precision=lax.Precision.HIGHEST)))
        queries_cross = low(low_back(matmul(normed_cross, w_query_cross)))
        keys_cross = low(low_back(matmul(memory, w_key_cross)))
        values_cross = low(low_back(matmul(memory, w_value_cross)))
        attn_cross = grouped(split_heads(queries_cross), split_heads(keys_cross), split_heads(values_cross), cross_mask).reshape(-1, width)
        after_cross = after_self + low_back(matmul(attn_cross, w_out_cross))
        normed_feed = low(layer_norm(after_cross, g_feed))
        hidden_pre = low_back(matmul(normed_feed, w_feed_up))
        hidden = low(jax.nn.gelu(hidden_pre))
        return after_cross + low_back(matmul(hidden, w_feed_down))
    floats = [array.astype(jnp.float32) for array in (inputs, encoder_out, query_self, key_self, value_self, out_self, query_cross, key_cross, value_cross, out_cross, feed_up, feed_down, gain_self, gain_cross, gain_feed)]
    result, pullback = jax.vjp(forward, *floats)
    grads = pullback(out_grad.astype(jnp.float32))
    return (result.astype(jnp.bfloat16), grads[0].astype(jnp.bfloat16), grads[1], grads[2], grads[3], grads[4], grads[5], grads[6], grads[7], grads[8], grads[9], grads[10], grads[11], grads[12], grads[13], grads[14])
```

```python
import functools
import math

import jax
import jax.numpy as jnp
from jax import lax
from jax.experimental import pallas as pl
from jax.experimental.pallas import tpu as pltpu
from jax.sharding import PartitionSpec as P

HEADS = 8
HEAD = 80
MAIN = 64
REST = 16
ROW_LEN = 256
BLOCK = 256
SCALE = 1.0 / math.sqrt(HEAD)
LOW = jnp.bfloat16
FULL = jnp.float32
VMEM_BYTES = 56 * 1024 * 1024


def dot(left, right, left_dim, right_dim):
    return lax.dot_general(
        left, right, (((left_dim,), (right_dim,)), ((), ())), preferred_element_type=FULL
    )


def nn(left, right):
    return dot(left, right, 1, 0)


def nt(left, right):
    return dot(left, right, 1, 1)


def tn(left, right):
    return dot(left, right, 0, 0)


def norm_parts(value):
    centred = value - jnp.mean(value, axis=-1, keepdims=True)
    inverse = lax.rsqrt(jnp.mean(centred * centred, axis=-1, keepdims=True) + 1e-05)
    return (centred * inverse, inverse)


def norm_forward(value, gain):
    return (norm_parts(value)[0] * gain).astype(LOW)


def norm_backward(grad, value, gain):
    normed, inverse = norm_parts(value)
    scaled = grad * gain
    inner = (
        scaled
        - jnp.mean(scaled, axis=-1, keepdims=True)
        - normed * jnp.mean(scaled * normed, axis=-1, keepdims=True)
    )
    return inner * inverse


def source_column(position):
    rest = position - HEADS * MAIN
    return jnp.where(
        rest < 0,
        HEAD * (position // MAIN) + position % MAIN,
        HEAD * (rest // REST) + MAIN + rest % REST,
    )


def order_matrix(width, transposed):
    rows = lax.broadcasted_iota(jnp.int32, (width, width), 0)
    columns = lax.broadcasted_iota(jnp.int32, (width, width), 1)
    if transposed:
        rows, columns = columns, rows
    return (rows == source_column(columns)).astype(FULL).astype(LOW)


def head_groups(array, head):
    pair = head // 2
    return jnp.concatenate(
        [array[:, 2 * MAIN * pair : 2 * MAIN * (pair + 1)], array[:, HEADS * MAIN :]], axis=1
    )


def head_mask(head):
    lane = lax.broadcasted_iota(jnp.int32, (1, 2 * MAIN + HEADS * REST), 1)
    rest = lane - 2 * MAIN
    owner = jnp.where(rest < 0, 2 * (head // 2) + lane // MAIN, rest // REST)
    return (owner == head).astype(FULL).astype(LOW)


def same_segment(key_seg, query_seg):
    shape = (16, key_seg.shape[1])
    number = lax.broadcasted_iota(jnp.int32, shape, 0)
    key_hot = (number == key_seg).astype(FULL).astype(LOW)
    query_hot = (number == query_seg).astype(FULL).astype(LOW)
    return tn(key_hot, query_hot)


def merge_heads(parts):
    mains = [
        parts[2 * pair][:, : 2 * MAIN] + parts[2 * pair + 1][:, : 2 * MAIN]
        for pair in range(HEADS // 2)
    ]
    rests = [part[:, 2 * MAIN :] for part in parts]
    while len(rests) > 1:
        rests = [rests[i] + rests[i + 1] for i in range(0, len(rests), 2)]
    return jnp.concatenate(mains + rests, axis=1)


def attend(queries, keys, values, bias, probs_ref):
    parts = []
    for head in range(HEADS):
        mask = head_mask(head)
        scores = nt(head_groups(keys, head), head_groups(queries, head) * mask) * SCALE + bias
        raised = jnp.exp(scores - jnp.max(scores, axis=0, keepdims=True))
        probs = (raised * (1.0 / jnp.sum(raised, axis=0, keepdims=True))).astype(LOW)
        probs_ref[0, head] = probs
        parts.append(tn(probs, head_groups(values, head) * mask))
    return merge_heads(parts).astype(LOW)


def attend_back(grad, queries, keys, values, probs_ref):
    query_parts, key_parts, value_parts = [], [], []
    for head in range(HEADS):
        mask = head_mask(head)
        grad_head = head_groups(grad, head) * mask
        probs = probs_ref[0, head]
        wide = probs.astype(FULL)
        prob_grad = nt(head_groups(values, head), grad_head)
        delta = jnp.sum(prob_grad * wide, axis=0, keepdims=True)
        score_grad = (wide * (prob_grad - delta)).astype(LOW)
        value_parts.append(nn(probs, grad_head))
        key_parts.append(nn(score_grad, head_groups(queries, head) * mask))
        query_parts.append(tn(score_grad, head_groups(keys, head) * mask))
    return (
        (merge_heads(query_parts) * SCALE).astype(LOW),
        (merge_heads(key_parts) * SCALE).astype(LOW),
        merge_heads(value_parts).astype(LOW),
    )


def order_kernel(*refs):
    count = len(refs) // 2
    order = order_matrix(refs[0].shape[0], False)
    for source, target in zip(refs[: count - 2], refs[count:-2]):
        target[...] = nn(source[...], order).astype(LOW)
    for source, target in zip(refs[count - 2 : count], refs[-2:]):
        for head in range(HEADS):
            base = HEAD * head
            target[MAIN * head : MAIN * (head + 1)] = source[base : base + MAIN]
            rest = HEADS * MAIN + REST * head
            target[rest : rest + REST] = source[base + MAIN : base + HEAD]


def self_forward_kernel(
    x_ref, seg_ref, gain_ref, next_gain_ref, wq_ref, wk_ref, wv_ref, wo_ref, next_wq_ref,
    normed_ref, q_ref, k_ref, v_ref, probs_ref, attn_ref, after_ref, next_normed_ref, next_q_ref,
):
    value = x_ref[...].astype(FULL)
    normed = norm_forward(value, gain_ref[...])
    normed_ref[...] = normed
    queries = nn(normed, wq_ref[...]).astype(LOW)
    keys = nn(normed, wk_ref[...]).astype(LOW)
    values = nn(normed, wv_ref[...]).astype(LOW)
    q_ref[...], k_ref[...], v_ref[...] = queries, keys, values
    seg = seg_ref[0]
    key_at = lax.broadcasted_iota(jnp.int32, (ROW_LEN, ROW_LEN), 0)
    query_at = lax.broadcasted_iota(jnp.int32, (ROW_LEN, ROW_LEN), 1)
    allowed = (same_segment(seg, seg) > 0.5) & (key_at <= query_at)
    attn = attend(queries, keys, values, jnp.where(allowed, 0.0, -1e9), probs_ref)
    attn_ref[...] = attn
    after = value + nn(attn, wo_ref[...])
    after_ref[...] = after
    next_normed = norm_forward(after, next_gain_ref[...])
    next_normed_ref[...] = next_normed
    next_q_ref[...] = nn(next_normed, next_wq_ref[...]).astype(LOW)


def cross_forward_kernel(
    near_ref, far_ref, q_ref, after_ref, seg_target_ref, seg_source_ref, gain_ref, wk_ref, wv_ref, wo_ref,
    memory_ref, k_ref, v_ref, probs_ref, attn_ref, next_after_ref, next_normed_ref,
):
    memory = (near_ref[...].astype(FULL) + far_ref[...].astype(FULL)).astype(LOW)
    memory_ref[...] = memory
    keys = nn(memory, wk_ref[...]).astype(LOW)
    values = nn(memory, wv_ref[...]).astype(LOW)
    k_ref[...], v_ref[...] = keys, values
    allowed = same_segment(seg_source_ref[0], seg_target_ref[0]) > 0.5
    attn = attend(q_ref[...], keys, values, jnp.where(allowed, 0.0, -1e9), probs_ref)
    attn_ref[...] = attn
    after = after_ref[...] + nn(attn, wo_ref[...])
    next_after_ref[...] = after
    next_normed_ref[...] = norm_forward(after, gain_ref[...])


def put_chunk(place_ref, keep_ref, send_ref, quarter, chunk, columns, piece):
    x_at = lax.bitwise_xor(quarter // 2, lax.shift_right_logical(place_ref[0], 1))
    core = lax.bitwise_and(place_ref[0], 1)
    dp_at = lax.bitwise_xor(chunk, place_ref[1])

    @pl.when(core == quarter % 2)
    def _():
        keep_ref[x_at, dp_at, :, columns] = piece

    @pl.when(core != quarter % 2)
    def _():
        send_ref[x_at, dp_at, :, columns] = piece


def feed_kernel(
    chunks, place_ref, normed_ref, grad_ref, up_ref, down_ref, after_ref, *refs
):
    if chunks:
        out_ref, back_ref, up_keep, up_send, down_keep, down_send = refs[:6]
    else:
        out_ref, back_ref, up_all, down_all = refs[:4]
    acc_ref, normed_t, grad_t, hidden_ref, pre_ref = refs[-5:]
    step = pl.program_id(0)
    tokens, width = normed_ref.shape
    share = up_ref.shape[1]

    @pl.when(step == 0)
    def _():
        acc_ref[...] = after_ref[...]
        back_ref[...] = jnp.zeros_like(back_ref)
        for start in range(0, tokens, BLOCK):
            rows = slice(start, start + BLOCK)
            normed_t[:, rows] = normed_ref[rows, :].T
            grad_t[:, rows] = grad_ref[rows, :].T

    @pl.loop(0, tokens // BLOCK)
    def _(at):
        rows = pl.ds(pl.multiple_of(at * BLOCK, BLOCK), BLOCK)
        pre = nn(normed_ref[rows, :], up_ref[...])
        square = pre * pre
        slope = math.sqrt(2.0 / math.pi)
        bend = jnp.tanh(slope * pre * (1.0 + 0.044715 * square))
        half = 0.5 * (1.0 + bend)
        hidden = (pre * half).astype(LOW)
        rate = half + 0.5 * pre * (1.0 - bend * bend) * (slope * (1.0 + 3 * 0.044715 * square))
        pre_grad = (nt(grad_ref[rows, :], down_ref[...]) * rate).astype(LOW)
        hidden_ref[rows, :] = hidden
        pre_ref[rows, :] = pre_grad
        acc_ref[rows, :] += nn(hidden, down_ref[...])
        back_ref[rows, :] += nt(pre_grad, up_ref[...])

    for start in range(0, share, BLOCK):
        columns = slice(start, start + BLOCK)
        up_grad = nn(normed_t[...], pre_ref[:, columns]).astype(LOW)
        down_grad = nn(grad_t[...], hidden_ref[:, columns]).astype(LOW).T
        if not chunks:
            up_all[:, columns] = up_grad
            down_all[columns, :] = down_grad
            continue
        length = width // chunks
        x_at = lax.bitwise_xor(step // 2, lax.shift_right_logical(place_ref[0], 1))
        core = lax.bitwise_and(place_ref[0], 1)
        for chunk in range(chunks):
            piece = up_grad[length * chunk : length * (chunk + 1)]
            dp_at = lax.bitwise_xor(chunk, place_ref[1])

            @pl.when(core == step % 2)
            def _():
                up_keep[x_at, dp_at, :, columns] = piece

            @pl.when(core != step % 2)
            def _():
                up_send[x_at, dp_at, :, columns] = piece

        part = share // 8
        for row in range(start, start + BLOCK, 32):
            chunk = 2 * step + row // (share // 2)
            inside = row % (share // 2)
            quarter, offset = inside // part, inside % part
            x_at = lax.bitwise_xor(quarter // 2, lax.shift_right_logical(place_ref[0], 1))
            dp_at = lax.bitwise_xor(chunk, place_ref[1])
            piece = down_grad[row - start : row - start + 32]
            target = slice(offset, offset + 32)

            @pl.when(core == quarter % 2)
            def _():
                down_keep[x_at, dp_at, target, :] = piece

            @pl.when(core != quarter % 2)
            def _():
                down_send[x_at, dp_at, target, :] = piece

    @pl.when(step == pl.num_programs(0) - 1)
    def _():
        out_ref[...] = acc_ref[...].astype(LOW)


def cross_backward_kernel(
    back_ref, after_cross_ref, gain_feed_ref, grad_ref, after_self_ref, gain_cross_ref,
    q_ref, k_ref, v_ref, probs_ref, wq_ref, wk_ref, wv_ref, wo_ref,
    in_ref, dq_ref, dk_ref, dv_ref, memory_ref, grad_self_ref,
):
    grad = grad_ref[...].astype(FULL) + norm_backward(
        back_ref[...], after_cross_ref[...], gain_feed_ref[...]
    )
    branch = grad.astype(LOW)
    in_ref[...] = branch
    query_grad, key_grad, value_grad = attend_back(
        nt(branch, wo_ref[...]).astype(LOW), q_ref[...], k_ref[...], v_ref[...], probs_ref
    )
    dq_ref[...], dk_ref[...], dv_ref[...] = query_grad, key_grad, value_grad
    memory_ref[...] = (nt(key_grad, wk_ref[...]) + nt(value_grad, wv_ref[...])).astype(LOW)
    grad_self_ref[...] = grad + norm_backward(
        nt(query_grad, wq_ref[...]), after_self_ref[...], gain_cross_ref[...]
    )


def self_backward_kernel(
    grad_ref, q_ref, k_ref, v_ref, probs_ref, wo_ref, in_ref, dq_ref, dk_ref, dv_ref
):
    branch = grad_ref[...].astype(LOW)
    in_ref[...] = branch
    dq_ref[...], dk_ref[...], dv_ref[...] = attend_back(
        nt(branch, wo_ref[...]).astype(LOW), q_ref[...], k_ref[...], v_ref[...], probs_ref
    )


def input_grad_kernel(dq_ref, dk_ref, dv_ref, wq_ref, wk_ref, wv_ref, x_ref, gain_ref, grad_ref, out_ref):
    inner = (
        nt(dq_ref[...], wq_ref[...]) + nt(dk_ref[...], wk_ref[...]) + nt(dv_ref[...], wv_ref[...])
    )
    back = norm_backward(inner, x_ref[...].astype(FULL), gain_ref[...])
    out_ref[...] = (grad_ref[...] + back).astype(LOW)


def weight_kernel(chunks, sources, place_ref, *refs):
    lefts = refs[: max(sources) + 1]
    rights = refs[len(lefts) : len(lefts) + 4]
    targets, left_t = refs[len(lefts) + 4 : -1], refs[-1]
    tokens, width = rights[0].shape
    ready = None
    for weight in range(4):
        if sources[weight] != ready:
            ready = sources[weight]
            for start in range(0, tokens, BLOCK):
                rows = slice(start, start + BLOCK)
                left_t[:, rows] = lefts[ready][rows, :].T
        for start in range(0, width, BLOCK):
            columns = slice(start, min(start + BLOCK, width))
            grad = nn(left_t[...], rights[weight][:, columns]).astype(LOW)
            if not chunks:
                targets[0][weight, :, columns] = grad
                continue
            length = width // chunks
            for chunk in range(chunks):
                piece = grad[length * chunk : length * (chunk + 1)]
                if weight == 3:
                    rest = HEADS * MAIN + REST * chunk
                    piece = jnp.concatenate(
                        [grad[MAIN * chunk : MAIN * (chunk + 1)], grad[rest : rest + REST]], axis=0
                    )
                put_chunk(place_ref, *targets, weight, chunk, columns, piece)


def encoder_grad_kernel(place_ref, hits_ref, *refs):
    out_ref = refs[-1]
    step = pl.program_id(0)
    rows = pl.num_programs(0) // 4
    for turn in range(4):

        @pl.when(step // rows == turn)
        def _():
            owner = lax.bitwise_xor(place_ref[0], turn)
            weight = 0.5 * hits_ref[owner * rows + step % rows]
            out_ref[0] = weight * refs[turn][...].astype(FULL)


def final_kernel(place_ref, *refs):
    sources, weights, gains, targets = refs[:16], refs[16:21], refs[21:24], refs[24:-2]
    cross_ref, self_ref = refs[-2:]
    up_out, down_out = targets[8:10]
    part = down_out.shape[0] // 4
    share = up_out.shape[1] // 4
    for turn in range(4):
        up, down, cross, own = sources[4 * turn : 4 * (turn + 1)]
        owner = lax.bitwise_xor(place_ref[0], turn)
        up_out[:, pl.ds(pl.multiple_of(owner * share, share), share)] = up[...].astype(FULL)
        down_out[pl.ds(pl.multiple_of(owner * part, part), part), :] = down[...].astype(FULL)
        cross_ref[owner] = cross[...]
        self_ref[owner] = own[...]
    order = order_matrix(cross_ref.shape[2], True)
    for at in range(3):
        targets[at][...] = nn(self_ref[at], order)
        targets[4 + at][...] = nn(cross_ref[at], order)
    targets[3][...] = self_ref[3].astype(FULL)
    targets[7][...] = cross_ref[3].astype(FULL)

    def gain_grad(pairs, gain_ref, target):
        total = sum(
            jnp.sum(weight.astype(FULL) * grad.astype(FULL), axis=1, keepdims=True)
            for weight, grad in pairs
        )
        turned = jnp.broadcast_to(total, (total.shape[0], 128)).T
        target[0] = turned[:1] / gain_ref[0]

    gain_grad([(weights[at][...], self_ref[at]) for at in range(3)], gains[0], targets[10])
    gain_grad([(weights[3][...], cross_ref[0])], gains[1], targets[11])
    gain_grad([(weights[4][...], up_out[...])], gains[2], targets[12])


def whole(array):
    return pl.BlockSpec(array.shape, lambda *at: (0,) * array.ndim)


def by_row(array):
    if array.ndim == 2:
        return pl.BlockSpec((ROW_LEN, array.shape[1]), lambda at, *_: (at, 0))
    return pl.BlockSpec(
        (1,) + array.shape[1:], lambda at, *_: (at,) + (0,) * (array.ndim - 1)
    )


def run(body, name, grid, ins, in_specs, outs, out_specs, flops, scratch=(), prefetch=()):
    moved = sum(array.size * array.dtype.itemsize for array in list(ins) + list(outs))
    return pl.pallas_call(
        body,
        name=name,
        out_shape=outs,
        grid_spec=pltpu.PrefetchScalarGridSpec(
            num_scalar_prefetch=len(prefetch),
            grid=grid,
            in_specs=in_specs,
            out_specs=out_specs,
            scratch_shapes=scratch,
        ),
        compiler_params=pltpu.CompilerParams(vmem_limit_bytes=VMEM_BYTES),
        cost_estimate=pl.CostEstimate(
            flops=int(flops), bytes_accessed=int(moved), transcendentals=0
        ),
    )(*prefetch, *ins)


def shape_of(shape, dtype=LOW):
    return jax.ShapeDtypeStruct(tuple(shape), dtype)


def row_call(body, name, rowed, fixed, outs, flops, order):
    ins, specs = [], []
    rowed, fixed = list(rowed), list(fixed)
    for kind in order:
        array = rowed.pop(0) if kind == "r" else fixed.pop(0)
        ins.append(array)
        specs.append(by_row(array) if kind == "r" else whole(array))
    tokens = outs[0].shape[0]
    return run(
        body, name, (tokens // ROW_LEN,), ins, specs, outs, [by_row(out) for out in outs], flops
    )


def permuted(value, axes, sizes, flip):
    count = math.prod(sizes)
    return lax.ppermute(value, axes, [(at, at ^ flip) for at in range(count)])


def added(parts):
    total = parts[0].astype(FULL)
    for part in parts[1:]:
        total = total + part.astype(FULL)
    return total.astype(LOW)


def on_device(
    layer_size,
    dp_size,
    inputs,
    encoder_out,
    query_self,
    key_self,
    value_self,
    out_self,
    query_cross,
    key_cross,
    value_cross,
    out_cross,
    feed_up,
    feed_down,
    gain_self,
    gain_cross,
    gain_feed,
    seg_target,
    seg_source,
    subnet_of_row,
    chosen_layers,
    out_grad,
):
    tokens, width = inputs.shape
    rows = tokens // ROW_LEN
    layer_at = lax.axis_index("layer")
    dp_at = lax.axis_index("dp")
    place = jnp.stack([layer_at, dp_at]).astype(jnp.int32)
    axes, sizes = ("dp", "layer"), (dp_size, layer_size)

    def across(value, layer_flip, dp_flip=0):
        return permuted(value, axes, sizes, dp_flip * layer_size + layer_flip)

    picked = jnp.sum(
        (chosen_layers[:, :, None] == jnp.arange(layer_size)[None, None, :]).astype(FULL), axis=1
    )
    row_pick = (subnet_of_row[:, None] == jnp.arange(chosen_layers.shape[0])[None, :]).astype(FULL)
    block_hits = jnp.sum(row_pick[:, :, None] * picked[None], axis=1)
    own_layer = encoder_out.reshape(layer_size, rows, ROW_LEN, width)

    def own_block(flip):
        return lax.dynamic_index_in_dim(own_layer, layer_at ^ flip, 0, keepdims=False)

    def hits_of(flip, layer_flip):
        hits = lax.dynamic_slice_in_dim(block_hits, (layer_at ^ flip) * rows, rows, 0)
        hits = lax.dynamic_slice_in_dim(hits, layer_at ^ layer_flip, 1, 1)
        return 0.5 * hits[:, :, None]

    def chip_sum(flip, arrived):
        total = hits_of(flip, 0) * own_block(flip).astype(FULL)
        total = total + hits_of(flip, 1) * arrived.astype(FULL)
        return total.astype(LOW).reshape(tokens, width)

    far_half = across(own_block(3), 1)
    near_half = across(own_block(1), 1)
    far_memory = across(chip_sum(2, far_half), 2)
    near_memory = chip_sum(0, near_half)

    weights = [query_self, key_self, value_self, query_cross, key_cross, value_cross, out_self, out_cross]
    ordered = run(
        order_kernel,
        "order_weights",
        (1,),
        weights,
        [whole(array) for array in weights],
        [shape_of(array.shape) for array in weights],
        [whole(array) for array in weights],
        12 * width**3,
    )
    wq_self, wk_self, wv_self, wq_cross, wk_cross, wv_cross, wo_self, wo_cross = ordered
    target = seg_target.reshape(rows, 1, ROW_LEN)
    source = seg_source.reshape(rows, 1, ROW_LEN)
    g_self, g_cross, g_feed = (gain.reshape(1, width) for gain in (gain_self, gain_cross, gain_feed))
    flat = shape_of((tokens, width))
    wide = shape_of((tokens, width), FULL)
    probs = shape_of((rows, HEADS, ROW_LEN, ROW_LEN))
    dense_flops = 2 * tokens * width * width
    head_flops = 2 * tokens * ROW_LEN * ROW_LEN * HEADS

    normed_self, q_self, k_self, v_self, probs_self, attn_self, after_self, normed_cross, q_cross = row_call(
        self_forward_kernel,
        "self_forward",
        (inputs, target),
        (g_self, g_cross, wq_self, wk_self, wv_self, wo_self, wq_cross),
        [flat, flat, flat, flat, probs, flat, wide, flat, flat],
        5 * dense_flops + 2 * head_flops,
        "rrfffffff",
    )
    memory, k_cross, v_cross, probs_cross, attn_cross, after_cross, normed_feed = row_call(
        cross_forward_kernel,
        "cross_forward",
        (near_memory, far_memory, q_cross, after_self, target, source),
        (g_feed, wk_cross, wv_cross, wo_cross),
        [flat, flat, flat, probs, flat, wide, flat],
        3 * dense_flops + 2 * head_flops,
        "rrrrrrffff",
    )

    chunks = dp_size if dp_size == HEADS and layer_size == 4 else 0
    hidden = feed_up.shape[1]
    share = hidden // 4
    if chunks:
        up_shape = shape_of((2, chunks, width // chunks, share))
        down_shape = shape_of((2, chunks, share // 8, width))
        feed_outs = [up_shape, up_shape, down_shape, down_shape]
        feed_specs = [whole(out) for out in feed_outs]
        weight_outs = [shape_of((2, chunks, width // chunks, width))] * 2
    else:
        feed_outs = [shape_of(feed_up.shape), shape_of(feed_down.shape)]
        feed_specs = [
            pl.BlockSpec((width, share), lambda at, *_: (0, at)),
            pl.BlockSpec((share, width), lambda at, *_: (at, 0)),
        ]
        weight_outs = [shape_of((4, width, width))]
    layer_out, back_feed, *feed_grads = run(
        functools.partial(feed_kernel, chunks),
        "feed",
        (4,),
        [normed_feed, out_grad, feed_up, feed_down, after_cross],
        [
            whole(normed_feed),
            whole(out_grad),
            pl.BlockSpec((width, share), lambda at, *_: (0, at)),
            pl.BlockSpec((share, width), lambda at, *_: (at, 0)),
            whole(after_cross),
        ],
        [flat, wide] + feed_outs,
        [whole(flat), whole(wide)] + feed_specs,
        12 * tokens * width * hidden,
        scratch=[
            pltpu.VMEM((tokens, width), FULL),
            pltpu.VMEM((width, tokens), LOW),
            pltpu.VMEM((width, tokens), LOW),
            pltpu.VMEM((tokens, share), LOW),
            pltpu.VMEM((tokens, share), LOW),
        ],
        prefetch=(place,),
    )

    def weight_call(name, sources, lefts, rights):
        ins = list(lefts) + list(rights)
        return run(
            functools.partial(weight_kernel, chunks, sources),
            name,
            (1,),
            ins,
            [whole(array) for array in ins],
            weight_outs,
            [whole(out) for out in weight_outs],
            4 * dense_flops,
            scratch=[pltpu.VMEM((width, tokens), LOW)],
            prefetch=(place,),
        )

    cross_in, dq_cross, dk_cross, dv_cross, memory_grad, grad_after_self = row_call(
        cross_backward_kernel,
        "cross_backward",
        (back_feed, after_cross, out_grad, after_self, q_cross, k_cross, v_cross, probs_cross),
        (g_feed, g_cross, wq_cross, wk_cross, wv_cross, wo_cross),
        [flat, flat, flat, flat, flat, wide],
        4 * dense_flops + 4 * head_flops,
        "rrfrrfrrrrffff",
    )
    cross_grads = weight_call(
        "cross_weights",
        (0, 1, 1, 2),
        (normed_cross, memory, attn_cross),
        (dq_cross, dk_cross, dv_cross, cross_in),
    )
    self_in, dq_self, dk_self, dv_self = row_call(
        self_backward_kernel,
        "self_backward",
        (grad_after_self, q_self, k_self, v_self, probs_self),
        (wo_self,),
        [flat, flat, flat, flat],
        dense_flops + 4 * head_flops,
        "rrrrrf",
    )
    self_grads = weight_call(
        "self_weights",
        (0, 0, 0, 1),
        (normed_self, attn_self),
        (dq_self, dk_self, dv_self, self_in),
    )
    (input_grad,) = row_call(
        input_grad_kernel,
        "input_grad",
        (dq_self, dk_self, dv_self, inputs, grad_after_self),
        (wq_self, wk_self, wv_self, g_self),
        [flat],
        3 * dense_flops,
        "rrrfffrfr",
    )

    from_core = across(memory_grad, 1)
    from_chip = across(memory_grad, 2)
    from_both = across(from_chip, 1)
    own_hits = lax.dynamic_slice_in_dim(block_hits, layer_at, 1, 1)[:, 0]
    arrived = [memory_grad, from_core, from_chip, from_both]

    def arrived_spec(turn):
        return pl.BlockSpec(
            (ROW_LEN, width), lambda at, *_: (jnp.clip(at - turn * rows, 0, rows - 1), 0)
        )

    encoder_shape = shape_of(encoder_out.shape, FULL)
    (encoder_grad,) = run(
        encoder_grad_kernel,
        "encoder_grad",
        (4 * rows,),
        arrived,
        [arrived_spec(turn) for turn in range(4)],
        [encoder_shape],
        [
            pl.BlockSpec(
                (1, ROW_LEN, width),
                lambda at, place, hits: (0, (place[0] ^ (at // rows)) * rows + at % rows, 0),
            )
        ],
        encoder_out.size,
        prefetch=(place, own_hits),
    )

    if chunks:

        def scatter(keep, send):
            parts = [part.reshape((2, 4, 2) + part.shape[2:]) for part in (keep, across(send, 1))]
            x_send = added([part[1, :, 0] for part in parts])
            y_send = added([part[0, :, 1] for part in parts])
            both_send = added([part[1, :, 1] for part in parts])
            parts = [part[0, :, 0] for part in parts]
            parts += [across(both_send, 2, 1), across(x_send, 2), across(y_send, 0, 1)]
            sends = [added([part[flip] for part in parts]) for flip in (1, 2, 3)]
            arrived = [across(sends[flip - 1], 0, 2 * flip) for flip in (1, 2, 3)]
            return added([part[0] for part in parts] + arrived)

        pieces = [
            scatter(feed_grads[0], feed_grads[1]),
            scatter(feed_grads[2], feed_grads[3]),
            scatter(*cross_grads),
            scatter(*self_grads),
        ]
        gathered = pieces + [across(piece, flip) for flip in (1, 2, 3) for piece in pieces]
        length = width // chunks
        square = shape_of((length, width), FULL)
        outs = [square] * 8 + [
            shape_of((length, hidden), FULL),
            shape_of((hidden // chunks, width), FULL),
        ]
        outs += [shape_of((1, 1, length), FULL)] * 3
        chunk_weights = [wq_self, wk_self, wv_self, wq_cross, feed_up]
        gains = [gain.reshape(chunks, 1, length) for gain in (gain_self, gain_cross, gain_feed)]
        finals = run(
            final_kernel,
            "final",
            (1,),
            gathered + chunk_weights + gains,
            [whole(array) for array in gathered]
            + [
                pl.BlockSpec((length, array.shape[1]), lambda at, place: (place[1], 0))
                for array in chunk_weights
            ]
            + [pl.BlockSpec((1, 1, length), lambda at, place: (place[1], 0, 0))] * 3,
            outs,
            [whole(out) for out in outs],
            12 * length * width * width,
            scratch=[pltpu.VMEM((4, length, width), LOW)] * 2,
            prefetch=(place,),
        )
        weight_grads = list(finals[:10])
        gain_grads = [value.reshape(length) for value in finals[10:]]
    else:
        back_order = order_matrix(width, True)

        def total(grad):
            part = lax.psum_scatter(grad.astype(FULL), "dp", scatter_dimension=0, tiled=True)
            return lax.psum(part.astype(LOW), "layer").astype(FULL)

        def natural(grads):
            back = [nn(grads[0][at], back_order).astype(LOW) for at in range(3)]
            return [total(grad) for grad in back + [nn(back_order.T, grads[0][3]).astype(LOW)]]

        grads_self, grads_cross = natural(self_grads), natural(cross_grads)
        weight_grads = grads_self + grads_cross + [total(grad) for grad in feed_grads]
        length = width // dp_size

        def my_rows(array):
            return lax.dynamic_slice_in_dim(array, dp_at * length, length, 0).astype(FULL)

        def gain_total(pairs, gain):
            sums = sum(jnp.sum(my_rows(weight) * grad, axis=1) for weight, grad in pairs)
            return sums / my_rows(gain)

        gain_grads = [
            gain_total(zip((query_self, key_self, value_self), grads_self), gain_self),
            gain_total([(query_cross, grads_cross[0])], gain_cross),
            gain_total([(feed_up, weight_grads[8])], gain_feed),
        ]
    return (layer_out, input_grad, encoder_grad, *weight_grads, *gain_grads)


def solution(mesh):
    in_specs = (
        P(("dp", "layer"), None),
        P("layer", "dp", None),
        *[P()] * 13,
        P(("dp", "layer"), None),
        P(("dp", "layer"), None),
        P("dp"),
        P(),
        P(("dp", "layer"), None),
    )
    out_specs = (
        P(("dp", "layer"), None),
        P(("dp", "layer"), None),
        P("layer", "dp", None),
        *[P("dp", None)] * 10,
        *[P("dp")] * 3,
    )
    body = functools.partial(on_device, mesh.shape["layer"], mesh.shape["dp"])
    return jax.shard_map(
        body, mesh=mesh, in_specs=in_specs, out_specs=out_specs, check_vma=False
    )
```

```python
import functools
import math

import jax
import jax.numpy as jnp
from jax import lax
from jax.experimental import pallas as pl
from jax.experimental.pallas import tpu as pltpu
from jax.sharding import PartitionSpec as P

HEADS = 8
HEAD = 80
MAIN = 64
REST = 16
ROW_LEN = 256
BLOCK = 256
SCALE = 1.0 / math.sqrt(HEAD)
LOW = jnp.bfloat16
FULL = jnp.float32
VMEM_BYTES = 56 * 1024 * 1024
WEIGHT = 0.01


def dot(left, right, left_dim, right_dim):
    return lax.dot_general(
        left, right, (((left_dim,), (right_dim,)), ((), ())), preferred_element_type=FULL
    )


def nn(left, right):
    return dot(left, right, 1, 0)


def nt(left, right):
    return dot(left, right, 1, 1)


def tn(left, right):
    return dot(left, right, 0, 0)


def norm_parts(value):
    centred = value - jnp.mean(value, axis=-1, keepdims=True)
    inverse = lax.rsqrt(jnp.mean(centred * centred, axis=-1, keepdims=True) + 1e-05)
    return (centred * inverse, inverse)


def norm_forward(value, gain):
    return (norm_parts(value)[0] * gain).astype(LOW)


def norm_backward(grad, value, gain):
    normed, inverse = norm_parts(value)
    scaled = grad * gain
    inner = (
        scaled
        - jnp.mean(scaled, axis=-1, keepdims=True)
        - normed * jnp.mean(scaled * normed, axis=-1, keepdims=True)
    )
    return inner * inverse


def source_column(position):
    rest = position - HEADS * MAIN
    return jnp.where(
        rest < 0,
        HEAD * (position // MAIN) + position % MAIN,
        HEAD * (rest // REST) + MAIN + rest % REST,
    )


def order_matrix(width, transposed):
    rows = lax.broadcasted_iota(jnp.int32, (width, width), 0)
    columns = lax.broadcasted_iota(jnp.int32, (width, width), 1)
    if transposed:
        rows, columns = columns, rows
    return (rows == source_column(columns)).astype(FULL).astype(LOW)


def head_groups(array, head):
    pair = head // 2
    return jnp.concatenate(
        [array[:, 2 * MAIN * pair : 2 * MAIN * (pair + 1)], array[:, HEADS * MAIN :]], axis=1
    )


def head_mask(head):
    lane = lax.broadcasted_iota(jnp.int32, (1, 2 * MAIN + HEADS * REST), 1)
    rest = lane - 2 * MAIN
    owner = jnp.where(rest < 0, 2 * (head // 2) + lane // MAIN, rest // REST)
    return (owner == head).astype(FULL).astype(LOW)


def same_segment(key_seg, query_seg):
    shape = (16, key_seg.shape[1])
    number = lax.broadcasted_iota(jnp.int32, shape, 0)
    key_hot = (number == key_seg).astype(FULL).astype(LOW)
    query_hot = (number == query_seg).astype(FULL).astype(LOW)
    return tn(key_hot, query_hot)


def merge_pairs(parts):
    mains = [part[:, : 2 * MAIN] for part in parts]
    rests = [part[:, 2 * MAIN :] for part in parts]
    while len(rests) > 1:
        rests = [rests[i] + rests[i + 1] for i in range(0, len(rests), 2)]
    return jnp.concatenate(mains + rests, axis=1)


def attend(queries, keys, values, bias, probs_ref):
    parts = []
    for pair in range(HEADS // 2):
        pair_probs, pair_values = [], []
        for head in (2 * pair, 2 * pair + 1):
            mask = head_mask(head)
            scores = nt(head_groups(keys, head), head_groups(queries, head) * mask) * SCALE + bias
            raised = jnp.exp(scores - jnp.max(scores, axis=0, keepdims=True))
            probs = (raised * (1.0 / jnp.sum(raised, axis=0, keepdims=True))).astype(LOW)
            probs_ref[0, head] = probs
            pair_probs.append(probs)
            pair_values.append(head_groups(values, head) * mask)
        parts.append(
            tn(jnp.concatenate(pair_probs, axis=0), jnp.concatenate(pair_values, axis=0))
        )
    return merge_pairs(parts).astype(LOW)


def attend_back(grad, queries, keys, values, probs_ref):
    query_parts, key_parts, value_parts = [], [], []
    for pair in range(HEADS // 2):
        pair_probs, pair_slopes, pair_grads, pair_queries, pair_keys = [], [], [], [], []
        for head in (2 * pair, 2 * pair + 1):
            mask = head_mask(head)
            grad_head = head_groups(grad, head) * mask
            probs = probs_ref[0, head]
            wide = probs.astype(FULL)
            prob_grad = nt(head_groups(values, head), grad_head)
            delta = jnp.sum(prob_grad * wide, axis=0, keepdims=True)
            pair_probs.append(probs)
            pair_slopes.append((wide * (prob_grad - delta)).astype(LOW))
            pair_grads.append(grad_head)
            pair_queries.append(head_groups(queries, head) * mask)
            pair_keys.append(head_groups(keys, head) * mask)
        query_parts.append(
            tn(jnp.concatenate(pair_slopes, axis=0), jnp.concatenate(pair_keys, axis=0))
        )
        key_parts.append(
            nn(jnp.concatenate(pair_slopes, axis=1), jnp.concatenate(pair_queries, axis=0))
        )
        value_parts.append(
            nn(jnp.concatenate(pair_probs, axis=1), jnp.concatenate(pair_grads, axis=0))
        )
    return (
        (merge_pairs(query_parts) * SCALE).astype(LOW),
        (merge_pairs(key_parts) * SCALE).astype(LOW),
        merge_pairs(value_parts).astype(LOW),
    )


def order_kernel(*refs):
    count = len(refs) // 2
    order = order_matrix(refs[0].shape[0], False)
    for source, target in zip(refs[: count - 2], refs[count:-2]):
        target[...] = nn(source[...], order).astype(LOW)
    for source, target in zip(refs[count - 2 : count], refs[-2:]):
        for head in range(HEADS):
            base = HEAD * head
            target[MAIN * head : MAIN * (head + 1)] = source[base : base + MAIN]
            rest = HEADS * MAIN + REST * head
            target[rest : rest + REST] = source[base + MAIN : base + HEAD]


def self_forward_kernel(
    x_ref, seg_ref, gain_ref, next_gain_ref, wq_ref, wk_ref, wv_ref, wo_ref, next_wq_ref,
    normed_ref, q_ref, k_ref, v_ref, probs_ref, attn_ref, after_ref, next_normed_ref, next_q_ref,
):
    value = x_ref[...].astype(FULL)
    normed = norm_forward(value, gain_ref[...])
    normed_ref[...] = normed
    queries = nn(normed, wq_ref[...]).astype(LOW)
    keys = nn(normed, wk_ref[...]).astype(LOW)
    values = nn(normed, wv_ref[...]).astype(LOW)
    q_ref[...], k_ref[...], v_ref[...] = queries, keys, values
    seg = seg_ref[0]
    key_at = lax.broadcasted_iota(jnp.int32, (ROW_LEN, ROW_LEN), 0)
    query_at = lax.broadcasted_iota(jnp.int32, (ROW_LEN, ROW_LEN), 1)
    allowed = (same_segment(seg, seg) > 0.5) & (key_at <= query_at)
    attn = attend(queries, keys, values, jnp.where(allowed, 0.0, -1e9), probs_ref)
    attn_ref[...] = attn
    after = value + nn(attn, wo_ref[...])
    after_ref[...] = after
    next_normed = norm_forward(after, next_gain_ref[...])
    next_normed_ref[...] = next_normed
    next_q_ref[...] = nn(next_normed, next_wq_ref[...]).astype(LOW)


def cross_forward_kernel(
    near_ref, far_ref, q_ref, after_ref, seg_target_ref, seg_source_ref, gain_ref, wk_ref, wv_ref, wo_ref,
    memory_ref, k_ref, v_ref, probs_ref, attn_ref, next_after_ref, next_normed_ref,
):
    memory = (near_ref[...].astype(FULL) + far_ref[...].astype(FULL)).astype(LOW)
    memory_ref[...] = memory
    keys = nn(memory, wk_ref[...]).astype(LOW)
    values = nn(memory, wv_ref[...]).astype(LOW)
    k_ref[...], v_ref[...] = keys, values
    allowed = same_segment(seg_source_ref[0], seg_target_ref[0]) > 0.5
    attn = attend(q_ref[...], keys, values, jnp.where(allowed, 0.0, -1e9), probs_ref)
    attn_ref[...] = attn
    after = after_ref[...] + nn(attn, wo_ref[...])
    next_after_ref[...] = after
    next_normed_ref[...] = norm_forward(after, gain_ref[...])


def store_piece(place_ref, held_ref, quarter, chunk, rows, columns, piece):
    owner = lax.bitwise_xor(place_ref[0], quarter)
    dp_at = lax.bitwise_xor(chunk, place_ref[1])
    held_ref[
        lax.bitwise_and(owner, 1), lax.shift_right_logical(owner, 1), dp_at, rows, columns
    ] = piece


def hand_out(place_ref, held_ref, targets, sem, quarter, region):
    owner = lax.bitwise_xor(place_ref[0], quarter)
    x_at = lax.shift_right_logical(owner, 1)
    for half in range(2):

        @pl.when(lax.bitwise_and(owner, 1) == half)
        def _():
            pltpu.make_async_copy(
                held_ref.at[(half, x_at) + region], targets[half].at[(x_at,) + region], sem
            ).start()


def hand_out_done(held_ref, targets, sem, region):
    pltpu.make_async_copy(held_ref.at[(0, 0) + region], targets[0].at[(0,) + region], sem).wait()


def feed_kernel(chunks, place_ref, normed_ref, grad_ref, up_ref, down_ref, after_ref, out_ref, back_ref, *refs):
    targets, refs = refs[:2], refs[2:]
    acc_ref, total_ref, low_ref, start_ref, normed_t, grad_t, hidden_ref, pre_ref, sems, *held = refs
    step, steps = pl.program_id(0), pl.num_programs(0)
    tokens, width = normed_ref.shape
    share = up_ref.shape[1]
    fetch = pltpu.make_async_copy(after_ref, start_ref, sems.at[0])
    copies = [
        pltpu.make_async_copy(low_ref, out_ref, sems.at[1]),
        pltpu.make_async_copy(total_ref, back_ref, sems.at[2]),
    ]

    @pl.when(step == 0)
    def _():
        fetch.start()
        for start in range(0, tokens, BLOCK):
            rows = slice(start, start + BLOCK)
            normed_t[:, rows] = normed_ref[rows, :].T
            grad_t[:, rows] = grad_ref[rows, :].T

    for start in range(0, tokens, 2 * BLOCK):
        rows = slice(start, start + 2 * BLOCK)
        pre = nn(normed_ref[rows, :], up_ref[...])
        hidden_grad = nt(grad_ref[rows, :], down_ref[...])
        square = pre * pre
        slope = math.sqrt(2.0 / math.pi)
        bend = jnp.tanh(pre * (slope + slope * 0.044715 * square))
        half = 0.5 + 0.5 * bend
        hidden = (pre * half).astype(LOW)
        rate = half + pre * half * (1.0 - bend) * (slope + slope * 3 * 0.044715 * square)
        pre_grad = (hidden_grad * rate).astype(LOW)
        hidden_ref[rows, :] = hidden
        pre_ref[rows, :] = pre_grad
        out_part = nn(hidden, down_ref[...])
        back_part = nt(pre_grad, up_ref[...])

        @pl.when(step == 0)
        def _():
            acc_ref[rows, :] = out_part
            total_ref[rows, :] = back_part

        @pl.when(step > 0)
        def _():
            acc_ref[rows, :] += out_part
            total_ref[rows, :] += back_part

    @pl.when(step == steps - 1)
    def _():
        fetch.wait()
        low_ref[...] = (start_ref[...] + acc_ref[...]).astype(LOW)
        for copy in copies:
            copy.start()

    if not chunks:
        targets[0][...] = nn(normed_t[...], pre_ref[...]).astype(LOW)
        targets[1][...] = nn(grad_t[...], hidden_ref[...]).astype(LOW).T
    else:
        held_ref, held_sems = held
        length = width // chunks
        part = share // 8
        fold = share - width
        top = length + REST
        for start in range(0, share, BLOCK):
            up_grad = nn(normed_t[...], pre_ref[:, start : start + BLOCK]).astype(LOW)
            for chunk in range(chunks):
                piece = up_grad[length * chunk : length * (chunk + 1)]
                inside = min(width - start, BLOCK)
                store_piece(
                    place_ref, held_ref, step, chunk,
                    slice(0, length), slice(start, start + inside), piece[:, :inside],
                )
                if inside < BLOCK:
                    for at in range(width // fold):
                        rows = REST * at
                        store_piece(
                            place_ref, held_ref, step, chunk,
                            slice(length, top), slice(fold * at, fold * (at + 1)),
                            piece[rows : rows + REST, inside:],
                        )
        up_region = (slice(None), slice(0, top))
        hand_out(place_ref, held_ref, targets, held_sems.at[step, 0], step, up_region)
        for start in range(0, share, BLOCK):
            down_grad = nn(grad_t[...], hidden_ref[:, start : start + BLOCK]).astype(LOW).T
            for row in range(start, start + BLOCK, 32):
                chunk, inside = 2 * step + row // (share // 2), row % (share // 2)
                base = top + inside % part
                store_piece(
                    place_ref, held_ref, inside // part, chunk,
                    slice(base, base + 32), slice(0, width), down_grad[row - start : row - start + 32],
                )
        for side in range(2):
            dp_at = lax.bitwise_xor(2 * step + side, place_ref[1])
            for half in range(2):
                pltpu.make_async_copy(
                    held_ref.at[half, :, dp_at, top:],
                    targets[half].at[:, dp_at, top:],
                    held_sems.at[step, 1 + 2 * side + half],
                ).start()

    @pl.when(step == steps - 1)
    def _():
        for copy in copies:
            copy.wait()
        if chunks:
            for at in range(4):
                hand_out_done(held_ref, targets, held_sems.at[at, 0], up_region)
                for index in range(1, 5):
                    pltpu.make_async_copy(
                        held_ref.at[0, :, 0, top:], targets[0].at[:, 0, top:], held_sems.at[at, index]
                    ).wait()


def cross_backward_kernel(
    back_ref, after_cross_ref, gain_feed_ref, grad_ref, after_self_ref, gain_cross_ref,
    q_ref, k_ref, v_ref, probs_ref, wq_ref, wk_ref, wv_ref, wo_ref,
    in_ref, dq_ref, dk_ref, dv_ref, memory_ref, grad_self_ref,
):
    grad = grad_ref[...].astype(FULL) + norm_backward(
        back_ref[...], after_cross_ref[...], gain_feed_ref[...]
    )
    branch = grad.astype(LOW)
    in_ref[...] = branch
    query_grad, key_grad, value_grad = attend_back(
        nt(branch, wo_ref[...]).astype(LOW), q_ref[...], k_ref[...], v_ref[...], probs_ref
    )
    dq_ref[...], dk_ref[...], dv_ref[...] = query_grad, key_grad, value_grad
    memory_ref[...] = (nt(key_grad, wk_ref[...]) + nt(value_grad, wv_ref[...])).astype(LOW)
    grad_self_ref[...] = grad + norm_backward(
        nt(query_grad, wq_ref[...]), after_self_ref[...], gain_cross_ref[...]
    )


def self_backward_kernel(
    grad_ref, q_ref, k_ref, v_ref, probs_ref, wo_ref, in_ref, dq_ref, dk_ref, dv_ref
):
    branch = grad_ref[...].astype(LOW)
    in_ref[...] = branch
    dq_ref[...], dk_ref[...], dv_ref[...] = attend_back(
        nt(branch, wo_ref[...]).astype(LOW), q_ref[...], k_ref[...], v_ref[...], probs_ref
    )


def input_grad_kernel(dq_ref, dk_ref, dv_ref, wq_ref, wk_ref, wv_ref, x_ref, gain_ref, grad_ref, out_ref):
    inner = (
        nt(dq_ref[...], wq_ref[...]) + nt(dk_ref[...], wk_ref[...]) + nt(dv_ref[...], wv_ref[...])
    )
    back = norm_backward(inner, x_ref[...].astype(FULL), gain_ref[...])
    out_ref[...] = (grad_ref[...] + back).astype(LOW)


def weight_kernel(chunks, sources, place_ref, *refs):
    count = max(sources) + 1
    ins, targets, (left_ref, right_ref, sems, *held) = refs[: count + 4], refs[count + 4 : -5], refs[-5:]
    if not chunks:
        ins, targets, (left_ref, right_ref, sems) = refs[: count + 4], refs[count + 4 : -3], refs[-3:]
    width = right_ref.shape[2]
    copies = [
        pltpu.make_async_copy(ref, left_ref.at[at] if at < count else right_ref.at[at - count], sems.at[at])
        for at, ref in enumerate(ins)
    ]
    ready = set()
    for weight in range(4):
        for at in (sources[weight], count + weight):
            if at not in ready:
                copies[at].start()
                ready.add(at)
    ready = set()
    for weight in range(4):
        source = sources[weight]
        for at in (source, count + weight):
            if at not in ready:
                copies[at].wait()
                ready.add(at)
        for start in range(0, width, BLOCK):
            columns = slice(start, min(start + BLOCK, width))
            grad = tn(left_ref[source], right_ref[weight, :, columns]).astype(LOW)
            if not chunks:
                targets[0][weight, :, columns] = grad
                continue
            length = width // chunks
            for chunk in range(chunks):
                piece = grad[length * chunk : length * (chunk + 1)]
                if weight == 3:
                    rest = HEADS * MAIN + REST * chunk
                    piece = jnp.concatenate(
                        [grad[MAIN * chunk : MAIN * (chunk + 1)], grad[rest : rest + REST]], axis=0
                    )
                store_piece(place_ref, held[0], weight, chunk, slice(0, length), columns, piece)
        if chunks:
            hand_out(place_ref, held[0], targets, held[1].at[weight], weight, ())
    if chunks:
        for weight in range(4):
            hand_out_done(held[0], targets, held[1].at[weight], ())


def encoder_grad_kernel(place_ref, hits_ref, *refs):
    out_ref = refs[-1]
    step = pl.program_id(0)
    for turn in range(4):

        @pl.when(step == turn)
        def _():
            tokens = refs[turn].shape[0]
            rows = tokens // ROW_LEN
            owner = lax.bitwise_xor(place_ref[0], turn)
            for row in range(rows):
                here = slice(ROW_LEN * row, ROW_LEN * (row + 1))
                weight = 0.5 * hits_ref[owner * rows + row]
                out_ref[0, here, :] = weight * refs[turn][here, :].astype(FULL)


def final_kernel(place_ref, *refs):
    sources, weights, gains, targets = refs[:8], refs[8:13], refs[13:16], refs[16:-2]
    cross_ref, self_ref = refs[-2:]
    up_out, down_out = targets[8:10]
    length = up_out.shape[0]
    part = down_out.shape[0] // 4
    share = up_out.shape[1] // 4
    width = down_out.shape[1]
    fold = share - width
    for turn in range(4):
        early, late = sources[2 * turn : 2 * (turn + 1)]
        owner = lax.bitwise_xor(place_ref[0], turn)
        start = pl.multiple_of(owner * share, 128)
        down_end = length + REST + part
        up_out[:, pl.ds(start, width)] = early[:length, :].astype(FULL)
        for at in range(width // fold):
            up_out[REST * at : REST * (at + 1), pl.ds(pl.multiple_of(start + width, 128), fold)] = early[
                length : length + REST, fold * at : fold * (at + 1)
            ].astype(FULL)
        rows = pl.ds(pl.multiple_of(owner * part, 32), part)
        down_out[rows, :] = early[length + REST : down_end, :].astype(FULL)
        cross_ref[owner] = early[down_end:, :]
        self_ref[owner] = late[...]
    order = order_matrix(cross_ref.shape[2], True)
    for at in range(3):
        targets[at][...] = nn(self_ref[at], order)
        targets[4 + at][...] = nn(cross_ref[at], order)
    targets[3][...] = self_ref[3].astype(FULL)
    targets[7][...] = cross_ref[3].astype(FULL)

    def gain_grad(pairs, gain_ref, target):
        total = sum(
            jnp.sum(weight.astype(FULL) * grad.astype(FULL), axis=1, keepdims=True)
            for weight, grad in pairs
        )
        turned = jnp.broadcast_to(total, (total.shape[0], 128)).T
        target[0] = turned[:1] / gain_ref[0]

    gain_grad([(weights[at][...], self_ref[at]) for at in range(3)], gains[0], targets[10])
    gain_grad([(weights[3][...], cross_ref[0])], gains[1], targets[11])
    gain_grad([(weights[4][...], up_out[...])], gains[2], targets[12])


def whole(array):
    return pl.BlockSpec(array.shape, lambda *at: (0,) * array.ndim)


def by_row(array):
    if array.ndim == 2:
        return pl.BlockSpec((ROW_LEN, array.shape[1]), lambda at, *_: (at, 0))
    return pl.BlockSpec(
        (1,) + array.shape[1:], lambda at, *_: (at,) + (0,) * (array.ndim - 1)
    )


def run(body, name, grid, ins, in_specs, outs, out_specs, flops, scratch=(), prefetch=(), after=()):
    moved = sum(array.size * array.dtype.itemsize for array in list(ins) + list(outs))
    first, last = len(prefetch) + len(ins), len(prefetch) + len(ins) + len(after)

    def ordered_body(*refs):
        body(*refs[:first], *refs[last:])

    return pl.pallas_call(
        ordered_body,
        name=name,
        out_shape=outs,
        grid_spec=pltpu.PrefetchScalarGridSpec(
            num_scalar_prefetch=len(prefetch),
            grid=grid,
            in_specs=list(in_specs) + [pl.BlockSpec(memory_space=pl.ANY)] * len(after),
            out_specs=out_specs,
            scratch_shapes=scratch,
        ),
        compiler_params=pltpu.CompilerParams(vmem_limit_bytes=VMEM_BYTES),
        cost_estimate=pl.CostEstimate(
            flops=int(flops * WEIGHT), bytes_accessed=int(moved * WEIGHT), transcendentals=0
        ),
    )(*prefetch, *ins, *after)


def shape_of(shape, dtype=LOW):
    return jax.ShapeDtypeStruct(tuple(shape), dtype)


def row_call(body, name, rowed, fixed, outs, flops, order, after=()):
    ins, specs = [], []
    rowed, fixed = list(rowed), list(fixed)
    for kind in order:
        array = rowed.pop(0) if kind == "r" else fixed.pop(0)
        ins.append(array)
        specs.append(by_row(array) if kind == "r" else whole(array))
    tokens = outs[0].shape[0]
    return run(
        body,
        name,
        (tokens // ROW_LEN,),
        ins,
        specs,
        outs,
        [by_row(out) for out in outs],
        flops,
        after=after,
    )


def permuted(value, axes, sizes, flip):
    count = math.prod(sizes)
    return lax.ppermute(value, axes, [(at, at ^ flip) for at in range(count)])


def added(parts):
    total = parts[0].astype(FULL)
    for part in parts[1:]:
        total = total + part.astype(FULL)
    return total.astype(LOW)


def on_device(
    layer_size,
    dp_size,
    inputs,
    encoder_out,
    query_self,
    key_self,
    value_self,
    out_self,
    query_cross,
    key_cross,
    value_cross,
    out_cross,
    feed_up,
    feed_down,
    gain_self,
    gain_cross,
    gain_feed,
    seg_target,
    seg_source,
    subnet_of_row,
    chosen_layers,
    out_grad,
):
    tokens, width = inputs.shape
    rows = tokens // ROW_LEN
    layer_at = lax.axis_index("layer")
    dp_at = lax.axis_index("dp")
    place = jnp.stack([layer_at, dp_at]).astype(jnp.int32)
    axes, sizes = ("dp", "layer"), (dp_size, layer_size)

    def across(value, layer_flip, dp_flip=0):
        return permuted(value, axes, sizes, dp_flip * layer_size + layer_flip)

    picked = jnp.sum(
        (chosen_layers[:, :, None] == jnp.arange(layer_size)[None, None, :]).astype(FULL), axis=1
    )
    row_pick = (subnet_of_row[:, None] == jnp.arange(chosen_layers.shape[0])[None, :]).astype(FULL)
    block_hits = jnp.sum(row_pick[:, :, None] * picked[None], axis=1)
    own_layer = encoder_out.reshape(layer_size, rows, ROW_LEN, width)

    def own_block(flip):
        return lax.dynamic_index_in_dim(own_layer, layer_at ^ flip, 0, keepdims=False)

    def hits_of(flip, layer_flip):
        hits = lax.dynamic_slice_in_dim(block_hits, (layer_at ^ flip) * rows, rows, 0)
        hits = lax.dynamic_slice_in_dim(hits, layer_at ^ layer_flip, 1, 1)
        return 0.5 * hits[:, :, None]

    def chip_sum(flip, arrived):
        total = hits_of(flip, 0) * own_block(flip).astype(FULL)
        total = total + hits_of(flip, 1) * arrived.astype(FULL)
        return total.astype(LOW).reshape(tokens, width)

    far_half = across(own_block(3), 1)
    near_half = across(own_block(1), 1)
    far_memory = across(chip_sum(2, far_half), 2)
    near_memory = chip_sum(0, near_half)

    weights = [query_self, key_self, value_self, query_cross, key_cross, value_cross, out_self, out_cross]
    ordered = run(
        order_kernel,
        "order_weights",
        (1,),
        weights,
        [whole(array) for array in weights],
        [shape_of(array.shape) for array in weights],
        [whole(array) for array in weights],
        12 * width**3,
    )
    wq_self, wk_self, wv_self, wq_cross, wk_cross, wv_cross, wo_self, wo_cross = ordered
    target = seg_target.reshape(rows, 1, ROW_LEN)
    source = seg_source.reshape(rows, 1, ROW_LEN)
    g_self, g_cross, g_feed = (gain.reshape(1, width) for gain in (gain_self, gain_cross, gain_feed))
    flat = shape_of((tokens, width))
    wide = shape_of((tokens, width), FULL)
    probs = shape_of((rows, HEADS, ROW_LEN, ROW_LEN))
    dense_flops = 2 * tokens * width * width
    head_flops = 2 * tokens * ROW_LEN * ROW_LEN * HEADS

    normed_self, q_self, k_self, v_self, probs_self, attn_self, after_self, normed_cross, q_cross = row_call(
        self_forward_kernel,
        "self_forward",
        (inputs, target),
        (g_self, g_cross, wq_self, wk_self, wv_self, wo_self, wq_cross),
        [flat, flat, flat, flat, probs, flat, wide, flat, flat],
        5 * dense_flops + 2 * head_flops,
        "rrfffffff",
    )
    memory, k_cross, v_cross, probs_cross, attn_cross, after_cross, normed_feed = row_call(
        cross_forward_kernel,
        "cross_forward",
        (near_memory, far_memory, q_cross, after_self, target, source),
        (g_feed, wk_cross, wv_cross, wo_cross),
        [flat, flat, flat, probs, flat, wide, flat],
        3 * dense_flops + 2 * head_flops,
        "rrrrrrffff",
    )

    chunks = dp_size if dp_size == HEADS and layer_size == 4 else 0
    hidden = feed_up.shape[1]
    share = hidden // 4
    if chunks:
        length, part = width // chunks, share // 8
        feed_outs = [shape_of((2, chunks, length + REST + part, width))] * 2
        feed_specs = [pl.BlockSpec(memory_space=pl.ANY)] * 2
        weight_outs = [shape_of((2, chunks, length, width))] * 2
        weight_specs = feed_specs
    else:
        feed_outs = [shape_of(feed_up.shape), shape_of(feed_down.shape)]
        feed_specs = [
            pl.BlockSpec((width, share), lambda at, *_: (0, at)),
            pl.BlockSpec((share, width), lambda at, *_: (at, 0)),
        ]
        weight_outs = [shape_of((4, width, width))]
        weight_specs = [whole(out) for out in weight_outs]

    def held(outs, sems):
        if not chunks:
            return []
        return [pltpu.VMEM((2,) + outs[0].shape, LOW), pltpu.SemaphoreType.DMA(sems)]

    layer_out, back_feed, *feed_grads = run(
        functools.partial(feed_kernel, chunks),
        "feed",
        (4,),
        [normed_feed, out_grad, feed_up, feed_down, after_cross],
        [
            whole(normed_feed),
            whole(out_grad),
            pl.BlockSpec((width, share), lambda at, *_: (0, at)),
            pl.BlockSpec((share, width), lambda at, *_: (at, 0)),
            pl.BlockSpec(memory_space=pl.ANY),
        ],
        [flat, wide] + feed_outs,
        [pl.BlockSpec(memory_space=pl.ANY)] * 2 + feed_specs,
        12 * tokens * width * hidden,
        scratch=[
            pltpu.VMEM((tokens, width), FULL),
            pltpu.VMEM((tokens, width), FULL),
            pltpu.VMEM((tokens, width), LOW),
            pltpu.VMEM((tokens, width), FULL),
            pltpu.VMEM((width, tokens), LOW),
            pltpu.VMEM((width, tokens), LOW),
            pltpu.VMEM((tokens, share), LOW),
            pltpu.VMEM((tokens, share), LOW),
            pltpu.SemaphoreType.DMA((3,)),
        ]
        + held(feed_outs, (4, 5)),
        prefetch=(place,),
    )

    def weight_call(name, sources, lefts, rights, after=()):
        ins = list(lefts) + list(rights)
        return run(
            functools.partial(weight_kernel, chunks, sources),
            name,
            (1,),
            ins,
            [pl.BlockSpec(memory_space=pl.ANY)] * len(ins),
            weight_outs,
            weight_specs,
            4 * dense_flops,
            scratch=[
                pltpu.VMEM((len(lefts), tokens, width), LOW),
                pltpu.VMEM((4, tokens, width), LOW),
                pltpu.SemaphoreType.DMA((len(ins),)),
            ]
            + held(weight_outs, (4,)),
            prefetch=(place,),
            after=after,
        )

    flips = {"core": (1, 0), "x": (2, 0), "y": (0, 1), "z_near": (0, 2), "z_far": (0, 4)}

    def from_core(grads, rows=slice(None)):
        if not chunks:
            return None
        keep, send = grads
        parts = [part[:, :, rows] for part in (keep, across(send, 1))]
        return (["x", "z_far", "z_near", "y"], [part.reshape((2, 2, 2, 2) + part.shape[2:]) for part in parts])

    def to_send(flow, axis):
        if not chunks:
            return None
        left, parts = flow
        at = left.index(axis)
        return added([lax.index_in_dim(part, 1, at, keepdims=False) for part in parts])

    def received(flow, axis, sent):
        if not chunks:
            return None
        left, parts = flow
        at = left.index(axis)
        kept = [lax.index_in_dim(part, 0, at, keepdims=False) for part in parts]
        return (left[:at] + left[at + 1 :], kept + [across(sent, *flips[axis])])

    def before(*sent):
        return [value for value in sent if value is not None]

    chip_grads = feed_grads
    if chunks:
        chip_grads = (feed_grads[0], feed_grads[1])
    cross_in, dq_cross, dk_cross, dv_cross, memory_grad, grad_after_self = row_call(
        cross_backward_kernel,
        "cross_backward",
        (back_feed, after_cross, out_grad, after_self, q_cross, k_cross, v_cross, probs_cross),
        (g_feed, g_cross, wq_cross, wk_cross, wv_cross, wo_cross),
        [flat, flat, flat, flat, flat, wide],
        4 * dense_flops + 4 * head_flops,
        "rrfrrfrrrrffff",
    )
    feed_all = from_core(chip_grads)
    feed_a = feed_b = None
    if chunks:
        middle = feed_all[1][0].shape[4] // 2
        feed_a = (feed_all[0], [part[..., :middle, :] for part in feed_all[1]])
        feed_b = (feed_all[0], [part[..., middle:, :] for part in feed_all[1]])
    a_sent, b_sent = to_send(feed_a, "y"), to_send(feed_b, "z_near")
    cross_grads = weight_call(
        "cross_weights",
        (0, 1, 1, 2),
        (normed_cross, memory, attn_cross),
        (dq_cross, dk_cross, dv_cross, cross_in),
        after=before(a_sent, b_sent),
    )
    feed_a, feed_b = received(feed_a, "y", a_sent), received(feed_b, "z_near", b_sent)
    cross_flow = from_core(cross_grads)
    self_in, dq_self, dk_self, dv_self = row_call(
        self_backward_kernel,
        "self_backward",
        (grad_after_self, q_self, k_self, v_self, probs_self),
        (wo_self,),
        [flat, flat, flat, flat],
        dense_flops + 4 * head_flops,
        "rrrrrf",
        after=cross_grads[:1],
    )
    c_sent = to_send(cross_flow, "y")
    self_grads = weight_call(
        "self_weights",
        (0, 0, 0, 1),
        (normed_self, attn_self),
        (dq_self, dk_self, dv_self, self_in),
        after=before(c_sent),
    )
    cross_flow = received(cross_flow, "y", c_sent)
    self_flow = from_core(self_grads)
    a_sent, b_sent = to_send(feed_a, "x"), to_send(feed_b, "z_far")
    (input_grad,) = row_call(
        input_grad_kernel,
        "input_grad",
        (dq_self, dk_self, dv_self, inputs, grad_after_self),
        (wq_self, wk_self, wv_self, g_self),
        [flat],
        3 * dense_flops,
        "rrrfffrfr",
        after=before(self_grads[0], a_sent, b_sent),
    )
    feed_a, feed_b = received(feed_a, "x", a_sent), received(feed_b, "z_far", b_sent)
    s_sent = to_send(self_flow, "x")

    from_chip = across(memory_grad, 2)
    arrived = [memory_grad, across(memory_grad, 1), from_chip, across(from_chip, 1)]
    own_hits = lax.dynamic_slice_in_dim(block_hits, layer_at, 1, 1)[:, 0]

    encoder_shape = shape_of(encoder_out.shape, FULL)
    (encoder_grad,) = run(
        encoder_grad_kernel,
        "encoder_grad",
        (4,),
        arrived,
        [whole(array) for array in arrived],
        [encoder_shape],
        [pl.BlockSpec((1, tokens, width), lambda at, place, hits: (0, place[0] ^ at, 0))],
        encoder_out.size,
        prefetch=(place, own_hits),
        after=before(s_sent, input_grad),
    )

    if chunks:
        self_flow = received(self_flow, "x", s_sent)

        def finish(flow, axes):
            for axis in axes:
                flow = received(flow, axis, to_send(flow, axis))
            return flow

        feed_a = finish(feed_a, ("z_near", "z_far"))
        feed_b = finish(feed_b, ("y", "x"))
        cross_flow = finish(cross_flow, ("x", "z_near", "z_far"))
        self_flow = finish(self_flow, ("y", "z_near", "z_far"))
        early = jnp.concatenate([added(flow[1]) for flow in (feed_a, feed_b, cross_flow)], axis=0)
        late = added(self_flow[1])
        from_chip = across(early, 2)
        gathered = []
        for first, second in (
            (early, late),
            (across(early, 1), across(late, 1)),
            (from_chip, across(late, 2)),
            (across(from_chip, 1), across(late, 3)),
        ):
            gathered += [first, second]
        length = width // chunks
        square = shape_of((length, width), FULL)
        outs = [square] * 8 + [
            shape_of((length, hidden), FULL),
            shape_of((hidden // chunks, width), FULL),
        ]
        outs += [shape_of((1, 1, length), FULL)] * 3
        chunk_weights = [wq_self, wk_self, wv_self, wq_cross, feed_up]
        gains = [gain.reshape(chunks, 1, length) for gain in (gain_self, gain_cross, gain_feed)]
        finals = run(
            final_kernel,
            "final",
            (1,),
            gathered + chunk_weights + gains,
            [whole(array) for array in gathered]
            + [
                pl.BlockSpec((length, array.shape[1]), lambda at, place: (place[1], 0))
                for array in chunk_weights
            ]
            + [pl.BlockSpec((1, 1, length), lambda at, place: (place[1], 0, 0))] * 3,
            outs,
            [whole(out) for out in outs],
            12 * length * width * width,
            scratch=[pltpu.VMEM((4, length, width), LOW)] * 2,
            prefetch=(place,),
        )
        weight_grads = list(finals[:10])
        gain_grads = [value.reshape(length) for value in finals[10:]]
    else:
        back_order = order_matrix(width, True)

        def total(grad):
            part = lax.psum_scatter(grad.astype(FULL), "dp", scatter_dimension=0, tiled=True)
            return lax.psum(part.astype(LOW), "layer").astype(FULL)

        def natural(grads):
            back = [nn(grads[0][at], back_order).astype(LOW) for at in range(3)]
            return [total(grad) for grad in back + [nn(back_order.T, grads[0][3]).astype(LOW)]]

        grads_self, grads_cross = natural(self_grads), natural(cross_grads)
        weight_grads = grads_self + grads_cross + [total(grad) for grad in feed_grads]
        length = width // dp_size

        def my_rows(array):
            return lax.dynamic_slice_in_dim(array, dp_at * length, length, 0).astype(FULL)

        def gain_total(pairs, gain):
            sums = sum(jnp.sum(my_rows(weight) * grad, axis=1) for weight, grad in pairs)
            return sums / my_rows(gain)

        gain_grads = [
            gain_total(zip((query_self, key_self, value_self), grads_self), gain_self),
            gain_total([(query_cross, grads_cross[0])], gain_cross),
            gain_total([(feed_up, weight_grads[8])], gain_feed),
        ]
    return (layer_out, input_grad, encoder_grad, *weight_grads, *gain_grads)


def solution(mesh):
    in_specs = (
        P(("dp", "layer"), None),
        P("layer", "dp", None),
        *[P()] * 13,
        P(("dp", "layer"), None),
        P(("dp", "layer"), None),
        P("dp"),
        P(),
        P(("dp", "layer"), None),
    )
    out_specs = (
        P(("dp", "layer"), None),
        P(("dp", "layer"), None),
        P("layer", "dp", None),
        *[P("dp", None)] * 10,
        *[P("dp")] * 3,
    )
    body = functools.partial(on_device, mesh.shape["layer"], mesh.shape["dp"])
    return jax.shard_map(
        body, mesh=mesh, in_specs=in_specs, out_specs=out_specs, check_vma=False
    )
```

```python
import functools
import math

import jax
import jax.numpy as jnp
from jax import lax
from jax.experimental import pallas as pl
from jax.experimental.pallas import tpu as pltpu
from jax.sharding import PartitionSpec as P

HEADS = 8
HEAD = 80
MAIN = 64
REST = 16
ROW_LEN = 256
BLOCK = 256
UNITS = 384
SCALE = 1.0 / math.sqrt(HEAD)
LOW = jnp.bfloat16
FULL = jnp.float32
VMEM_BYTES = 56 * 1024 * 1024
WEIGHT = 1.0
LIGHT = 0.05
FEED_PLANE_ROWS = 144
WEIGHT_PLANE_ROWS = 144


def dot(left, right, left_dim, right_dim):
    return lax.dot_general(
        left, right, (((left_dim,), (right_dim,)), ((), ())), preferred_element_type=FULL
    )


def nn(left, right):
    return dot(left, right, 1, 0)


def nt(left, right):
    return dot(left, right, 1, 1)


def tn(left, right):
    return dot(left, right, 0, 0)


def norm_parts(value):
    centred = value - jnp.mean(value, axis=-1, keepdims=True)
    inverse = lax.rsqrt(jnp.mean(centred * centred, axis=-1, keepdims=True) + 1e-05)
    return (centred * inverse, inverse)


def norm_forward(value, gain):
    return (norm_parts(value)[0] * gain).astype(LOW)


def norm_backward(grad, value, gain):
    normed, inverse = norm_parts(value)
    scaled = grad * gain
    inner = (
        scaled
        - jnp.mean(scaled, axis=-1, keepdims=True)
        - normed * jnp.mean(scaled * normed, axis=-1, keepdims=True)
    )
    return inner * inverse


def source_column(position):
    rest = position - HEADS * MAIN
    return jnp.where(
        rest < 0,
        HEAD * (position // MAIN) + position % MAIN,
        HEAD * (rest // REST) + MAIN + rest % REST,
    )


def order_matrix(width, transposed):
    rows = lax.broadcasted_iota(jnp.int32, (width, width), 0)
    columns = lax.broadcasted_iota(jnp.int32, (width, width), 1)
    if transposed:
        rows, columns = columns, rows
    return (rows == source_column(columns)).astype(FULL).astype(LOW)


def head_groups(array, head):
    pair = head // 2
    return jnp.concatenate(
        [array[:, 2 * MAIN * pair : 2 * MAIN * (pair + 1)], array[:, HEADS * MAIN :]], axis=1
    )


def head_mask(head):
    lane = lax.broadcasted_iota(jnp.int32, (1, 2 * MAIN + HEADS * REST), 1)
    rest = lane - 2 * MAIN
    owner = jnp.where(rest < 0, 2 * (head // 2) + lane // MAIN, rest // REST)
    return (owner == head).astype(FULL).astype(LOW)


def same_segment(key_seg, query_seg):
    shape = (16, key_seg.shape[1])
    number = lax.broadcasted_iota(jnp.int32, shape, 0)
    key_hot = (number == key_seg).astype(FULL).astype(LOW)
    query_hot = (number == query_seg).astype(FULL).astype(LOW)
    return tn(key_hot, query_hot)


def merge_pairs(parts):
    mains = [part[:, : 2 * MAIN] for part in parts]
    rests = [part[:, 2 * MAIN :] for part in parts]
    while len(rests) > 1:
        rests = [rests[i] + rests[i + 1] for i in range(0, len(rests), 2)]
    return jnp.concatenate(mains + rests, axis=1)


def attend(queries, keys, values, bias, probs_ref):
    parts = []
    for pair in range(HEADS // 2):
        pair_probs, pair_values = [], []
        for head in (2 * pair, 2 * pair + 1):
            mask = head_mask(head)
            scores = nt(head_groups(keys, head), head_groups(queries, head) * mask) * SCALE + bias
            raised = jnp.exp(scores - jnp.max(scores, axis=0, keepdims=True))
            probs = (raised * (1.0 / jnp.sum(raised, axis=0, keepdims=True))).astype(LOW)
            probs_ref[0, head] = probs
            pair_probs.append(probs)
            pair_values.append(head_groups(values, head) * mask)
        parts.append(
            tn(jnp.concatenate(pair_probs, axis=0), jnp.concatenate(pair_values, axis=0))
        )
    return merge_pairs(parts).astype(LOW)


def attend_back(grad, queries, keys, values, probs_ref):
    query_parts, key_parts, value_parts = [], [], []
    for pair in range(HEADS // 2):
        pair_probs, pair_slopes, pair_grads, pair_queries, pair_keys = [], [], [], [], []
        for head in (2 * pair, 2 * pair + 1):
            mask = head_mask(head)
            grad_head = head_groups(grad, head) * mask
            probs = probs_ref[0, head]
            wide = probs.astype(FULL)
            prob_grad = nt(head_groups(values, head), grad_head)
            delta = jnp.sum(prob_grad * wide, axis=0, keepdims=True)
            pair_probs.append(probs)
            pair_slopes.append((wide * (prob_grad - delta)).astype(LOW))
            pair_grads.append(grad_head)
            pair_queries.append(head_groups(queries, head) * mask)
            pair_keys.append(head_groups(keys, head) * mask)
        query_parts.append(
            tn(jnp.concatenate(pair_slopes, axis=0), jnp.concatenate(pair_keys, axis=0))
        )
        key_parts.append(
            nn(jnp.concatenate(pair_slopes, axis=1), jnp.concatenate(pair_queries, axis=0))
        )
        value_parts.append(
            nn(jnp.concatenate(pair_probs, axis=1), jnp.concatenate(pair_grads, axis=0))
        )
    return (
        (merge_pairs(query_parts) * SCALE).astype(LOW),
        (merge_pairs(key_parts) * SCALE).astype(LOW),
        merge_pairs(value_parts).astype(LOW),
    )


PLANE = ((1, 1), (1, 0), (0, 1))


def pick_matrix(core, transposed):
    shape = (2 * UNITS, UNITS)
    if transposed:
        shape = shape[::-1]
    unit = lax.broadcasted_iota(jnp.int32, shape, int(transposed))
    taken = lax.broadcasted_iota(jnp.int32, shape, 1 - int(transposed))
    half = UNITS // 2
    source = UNITS * (taken // half) + half * core + taken % half
    return (unit == source).astype(FULL).astype(LOW)


def order_kernel(place_ref, *refs):
    sources, targets, refs = refs[:9], refs[9:18], refs[18:]
    froms, tos, refs = (*refs[:2], refs[2]), (*refs[3:5], refs[5]), refs[6:]
    in_sems, out_sems = refs
    columns_in, rows_in, up_in = froms
    columns_out, rows_out, up_out = tos
    ins = [columns_in.at[at] for at in range(6)] + [rows_in.at[at] for at in range(2)] + [up_in]
    outs = [columns_out.at[at] for at in range(6)] + [rows_out.at[at] for at in range(2)] + [up_out]
    fetches = [pltpu.make_async_copy(*pair, in_sems.at[at]) for at, pair in enumerate(zip(sources, ins))]
    stores = [pltpu.make_async_copy(*pair, out_sems.at[at]) for at, pair in enumerate(zip(outs, targets))]
    for fetch in fetches:
        fetch.start()
    order = order_matrix(columns_in.shape[1], False)
    for at in range(6):
        fetches[at].wait()
        columns_out[at] = nn(columns_in[at], order).astype(LOW)
        stores[at].start()
    for at in range(2):
        fetches[6 + at].wait()
        for head in range(HEADS):
            base = HEAD * head
            rows_out[at, MAIN * head : MAIN * (head + 1)] = rows_in[at, base : base + MAIN]
            rest = HEADS * MAIN + REST * head
            rows_out[at, rest : rest + REST] = rows_in[at, base + MAIN : base + HEAD]
        stores[6 + at].start()
    pick = pick_matrix(lax.bitwise_and(place_ref[0], 1), False)
    fetches[8].wait()
    for pair in range(up_in.shape[1] // (2 * UNITS)):
        columns = slice(2 * UNITS * pair, 2 * UNITS * (pair + 1))
        up_out[:, UNITS * pair : UNITS * (pair + 1)] = nn(up_in[:, columns], pick).astype(LOW)
    stores[8].start()
    for store in stores:
        store.wait()


def self_forward_kernel(
    x_ref, seg_ref, gain_ref, next_gain_ref, wq_ref, wk_ref, wv_ref, wo_ref, next_wq_ref,
    normed_ref, q_ref, k_ref, v_ref, probs_ref, attn_ref, after_ref, next_normed_ref, next_q_ref,
):
    value = x_ref[...].astype(FULL)
    normed = norm_forward(value, gain_ref[...])
    normed_ref[...] = normed
    queries = nn(normed, wq_ref[...]).astype(LOW)
    keys = nn(normed, wk_ref[...]).astype(LOW)
    values = nn(normed, wv_ref[...]).astype(LOW)
    q_ref[...], k_ref[...], v_ref[...] = queries, keys, values
    seg = seg_ref[pl.ds(pl.program_id(0), 1), :]
    key_at = lax.broadcasted_iota(jnp.int32, (ROW_LEN, ROW_LEN), 0)
    query_at = lax.broadcasted_iota(jnp.int32, (ROW_LEN, ROW_LEN), 1)
    allowed = (same_segment(seg, seg) > 0.5) & (key_at <= query_at)
    attn = attend(queries, keys, values, jnp.where(allowed, 0.0, -1e9), probs_ref)
    attn_ref[...] = attn
    after = value + nn(attn, wo_ref[...])
    after_ref[...] = after
    next_normed = norm_forward(after, next_gain_ref[...])
    next_normed_ref[...] = next_normed
    next_q_ref[...] = nn(next_normed, next_wq_ref[...]).astype(LOW)


def cross_forward_kernel(
    place_ref, hits_ref, own_ref, near_ref, far_ref, q_ref, after_ref, seg_target_ref, seg_source_ref, gain_ref,
    wk_ref, wv_ref, wo_ref, memory_ref, k_ref, v_ref, probs_ref, attn_ref, next_after_ref, next_normed_ref,
):
    step = pl.program_id(0)
    own = 0.5 * hits_ref[0, step] * own_ref[0].astype(FULL)
    near = 0.5 * hits_ref[1, step] * near_ref[0].astype(FULL)
    memory = (own + near + far_ref[...].astype(FULL)).astype(LOW)
    memory_ref[...] = memory
    keys = nn(memory, wk_ref[...]).astype(LOW)
    values = nn(memory, wv_ref[...]).astype(LOW)
    k_ref[...], v_ref[...] = keys, values
    row = pl.ds(pl.program_id(0), 1)
    allowed = same_segment(seg_source_ref[row, :], seg_target_ref[row, :]) > 0.5
    attn = attend(q_ref[...], keys, values, jnp.where(allowed, 0.0, -1e9), probs_ref)
    attn_ref[...] = attn
    after = after_ref[...] + nn(attn, wo_ref[...])
    next_after_ref[...] = after
    next_normed_ref[...] = norm_forward(after, gain_ref[...])


def store_piece(place_ref, held_ref, quarter, chunk, rows, columns, piece):
    owner = lax.bitwise_xor(place_ref[0], quarter)
    dp_at = lax.bitwise_xor(chunk, lax.bitwise_and(place_ref[1], 1))
    held_ref[
        lax.bitwise_and(owner, 1), lax.shift_right_logical(owner, 1), dp_at, rows, columns
    ] = piece


def store_feed(place_ref, held_ref, x_of, chunk, rows, columns, piece):
    x_at = lax.bitwise_xor(x_of, lax.shift_right_logical(place_ref[0], 1))
    y_at = lax.bitwise_xor(lax.bitwise_and(chunk, 1), lax.bitwise_and(place_ref[1], 1))
    held_ref[x_at, y_at, lax.shift_right_logical(chunk, 1), rows, columns] = piece


def hand_out(place_ref, held_ref, targets, sem, quarter, region):
    owner = lax.bitwise_xor(place_ref[0], quarter)
    x_at = lax.shift_right_logical(owner, 1)
    for half in range(2):

        @pl.when(lax.bitwise_and(owner, 1) == half)
        def _():
            pltpu.make_async_copy(
                held_ref.at[(half, x_at) + region], targets[half].at[(x_at,) + region], sem
            ).start()


def hand_out_done(held_ref, targets, sem, region):
    pltpu.make_async_copy(held_ref.at[(0, 0) + region], targets[0].at[(0,) + region], sem).wait()


def feed_kernel(chunks, place_ref, *refs):
    normed_refs, grad_refs, up_ref, down_refs, after_ref, refs = refs[:2], refs[2:4], refs[4], refs[5:9], refs[9], refs[10:]
    own_refs, send_refs, refs = refs[:2], refs[2:4], refs[4:]
    targets, refs = (refs[:5], refs[5:]) if chunks else (refs[:2], refs[2:])
    acc_ref, total_ref, low_ref, normed_t, grad_t, hidden_ref, pre_ref, sems, *held = refs
    step, steps = pl.program_id(0), pl.num_programs(0)
    tokens, width = normed_refs[0].shape
    share = up_ref.shape[1]
    fetch = pltpu.make_async_copy(after_ref, acc_ref.at[0], sems.at[0])
    copies = [
        pltpu.make_async_copy(source, target, sems.at[1 + at])
        for at, (source, target) in enumerate(
            zip((low_ref.at[0], total_ref.at[0], low_ref.at[1], acc_ref.at[0]), (send_refs[1], own_refs[1], send_refs[0], own_refs[0]))
        )
    ]

    @pl.when(step == 0)
    def _():
        fetch.start()
        acc_ref[1] = jnp.zeros_like(acc_ref[1])
        total_ref[...] = jnp.zeros_like(total_ref)
        for side in range(2):
            for start in range(0, tokens, BLOCK):
                rows, columns = slice(start, start + BLOCK), slice(side * tokens + start, side * tokens + start + BLOCK)
                normed_t[:, columns] = normed_refs[side][rows, :].T
                grad_t[:, columns] = grad_refs[side][rows, :].T
        fetch.wait()

    down = jnp.concatenate([ref[0] for ref in down_refs], axis=0)
    for side in (1, 0):
        for start in range(0, tokens, 2 * BLOCK):
            rows = slice(start, start + 2 * BLOCK)
            both = slice(side * tokens + start, side * tokens + start + 2 * BLOCK)
            pre = nn(normed_refs[side][rows, :], up_ref[...])
            hidden_grad = nt(grad_refs[side][rows, :], down)
            square = pre * pre
            slope = math.sqrt(2.0 / math.pi)
            bend = jnp.tanh(pre * (slope + slope * 0.044715 * square))
            half = 0.5 + 0.5 * bend
            hidden = (pre * half).astype(LOW)
            rate = half + pre * half * (1.0 - bend) * (slope + slope * 3 * 0.044715 * square)
            pre_grad = (hidden_grad * rate).astype(LOW)
            hidden_ref[both, :] = hidden
            pre_ref[both, :] = pre_grad
            acc_ref[side, rows, :] += nn(hidden, down)
            total_ref[side, rows, :] += nt(pre_grad, up_ref[...])

    @pl.when(step == steps - 1)
    def _():
        low_ref[0] = total_ref[1].astype(LOW)
        low_ref[1] = acc_ref[1].astype(LOW)
        for copy in copies:
            copy.start()

    if not chunks:
        targets[0][...] = nn(normed_t[...], pre_ref[...]).astype(LOW)
        targets[1][...] = nn(grad_t[...], hidden_ref[...]).astype(LOW).T
    else:
        held_ref, held_sems = held
        length = width // chunks
        part = UNITS // 4
        fold = share - width
        top = length + REST
        for start in range(0, share, BLOCK):
            columns = slice(start, start + BLOCK)
            up_grad = nn(normed_t[...], pre_ref[:, columns]).astype(LOW)
            for chunk in range(chunks):
                piece = up_grad[length * chunk : length * (chunk + 1)]
                inside = min(width - start, BLOCK)
                store_feed(
                    place_ref, held_ref, step, chunk,
                    slice(0, length), slice(start, start + inside), piece[:, :inside],
                )
                if inside < BLOCK:
                    for at in range(width // fold):
                        rows = REST * at
                        store_feed(
                            place_ref, held_ref, step, chunk,
                            slice(length, top), slice(fold * at, fold * (at + 1)),
                            piece[rows : rows + REST, inside:],
                        )
            down_grad = nn(grad_t[...], hidden_ref[:, columns]).astype(LOW).T
            for row in range(start, start + BLOCK, 32):
                chunk, inside = 4 * step + row // (2 * part), row % (2 * part)
                base = top + inside % part
                store_feed(
                    place_ref, held_ref, inside // part, chunk,
                    slice(base, base + 32), slice(0, width), down_grad[row - start : row - start + 32],
                )

    @pl.when(step == steps - 1)
    def _():
        if chunks:
            plane_rows = targets[0].shape[1]
            outs = []
            for at, (x_at, y_at) in enumerate(((0, 0),) + PLANE):
                piece = held_ref.at[x_at, y_at]
                outs.append(
                    pltpu.make_async_copy(piece.at[:, plane_rows:], targets[4].at[:, x_at, y_at], held_sems.at[at])
                )
                outs.append(pltpu.make_async_copy(piece.at[:, :plane_rows], targets[at], held_sems.at[4 + at]))
            for copy in outs:
                copy.start()
            for copy in outs:
                copy.wait()
        for copy in copies:
            copy.wait()


def cross_backward_kernel(
    back_ref, back_other_ref, after_cross_ref, gain_feed_ref, grad_ref, after_self_ref, gain_cross_ref,
    q_ref, k_ref, v_ref, probs_ref, wq_ref, wk_ref, wv_ref, wo_ref,
    in_ref, dq_ref, dk_ref, dv_ref, memory_ref, grad_self_ref,
):
    grad = grad_ref[...].astype(FULL) + norm_backward(
        back_ref[...] + back_other_ref[...].astype(FULL), after_cross_ref[...], gain_feed_ref[...]
    )
    branch = grad.astype(LOW)
    in_ref[...] = branch
    query_grad, key_grad, value_grad = attend_back(
        nt(branch, wo_ref[...]).astype(LOW), q_ref[...], k_ref[...], v_ref[...], probs_ref
    )
    dq_ref[...], dk_ref[...], dv_ref[...] = query_grad, key_grad, value_grad
    memory_ref[...] = (nt(key_grad, wk_ref[...]) + nt(value_grad, wv_ref[...])).astype(LOW)
    grad_self_ref[...] = grad + norm_backward(
        nt(query_grad, wq_ref[...]), after_self_ref[...], gain_cross_ref[...]
    )


def input_grad_kernel(dq_ref, dk_ref, dv_ref, wq_ref, wk_ref, wv_ref, x_ref, gain_ref, grad_ref, out_ref):
    inner = (
        nt(dq_ref[...], wq_ref[...]) + nt(dk_ref[...], wk_ref[...]) + nt(dv_ref[...], wv_ref[...])
    )
    back = norm_backward(inner, x_ref[...].astype(FULL), gain_ref[...])
    out_ref[...] = (grad_ref[...] + back).astype(LOW)


def weight_product(chunks, place_ref, left, right, weight, base, target, held_ref):
    width = right.shape[1]
    for start in range(0, width, BLOCK):
        columns = slice(start, min(start + BLOCK, width))
        grad = tn(left[...], right[:, columns]).astype(LOW)
        if not chunks:
            target[weight, :, columns] = grad
            continue
        length = width // chunks
        for chunk in range(chunks):
            piece = grad[length * chunk : length * (chunk + 1)]
            if weight == 3:
                rest = HEADS * MAIN + REST * chunk
                piece = jnp.concatenate(
                    [grad[MAIN * chunk : MAIN * (chunk + 1)], grad[rest : rest + REST]], axis=0
                )
            store_piece(place_ref, held_ref, weight, chunk, slice(base, base + length), columns, piece)


def self_backward_kernel(
    chunks, place_ref, grad_ref, q_ref, k_ref, v_ref, probs_ref, wo_ref, *refs
):
    sources, (dq_ref, dk_ref, dv_ref, *refs) = refs[:9], refs[9:]
    targets, (left_ref, right_ref, cross_left, cross_right, sems, *held) = refs[:2], refs[2:]
    held_ref, held_sems = held if chunks else (None, None)
    step, steps = pl.program_id(0), pl.num_programs(0)
    places = [left_ref.at[0], left_ref.at[1]]
    places += [cross_left.at[at] for at in range(3)] + [cross_right.at[at] for at in range(4)]
    copies = [
        pltpu.make_async_copy(source, place, sems.at[at])
        for at, (source, place) in enumerate(zip(sources, places))
    ]
    needs = ((2, 5), (3, 6), (7,), (4, 8))

    @pl.when(step == 0)
    def _():
        for at in sum(needs, ()) + (0, 1):
            copies[at].start()

    rows = pl.ds(pl.multiple_of(step * ROW_LEN, ROW_LEN), ROW_LEN)
    branch = grad_ref[...].astype(LOW)
    grads = attend_back(
        nt(branch, wo_ref[...]).astype(LOW), q_ref[...], k_ref[...], v_ref[...], probs_ref
    )
    for at, (ref, grad) in enumerate(zip((dq_ref, dk_ref, dv_ref), grads)):
        ref[...] = grad
        right_ref[at, rows, :] = grad
    right_ref[3, rows, :] = branch
    length = dq_ref.shape[1] // HEADS
    cross_rows, self_rows = slice(0, length), slice(length, 2 * length)

    def region(part):
        return (slice(None), part)

    for weight in range(4):

        @pl.when(step == weight)
        def _():
            for at in needs[weight]:
                copies[at].wait()
            left = cross_left.at[(0, 1, 1, 2)[weight]]
            weight_product(
                chunks, place_ref, left, cross_right.at[weight], weight, cross_rows.start, targets[0], held_ref
            )
            if chunks:
                hand_out(place_ref, held_ref, targets, held_sems.at[0, weight], weight, region(cross_rows))

    @pl.when(step == steps - 1)
    def _():
        for copy in copies[:2]:
            copy.wait()
        for weight in range(4):
            left = left_ref.at[weight // 3]
            weight_product(
                chunks, place_ref, left, right_ref.at[weight], weight, self_rows.start, targets[1], held_ref
            )
            if chunks:
                hand_out(place_ref, held_ref, targets, held_sems.at[1, weight], weight, region(self_rows))
        if chunks:
            for group, part in enumerate((cross_rows, self_rows)):
                for weight in range(4):
                    hand_out_done(held_ref, targets, held_sems.at[group, weight], region(part))


def encoder_grad_kernel(place_ref, hits_ref, *refs):
    out_ref = refs[-1]
    step = pl.program_id(0)
    for turn in range(4):

        @pl.when(step == turn)
        def _():
            tokens = refs[turn].shape[0]
            rows = tokens // ROW_LEN
            owner = lax.bitwise_xor(place_ref[0], turn)
            for row in range(rows):
                here = slice(ROW_LEN * row, ROW_LEN * (row + 1))
                weight = 0.5 * hits_ref[owner * rows + row]
                out_ref[0, here, :] = weight * refs[turn][here, :].astype(FULL)


def gain_grad(pairs, gain_ref, target):
    total = sum(
        jnp.sum(weight.astype(FULL) * grad.astype(FULL), axis=1, keepdims=True) for weight, grad in pairs
    )
    turned = jnp.broadcast_to(total, (total.shape[0], 128)).T
    target[0] = turned[:1] / gain_ref[0]


def feed_final_kernel(place_ref, *refs):
    sources, (up_ref, gain_ref, up_out, down_out, gain_out, half_ref) = refs[:4], refs[4:]
    length = up_out.shape[0]
    part = down_out.shape[0] // 4
    share = up_out.shape[1] // 4
    width = down_out.shape[1]
    fold = share - width
    for turn, piece in enumerate(sources):
        owner = lax.bitwise_xor(place_ref[0], turn)
        x_of, core = lax.shift_right_logical(owner, 1), lax.bitwise_and(owner, 1)
        start = pl.multiple_of(x_of * share, 128)
        half_ref[core, :, pl.ds(start, width)] = piece[:length, :]
        for at in range(width // fold):
            half_ref[
                core, REST * at : REST * (at + 1), pl.ds(pl.multiple_of(start + width, 128), fold)
            ] = piece[length : length + REST, fold * at : fold * (at + 1)]
        rows = pl.ds(pl.multiple_of((2 * core + x_of) * part, 32), part)
        down_out[rows, :] = piece[length + REST :, :].astype(FULL)
    picks = [pick_matrix(core, True) for core in range(2)]
    for pair in range(up_out.shape[1] // (2 * UNITS)):
        columns = slice(UNITS * pair, UNITS * (pair + 1))
        up_out[:, 2 * UNITS * pair : 2 * UNITS * (pair + 1)] = nn(
            half_ref[0, :, columns], picks[0]
        ) + nn(half_ref[1, :, columns], picks[1])
    gain_grad([(up_ref[...], up_out[...])], gain_ref, gain_out)


def weight_final_kernel(place_ref, *refs):
    sources, weights, gains, targets = refs[:4], refs[4:8], refs[8:10], refs[10:-2]
    cross_ref, self_ref = refs[-2:]
    length = cross_ref.shape[1]
    for turn, piece in enumerate(sources):
        owner = lax.bitwise_xor(place_ref[0], turn)
        cross_ref[owner] = piece[:length, :]
        self_ref[owner] = piece[length:, :]
    order = order_matrix(cross_ref.shape[2], True)
    for at in range(3):
        targets[at][...] = nn(self_ref[at], order)
        targets[4 + at][...] = nn(cross_ref[at], order)
    targets[3][...] = self_ref[3].astype(FULL)
    targets[7][...] = cross_ref[3].astype(FULL)
    gain_grad([(weights[at][...], self_ref[at]) for at in range(3)], gains[0], targets[8])
    gain_grad([(weights[3][...], cross_ref[0])], gains[1], targets[9])


def whole(array):
    return pl.BlockSpec(array.shape, lambda *at: (0,) * array.ndim)


def by_row(array, first=0):
    if array.ndim == 2:
        return pl.BlockSpec((ROW_LEN, array.shape[1]), lambda at, *_: (at + first, 0))
    return pl.BlockSpec(
        (1,) + array.shape[1:], lambda at, *_: (at + first,) + (0,) * (array.ndim - 1)
    )


def run(
    body, name, grid, ins, in_specs, outs, out_specs, flops, scratch=(), prefetch=(), after=(), into=()
):
    after = list(into) + list(after)
    outs = list(outs) + [shape_of((1, 1), FULL)]
    out_specs = list(out_specs) + [pl.BlockSpec(memory_space=pltpu.SMEM)]
    moved = sum(array.size * array.dtype.itemsize for array in list(ins) + list(outs))
    first, last = len(prefetch) + len(ins), len(prefetch) + len(ins) + len(after)

    tick_at = last + len(outs) - 1

    def ordered_body(*refs):
        refs[tick_at][0, 0] = 0.0
        body(*refs[:first], *refs[last:tick_at], *refs[tick_at + 1 :])

    return pl.pallas_call(
        ordered_body,
        name=name,
        out_shape=outs,
        grid_spec=pltpu.PrefetchScalarGridSpec(
            num_scalar_prefetch=len(prefetch),
            grid=grid,
            in_specs=list(in_specs) + [pl.BlockSpec(memory_space=pl.ANY)] * len(after),
            out_specs=out_specs,
            scratch_shapes=scratch,
        ),
        input_output_aliases={first + at: at for at in range(len(into))},
        compiler_params=pltpu.CompilerParams(vmem_limit_bytes=VMEM_BYTES),
        cost_estimate=pl.CostEstimate(
            flops=int(flops * WEIGHT), bytes_accessed=int(moved * WEIGHT), transcendentals=0
        ),
    )(*prefetch, *ins, *after)


def shape_of(shape, dtype=LOW):
    return jax.ShapeDtypeStruct(tuple(shape), dtype)


def row_call(body, name, rowed, fixed, outs, flops, order, after=(), part=None, into=()):
    first, last = part or (0, outs[0].shape[0] // ROW_LEN)
    ins, specs = [], []
    rowed, fixed = list(rowed), list(fixed)
    for kind in order:
        array = rowed.pop(0) if kind == "r" else fixed.pop(0)
        ins.append(array)
        specs.append(by_row(array, first) if kind == "r" else whole(array))
    return run(
        body,
        name,
        (last - first,),
        ins,
        specs,
        outs,
        [by_row(out, first) for out in outs],
        flops,
        after=after,
        into=into,
    )


def permuted(value, axes, sizes, flip):
    count = math.prod(sizes)
    return lax.ppermute(value, axes, [(at, at ^ flip) for at in range(count)])


def added(parts, tick=None):
    total = parts[0].astype(FULL)
    if tick is not None:
        total = total + tick[0, 0]
    for part in parts[1:]:
        total = total + part.astype(FULL)
    return total.astype(LOW)


def on_device(
    layer_size,
    dp_size,
    inputs,
    encoder_out,
    query_self,
    key_self,
    value_self,
    out_self,
    query_cross,
    key_cross,
    value_cross,
    out_cross,
    feed_up,
    feed_down,
    gain_self,
    gain_cross,
    gain_feed,
    seg_target,
    seg_source,
    subnet_of_row,
    chosen_layers,
    out_grad,
):
    tokens, width = inputs.shape
    rows = tokens // ROW_LEN
    layer_at = lax.axis_index("layer")
    dp_at = lax.axis_index("dp")
    place = jnp.stack([layer_at, dp_at]).astype(jnp.int32)
    axes, sizes = ("dp", "layer"), (dp_size, layer_size)

    def across(value, layer_flip, dp_flip=0):
        return permuted(value, axes, sizes, dp_flip * layer_size + layer_flip)

    picked = jnp.sum(
        (chosen_layers[:, :, None] == jnp.arange(layer_size)[None, None, :]).astype(FULL), axis=1
    )
    row_pick = (subnet_of_row[:, None] == jnp.arange(chosen_layers.shape[0])[None, :]).astype(FULL)
    block_hits = jnp.sum(row_pick[:, :, None] * picked[None], axis=1)
    own_layer = encoder_out.reshape(layer_size, rows, ROW_LEN, width)

    def own_block(flip):
        return lax.dynamic_index_in_dim(own_layer, layer_at ^ flip, 0, keepdims=False)

    def hits_of(flip, layer_flip):
        hits = lax.dynamic_slice_in_dim(block_hits, (layer_at ^ flip) * rows, rows, 0)
        hits = lax.dynamic_slice_in_dim(hits, layer_at ^ layer_flip, 1, 1)
        return 0.5 * hits[:, :, None]

    def chip_sum(flip, arrived):
        total = hits_of(flip, 0) * own_block(flip).astype(FULL)
        total = total + hits_of(flip, 1) * arrived.astype(FULL)
        return total.astype(LOW).reshape(tokens, width)

    far_half = across(own_block(3), 1)
    near_half = across(own_block(1), 1)
    far_memory = across(chip_sum(2, far_half), 2)

    weights = [query_self, key_self, value_self, query_cross, key_cross, value_cross, out_self, out_cross, feed_up]
    order_outs = [shape_of(array.shape) for array in weights[:8]]
    order_outs.append(shape_of((width, feed_up.shape[1] // 2)))
    ordered = run(
        order_kernel,
        "order_weights",
        (1,),
        weights,
        [pl.BlockSpec(memory_space=pl.ANY)] * 9,
        order_outs,
        [pl.BlockSpec(memory_space=pl.ANY)] * 9,
        12 * width**3,
        scratch=[
            pltpu.VMEM(shape, LOW)
            for columns in (feed_up.shape[1], feed_up.shape[1] // 2)
            for shape in ((6, width, width), (2, width, width), (width, columns))
        ]
        + [pltpu.SemaphoreType.DMA((9,))] * 2,
        prefetch=(place,),
    )
    wq_self, wk_self, wv_self, wq_cross, wk_cross, wv_cross, wo_self, wo_cross, up_half, _ = ordered
    g_self, g_cross, g_feed = gain_self, gain_cross, gain_feed
    flat = shape_of((tokens, width))
    wide = shape_of((tokens, width), FULL)
    probs = shape_of((rows, HEADS, ROW_LEN, ROW_LEN))
    dense_flops = 2 * tokens * width * width
    head_flops = 2 * tokens * ROW_LEN * ROW_LEN * HEADS

    normed_self, q_self, k_self, v_self, probs_self, attn_self, after_self, normed_cross, q_cross, _ = row_call(
        self_forward_kernel,
        "self_forward",
        (inputs,),
        (seg_target, g_self, g_cross, wq_self, wk_self, wv_self, wo_self, wq_cross),
        [flat, flat, flat, flat, probs, flat, wide, flat, flat],
        5 * dense_flops + 2 * head_flops,
        "rffffffff",
    )
    my_hits = lax.dynamic_slice_in_dim(block_hits, layer_at * rows, rows, 0)
    pair_hits = jnp.stack(
        [lax.dynamic_index_in_dim(my_hits, layer_at ^ flip, 1, keepdims=False) for flip in (0, 1)]
    )
    memory, k_cross, v_cross, probs_cross, attn_cross, after_cross, normed_feed, _ = run(
        cross_forward_kernel,
        "cross_forward",
        (rows,),
        [
            encoder_out, near_half, far_memory, q_cross, after_self, seg_target, seg_source, g_feed,
            wk_cross, wv_cross, wo_cross,
        ],
        [pl.BlockSpec((1, ROW_LEN, width), lambda at, place, hits: (0, place[0] * rows + at, 0))]
        + [by_row(array) for array in (near_half, far_memory, q_cross, after_self)]
        + [whole(array) for array in (seg_target, seg_source, g_feed, wk_cross, wv_cross, wo_cross)],
        [flat, flat, flat, probs, flat, wide, flat],
        [by_row(out) for out in (flat, flat, flat, probs, flat, wide, flat)],
        3 * dense_flops + 2 * head_flops,
        prefetch=(place, pair_hits),
    )

    chunks = dp_size if dp_size == HEADS and layer_size == 4 else 0
    hidden = feed_up.shape[1]
    share = hidden // 4
    anywhere = pl.BlockSpec(memory_space=pl.ANY)
    length = width // HEADS
    if chunks:
        weight_outs = [shape_of((2, chunks, 2 * length, width))] * 2
        weight_specs = [anywhere] * 2
    else:
        weight_outs = [shape_of((4, width, width))] * 2
        weight_specs = [whole(out) for out in weight_outs]

    def held(outs, sems):
        if not chunks:
            return []
        return [pltpu.VMEM((2,) + outs[0].shape, LOW), pltpu.SemaphoreType.DMA(sems)]

    if chunks:
        plane_rows, line_rows = FEED_PLANE_ROWS, length + REST + UNITS // 4 - FEED_PLANE_ROWS
        feed_outs = [shape_of((dp_size // 2, plane_rows, width))] * 4
        feed_outs.append(shape_of((dp_size // 2, 2, 2, line_rows, width)))
        feed_specs = [anywhere] * 5
        feed_held = [
            pltpu.VMEM((2, 2, dp_size // 2, plane_rows + line_rows, width), LOW),
            pltpu.SemaphoreType.DMA((8,)),
        ]
    else:
        feed_outs = [shape_of((width, hidden // 2)), shape_of((hidden // 2, width))]
        feed_specs = [
            pl.BlockSpec((width, share), lambda at, *_: (0, at)),
            pl.BlockSpec((share, width), lambda at, *_: (at, 0)),
        ]
        feed_held = []

    def down_spec(at_chunk):
        return pl.BlockSpec(
            (1, UNITS // 2, width), lambda at, place: (2 * (4 * at + at_chunk) + (place[0] & 1), 0, 0)
        )

    normed_other, grad_other = across(normed_feed, 1), across(out_grad, 1)
    down_halves = feed_down.reshape(hidden // (UNITS // 2), UNITS // 2, width)
    acc, back_feed, acc_send, back_send, *feed_grads, _ = run(
        functools.partial(feed_kernel, chunks),
        "feed",
        (2,),
        [normed_feed, normed_other, out_grad, grad_other, up_half] + [down_halves] * 4 + [after_cross],
        [whole(flat)] * 4
        + [pl.BlockSpec((width, share), lambda at, *_: (0, at))]
        + [down_spec(at_chunk) for at_chunk in range(4)]
        + [anywhere],
        [wide, wide, flat, flat] + feed_outs,
        [anywhere] * 4 + feed_specs,
        12 * tokens * width * hidden,
        scratch=[
            pltpu.VMEM((2, tokens, width), FULL),
            pltpu.VMEM((2, tokens, width), FULL),
            pltpu.VMEM((2, tokens, width), LOW),
            pltpu.VMEM((width, 2 * tokens), LOW),
            pltpu.VMEM((width, 2 * tokens), LOW),
            pltpu.VMEM((2 * tokens, share), LOW),
            pltpu.VMEM((2 * tokens, share), LOW),
            pltpu.SemaphoreType.DMA((5,)),
        ]
        + feed_held,
        prefetch=(place,),
    )
    layer_out = added([acc, across(acc_send, 1)])

    line_groups = [
        [(z_at * 2 + y_at) * layer_size + at for z_at in range(dp_size // 2)]
        for y_at in range(2)
        for at in range(layer_size)
    ]
    z_at = dp_at // 2

    def from_core(grads):
        keep, send = grads
        return [part.reshape((2, 4, 2) + part.shape[2:]) for part in (keep, across(send, 1))]

    def plane_arrived(sends):
        return [across(sent, 2 * x_flip, y_flip) for sent, (x_flip, y_flip) in zip(sends, PLANE)]

    def exchange(operand):
        return lax.all_to_all(operand, axes, 0, 0, axis_index_groups=line_groups, tiled=True)

    class Sum:
        def __init__(self, keeps, sends, operand):
            self.keeps, self.sends, self.operand = keeps, sends, operand
            self.started = sends + [operand]
            self.along_plane, self.along_line = plane_arrived(sends), exchange(operand)

        def turn(self, tick):
            first = self.keeps + self.along_plane
            self.line_parts = [self.along_line[at] for at in range(dp_size // 2)]
            self.operand = added(first, tick)
            self.sends = [added([part[flip] for part in self.line_parts], tick) for flip in PLANE]
            self.started = self.sends + [self.operand]
            self.along_plane, self.along_line = plane_arrived(self.sends), exchange(self.operand)

        def result(self, tick=None):
            first = added([self.along_line[at] for at in range(dp_size // 2)], tick)
            last = added([part[0, 0] for part in self.line_parts] + self.along_plane, tick)
            return jnp.concatenate([first, last], axis=0)

    cross_in, dq_cross, dk_cross, dv_cross, memory_grad, grad_after_self, tick = row_call(
        cross_backward_kernel,
        "cross_backward",
        (back_feed, across(back_send, 1), after_cross, out_grad, after_self, q_cross, k_cross, v_cross, probs_cross),
        (g_feed, g_cross, wq_cross, wk_cross, wv_cross, wo_cross),
        [flat, flat, flat, flat, flat, wide],
        4 * dense_flops + 4 * head_flops,
        "rrrfrrfrrrrffff",
    )
    if chunks:
        feed_sum = Sum(feed_grads[:1], feed_grads[1:4], feed_grads[4])
    moved = [normed_self, attn_self, normed_cross, memory, attn_cross]
    moved += [dq_cross, dk_cross, dv_cross, cross_in]
    dq_self, dk_self, dv_self, *weight_grads, tick = run(
        functools.partial(self_backward_kernel, chunks),
        "self_backward",
        (rows,),
        [grad_after_self, q_self, k_self, v_self, probs_self, wo_self] + moved,
        [by_row(array) for array in (grad_after_self, q_self, k_self, v_self, probs_self)]
        + [whole(wo_self)]
        + [anywhere] * len(moved),
        [flat] * 3 + weight_outs,
        [by_row(flat)] * 3 + weight_specs,
        LIGHT * dense_flops,
        scratch=[
            pltpu.VMEM((2, tokens, width), LOW),
            pltpu.VMEM((4, tokens, width), LOW),
            pltpu.VMEM((3, tokens, width), LOW),
            pltpu.VMEM((4, tokens, width), LOW),
            pltpu.SemaphoreType.DMA((len(moved),)),
        ]
        + held(weight_outs, (2, 4)),
        prefetch=(place,),
        after=[tick],
    )
    from_chip = across(memory_grad, 2)
    waits = []
    if chunks:
        feed_sum.turn(tick)
        waits = feed_sum.started
    input_grad, tick = row_call(
        input_grad_kernel,
        "input_grad",
        (dq_self, dk_self, dv_self, inputs, grad_after_self),
        (wq_self, wk_self, wv_self, g_self),
        [flat],
        30 * dense_flops,
        "rrrfffrfr",
        after=[tick] + waits,
    )
    waits = []
    if chunks:
        parts = from_core(weight_grads)
        first = [part[:, :, :, :WEIGHT_PLANE_ROWS] for part in parts]
        last = [part[:, :, :, WEIGHT_PLANE_ROWS:] for part in parts]
        weight_sends = [added([part[x_to, :, y_to] for part in first], tick) for x_to, y_to in PLANE]
        gain_chunks = [gain.reshape(chunks, 1, length) for gain in (gain_self, gain_cross, gain_feed)]
        waits = weight_sends + feed_sum.along_plane + gain_chunks + [layer_out]

    arrived = [memory_grad, across(memory_grad, 1), from_chip, across(from_chip, 1)]
    own_hits = lax.dynamic_slice_in_dim(block_hits, layer_at, 1, 1)[:, 0]
    encoder_shape = shape_of(encoder_out.shape, FULL)
    encoder_grad, tick = run(
        encoder_grad_kernel,
        "encoder_grad",
        (4,),
        arrived,
        [whole(array) for array in arrived],
        [encoder_shape],
        [pl.BlockSpec((1, tokens, width), lambda at, place, hits: (0, place[0] ^ at, 0))],
        LIGHT * encoder_out.size,
        prefetch=(place, own_hits),
        after=waits,
    )

    if chunks:
        weight_sum = Sum(
            [part[0, :, 0] for part in first],
            weight_sends,
            added([jnp.moveaxis(part, 1, 0) for part in last], tick),
        )

    if chunks:
        weight_sum.turn(tick)

        def gathered(piece):
            from_x = across(piece, 2)
            return [piece, across(piece, 1), from_x, across(from_x, 1)]

        def final_call(body, name, pieces, chunk_weights, gains, outs, scratch):
            ins = pieces + chunk_weights + gains
            outs = outs + [shape_of((1, 1, length), FULL)] * len(gains)
            return run(
                body,
                name,
                (1,),
                ins,
                [whole(array) for array in pieces]
                + [
                    pl.BlockSpec((length, array.shape[1]), lambda at, place: (place[1], 0))
                    for array in chunk_weights
                ]
                + [pl.BlockSpec((1, 1, length), lambda at, place: (place[1], 0, 0))] * len(gains),
                outs,
                [whole(out) for out in outs],
                LIGHT * length * width * width,
                scratch=scratch,
                prefetch=(place,),
                after=list(waits),
            )

        waits = weight_sum.started
        *feed_finals, tick = final_call(
            feed_final_kernel,
            "feed_final",
            gathered(feed_sum.result()),
            [feed_up],
            gain_chunks[2:],
            [shape_of((length, hidden), FULL), shape_of((hidden // chunks, width), FULL)],
            [pltpu.VMEM((2, length, hidden // 2), LOW)],
        )
        waits = []
        *finals, _ = final_call(
            weight_final_kernel,
            "weight_final",
            gathered(weight_sum.result(tick)),
            [wq_self, wk_self, wv_self, wq_cross],
            gain_chunks[:2],
            [shape_of((length, width), FULL)] * 8,
            [pltpu.VMEM((4, length, width), LOW)] * 2,
        )
        weight_grads = finals[:8] + feed_finals[:2]
        gain_grads = [value.reshape(length) for value in finals[8:] + feed_finals[2:]]
    else:
        back_order = order_matrix(width, True)

        def total(grad):
            part = lax.psum_scatter(grad.astype(FULL), "dp", scatter_dimension=0, tiled=True)
            return lax.psum(part.astype(LOW), "layer").astype(FULL)

        def natural(grads):
            back = [nn(grads[at], back_order).astype(LOW) for at in range(3)]
            return [total(grad) for grad in back + [nn(back_order.T, grads[3]).astype(LOW)]]

        grads_cross, grads_self = (natural(grads) for grads in weight_grads)
        core = layer_at % 2
        up_shape, down_shape = (width, -1, 2, UNITS // 2), (-1, 2, UNITS // 2, width)
        up_part = feed_grads[0].reshape(width, -1, 1, UNITS // 2)
        down_part = feed_grads[1].reshape(-1, 1, UNITS // 2, width)
        up_all = jnp.zeros(feed_up.shape, LOW).reshape(up_shape)
        down_all = jnp.zeros(feed_down.shape, LOW).reshape(down_shape)
        up_all = lax.dynamic_update_slice_in_dim(up_all, up_part, core, 2).reshape(feed_up.shape)
        down_all = lax.dynamic_update_slice_in_dim(down_all, down_part, core, 1).reshape(feed_down.shape)
        weight_grads = grads_self + grads_cross + [total(up_all), total(down_all)]
        length = width // dp_size

        def my_rows(array):
            return lax.dynamic_slice_in_dim(array, dp_at * length, length, 0).astype(FULL)

        def gain_total(pairs, gain):
            sums = sum(jnp.sum(my_rows(weight) * grad, axis=1) for weight, grad in pairs)
            return sums / my_rows(gain)

        gain_grads = [
            gain_total(zip((query_self, key_self, value_self), grads_self), gain_self),
            gain_total([(query_cross, grads_cross[0])], gain_cross),
            gain_total([(feed_up, weight_grads[8])], gain_feed),
        ]
    return (layer_out, input_grad, encoder_grad, *weight_grads, *gain_grads)


def solution(mesh):
    in_specs = (
        P(("dp", "layer"), None),
        P("layer", "dp", None),
        *[P()] * 13,
        P(("dp", "layer"), None),
        P(("dp", "layer"), None),
        P("dp"),
        P(),
        P(("dp", "layer"), None),
    )
    out_specs = (
        P(("dp", "layer"), None),
        P(("dp", "layer"), None),
        P("layer", "dp", None),
        *[P("dp", None)] * 10,
        *[P("dp")] * 3,
    )
    body = functools.partial(on_device, mesh.shape["layer"], mesh.shape["dp"])
    return jax.shard_map(
        body, mesh=mesh, in_specs=in_specs, out_specs=out_specs, check_vma=False
    )
```

```python
import functools
import math

import jax
import jax.numpy as jnp
from jax import lax
from jax.experimental import pallas as pl
from jax.experimental.pallas import tpu as pltpu
from jax.sharding import PartitionSpec as P

HEADS = 8
HEAD = 80
MAIN = 64
REST = 16
ROW_LEN = 256
BLOCK = 256
UNITS = 384
SCALE = 1.0 / math.sqrt(HEAD)
LOW = jnp.bfloat16
FULL = jnp.float32
VMEM_BYTES = 56 * 1024 * 1024
WEIGHT = 1.0
LIGHT = 0.05


def dot(left, right, left_dim, right_dim):
    return lax.dot_general(
        left, right, (((left_dim,), (right_dim,)), ((), ())), preferred_element_type=FULL
    )


def nn(left, right):
    return dot(left, right, 1, 0)


def nt(left, right):
    return dot(left, right, 1, 1)


def tn(left, right):
    return dot(left, right, 0, 0)


def norm_parts(value):
    centred = value - jnp.mean(value, axis=-1, keepdims=True)
    inverse = lax.rsqrt(jnp.mean(centred * centred, axis=-1, keepdims=True) + 1e-05)
    return (centred * inverse, inverse)


def norm_forward(value, gain):
    return (norm_parts(value)[0] * gain).astype(LOW)


def norm_backward(grad, value, gain):
    normed, inverse = norm_parts(value)
    scaled = grad * gain
    inner = (
        scaled
        - jnp.mean(scaled, axis=-1, keepdims=True)
        - normed * jnp.mean(scaled * normed, axis=-1, keepdims=True)
    )
    return inner * inverse


def source_column(position):
    rest = position - HEADS * MAIN
    return jnp.where(
        rest < 0,
        HEAD * (position // MAIN) + position % MAIN,
        HEAD * (rest // REST) + MAIN + rest % REST,
    )


def order_matrix(width, transposed):
    rows = lax.broadcasted_iota(jnp.int32, (width, width), 0)
    columns = lax.broadcasted_iota(jnp.int32, (width, width), 1)
    if transposed:
        rows, columns = columns, rows
    return (rows == source_column(columns)).astype(FULL).astype(LOW)


def head_groups(array, head):
    pair = head // 2
    return jnp.concatenate(
        [array[:, 2 * MAIN * pair : 2 * MAIN * (pair + 1)], array[:, HEADS * MAIN :]], axis=1
    )


def head_mask(head):
    lane = lax.broadcasted_iota(jnp.int32, (1, 2 * MAIN + HEADS * REST), 1)
    rest = lane - 2 * MAIN
    owner = jnp.where(rest < 0, 2 * (head // 2) + lane // MAIN, rest // REST)
    return (owner == head).astype(FULL).astype(LOW)


def same_segment(key_seg, query_seg):
    shape = (16, key_seg.shape[1])
    number = lax.broadcasted_iota(jnp.int32, shape, 0)
    key_hot = (number == key_seg).astype(FULL).astype(LOW)
    query_hot = (number == query_seg).astype(FULL).astype(LOW)
    return tn(key_hot, query_hot)


def merge_pairs(parts):
    mains = [part[:, : 2 * MAIN] for part in parts]
    rests = [part[:, 2 * MAIN :] for part in parts]
    while len(rests) > 1:
        rests = [rests[i] + rests[i + 1] for i in range(0, len(rests), 2)]
    return jnp.concatenate(mains + rests, axis=1)


def attend(queries, keys, values, bias, probs_ref):
    parts = []
    for pair in range(HEADS // 2):
        pair_probs, pair_values = [], []
        for head in (2 * pair, 2 * pair + 1):
            mask = head_mask(head)
            scores = nt(head_groups(keys, head), head_groups(queries, head) * mask) * SCALE + bias
            raised = jnp.exp(scores - jnp.max(scores, axis=0, keepdims=True))
            probs = (raised * (1.0 / jnp.sum(raised, axis=0, keepdims=True))).astype(LOW)
            probs_ref[0, head] = probs
            pair_probs.append(probs)
            pair_values.append(head_groups(values, head) * mask)
        parts.append(
            tn(jnp.concatenate(pair_probs, axis=0), jnp.concatenate(pair_values, axis=0))
        )
    return merge_pairs(parts).astype(LOW)


def attend_back(grad, queries, keys, values, probs_ref):
    query_parts, key_parts, value_parts = [], [], []
    for pair in range(HEADS // 2):
        pair_probs, pair_slopes, pair_grads, pair_queries, pair_keys = [], [], [], [], []
        for head in (2 * pair, 2 * pair + 1):
            mask = head_mask(head)
            grad_head = head_groups(grad, head) * mask
            probs = probs_ref[0, head]
            wide = probs.astype(FULL)
            prob_grad = nt(head_groups(values, head), grad_head)
            delta = jnp.sum(prob_grad * wide, axis=0, keepdims=True)
            pair_probs.append(probs)
            pair_slopes.append((wide * (prob_grad - delta)).astype(LOW))
            pair_grads.append(grad_head)
            pair_queries.append(head_groups(queries, head) * mask)
            pair_keys.append(head_groups(keys, head) * mask)
        query_parts.append(
            tn(jnp.concatenate(pair_slopes, axis=0), jnp.concatenate(pair_keys, axis=0))
        )
        key_parts.append(
            nn(jnp.concatenate(pair_slopes, axis=1), jnp.concatenate(pair_queries, axis=0))
        )
        value_parts.append(
            nn(jnp.concatenate(pair_probs, axis=1), jnp.concatenate(pair_grads, axis=0))
        )
    return (
        (merge_pairs(query_parts) * SCALE).astype(LOW),
        (merge_pairs(key_parts) * SCALE).astype(LOW),
        merge_pairs(value_parts).astype(LOW),
    )


PLANE = ((1, 1), (1, 0), (0, 1))


def pick_matrix(core, transposed):
    shape = (2 * UNITS, UNITS)
    if transposed:
        shape = shape[::-1]
    unit = lax.broadcasted_iota(jnp.int32, shape, int(transposed))
    taken = lax.broadcasted_iota(jnp.int32, shape, 1 - int(transposed))
    half = UNITS // 2
    source = UNITS * (taken // half) + half * core + taken % half
    return (unit == source).astype(FULL).astype(LOW)


def order_kernel(place_ref, *refs):
    sources, targets, refs = refs[:9], refs[9:18], refs[18:]
    froms, tos, refs = (*refs[:2], refs[2]), (*refs[3:5], refs[5]), refs[6:]
    in_sems, out_sems = refs
    columns_in, rows_in, up_in = froms
    columns_out, rows_out, up_out = tos
    ins = [columns_in.at[at] for at in range(6)] + [rows_in.at[at] for at in range(2)] + [up_in]
    outs = [columns_out.at[at] for at in range(6)] + [rows_out.at[at] for at in range(2)] + [up_out]
    fetches = [pltpu.make_async_copy(*pair, in_sems.at[at]) for at, pair in enumerate(zip(sources, ins))]
    stores = [pltpu.make_async_copy(*pair, out_sems.at[at]) for at, pair in enumerate(zip(outs, targets))]
    for fetch in fetches:
        fetch.start()
    order = order_matrix(columns_in.shape[1], False)
    for at in range(6):
        fetches[at].wait()
        columns_out[at] = nn(columns_in[at], order).astype(LOW)
        stores[at].start()
    for at in range(2):
        fetches[6 + at].wait()
        for head in range(HEADS):
            base = HEAD * head
            rows_out[at, MAIN * head : MAIN * (head + 1)] = rows_in[at, base : base + MAIN]
            rest = HEADS * MAIN + REST * head
            rows_out[at, rest : rest + REST] = rows_in[at, base + MAIN : base + HEAD]
        stores[6 + at].start()
    pick = pick_matrix(lax.bitwise_and(place_ref[0], 1), False)
    fetches[8].wait()
    for pair in range(up_in.shape[1] // (2 * UNITS)):
        columns = slice(2 * UNITS * pair, 2 * UNITS * (pair + 1))
        up_out[:, UNITS * pair : UNITS * (pair + 1)] = nn(up_in[:, columns], pick).astype(LOW)
    stores[8].start()
    for store in stores:
        store.wait()


def self_forward_kernel(
    x_ref, seg_ref, gain_ref, next_gain_ref, wq_ref, wk_ref, wv_ref, wo_ref, next_wq_ref,
    normed_ref, q_ref, k_ref, v_ref, probs_ref, attn_ref, after_ref, next_normed_ref, next_q_ref,
):
    value = x_ref[...].astype(FULL)
    normed = norm_forward(value, gain_ref[...])
    normed_ref[...] = normed
    queries = nn(normed, wq_ref[...]).astype(LOW)
    keys = nn(normed, wk_ref[...]).astype(LOW)
    values = nn(normed, wv_ref[...]).astype(LOW)
    q_ref[...], k_ref[...], v_ref[...] = queries, keys, values
    seg = seg_ref[pl.ds(pl.program_id(0), 1), :]
    key_at = lax.broadcasted_iota(jnp.int32, (ROW_LEN, ROW_LEN), 0)
    query_at = lax.broadcasted_iota(jnp.int32, (ROW_LEN, ROW_LEN), 1)
    allowed = (same_segment(seg, seg) > 0.5) & (key_at <= query_at)
    attn = attend(queries, keys, values, jnp.where(allowed, 0.0, -1e9), probs_ref)
    attn_ref[...] = attn
    after = value + nn(attn, wo_ref[...])
    after_ref[...] = after
    next_normed = norm_forward(after, next_gain_ref[...])
    next_normed_ref[...] = next_normed
    next_q_ref[...] = nn(next_normed, next_wq_ref[...]).astype(LOW)


def cross_forward_kernel(
    place_ref, hits_ref, own_ref, near_ref, far_ref, q_ref, after_ref, seg_target_ref, seg_source_ref, gain_ref,
    wk_ref, wv_ref, wo_ref, memory_ref, k_ref, v_ref, probs_ref, attn_ref, next_after_ref, next_normed_ref,
):
    step = pl.program_id(0)
    own = 0.5 * hits_ref[0, step] * own_ref[0].astype(FULL)
    near = 0.5 * hits_ref[1, step] * near_ref[0].astype(FULL)
    memory = (own + near + far_ref[...].astype(FULL)).astype(LOW)
    memory_ref[...] = memory
    keys = nn(memory, wk_ref[...]).astype(LOW)
    values = nn(memory, wv_ref[...]).astype(LOW)
    k_ref[...], v_ref[...] = keys, values
    row = pl.ds(pl.program_id(0), 1)
    allowed = same_segment(seg_source_ref[row, :], seg_target_ref[row, :]) > 0.5
    attn = attend(q_ref[...], keys, values, jnp.where(allowed, 0.0, -1e9), probs_ref)
    attn_ref[...] = attn
    after = after_ref[...] + nn(attn, wo_ref[...])
    next_after_ref[...] = after
    next_normed_ref[...] = norm_forward(after, gain_ref[...])


def store_piece(place_ref, held_ref, quarter, chunk, rows, columns, piece):
    owner = lax.bitwise_xor(place_ref[0], quarter)
    dp_at = lax.bitwise_xor(chunk, lax.bitwise_and(place_ref[1], 1))
    held_ref[
        lax.bitwise_and(owner, 1), lax.shift_right_logical(owner, 1), dp_at, rows, columns
    ] = piece


def store_feed(place_ref, held_ref, x_of, chunk, rows, columns, piece):
    x_at = lax.bitwise_xor(x_of, lax.shift_right_logical(place_ref[0], 1))
    y_at = lax.bitwise_xor(lax.bitwise_and(chunk, 1), lax.bitwise_and(place_ref[1], 1))
    held_ref[x_at, y_at, lax.shift_right_logical(chunk, 1), rows, columns] = piece


def hand_out(place_ref, held_ref, targets, sem, quarter, region):
    owner = lax.bitwise_xor(place_ref[0], quarter)
    x_at = lax.shift_right_logical(owner, 1)
    for half in range(2):

        @pl.when(lax.bitwise_and(owner, 1) == half)
        def _():
            pltpu.make_async_copy(
                held_ref.at[(half, x_at) + region], targets[half].at[(x_at,) + region], sem
            ).start()


def hand_out_done(held_ref, targets, sem, region):
    pltpu.make_async_copy(held_ref.at[(0, 0) + region], targets[0].at[(0,) + region], sem).wait()


def feed_kernel(chunks, place_ref, *refs):
    normed_refs, grad_refs, up_ref, down_refs, after_ref, refs = refs[:2], refs[2:4], refs[4], refs[5:9], refs[9], refs[10:]
    own_refs, send_refs, refs = refs[:2], refs[2:4], refs[4:]
    targets, refs = refs[:2], refs[2:]
    acc_ref, total_ref, low_ref, hidden_ref, pre_ref, sems, *held = refs
    step, steps = pl.program_id(0), pl.num_programs(0)
    tokens, width = normed_refs[0].shape
    share = up_ref.shape[1]
    fetch = pltpu.make_async_copy(after_ref, acc_ref.at[0], sems.at[0])
    copies = [
        pltpu.make_async_copy(source, target, sems.at[1 + at])
        for at, (source, target) in enumerate(
            zip((low_ref.at[0], total_ref.at[0], low_ref.at[1], acc_ref.at[0]), (send_refs[1], own_refs[1], send_refs[0], own_refs[0]))
        )
    ]

    @pl.when(step == 0)
    def _():
        fetch.start()
        acc_ref[1] = jnp.zeros_like(acc_ref[1])
        total_ref[...] = jnp.zeros_like(total_ref)
        fetch.wait()

    down = jnp.concatenate([ref[0] for ref in down_refs], axis=0)
    for side in (1, 0):
        for start in range(0, tokens, 4 * BLOCK):
            rows = slice(start, start + 4 * BLOCK)
            both = slice(side * tokens + start, side * tokens + start + 4 * BLOCK)
            pre = nn(normed_refs[side][rows, :], up_ref[...])
            hidden_grad = nt(grad_refs[side][rows, :], down)
            square = pre * pre
            slope = math.sqrt(2.0 / math.pi)
            bend = jnp.tanh(pre * (slope + slope * 0.044715 * square))
            half = 0.5 + 0.5 * bend
            hidden = (pre * half).astype(LOW)
            rate = half + pre * half * (1.0 - bend) * (slope + slope * 3 * 0.044715 * square)
            pre_grad = (hidden_grad * rate).astype(LOW)
            hidden_ref[both, :] = hidden
            pre_ref[both, :] = pre_grad
            acc_ref[side, rows, :] += nn(hidden, down)
            total_ref[side, rows, :] += nt(pre_grad, up_ref[...])

    @pl.when(step == steps - 1)
    def _():
        low_ref[0] = total_ref[1].astype(LOW)
        low_ref[1] = acc_ref[1].astype(LOW)
        for copy in copies:
            copy.start()

    def up_grad_of(columns):
        return sum(
            tn(normed_refs[side][...], pre_ref[side * tokens : (side + 1) * tokens, columns]) for side in range(2)
        ).astype(LOW)

    def down_grad_of(columns):
        return sum(
            tn(hidden_ref[side * tokens : (side + 1) * tokens, columns], grad_refs[side][...]) for side in range(2)
        ).astype(LOW)

    if not chunks:
        targets[0][...] = up_grad_of(slice(None))
        targets[1][...] = down_grad_of(slice(None))
    else:
        held_ref, held_sems = held
        length = width // chunks
        part = UNITS // 4
        fold = share - width
        top = length + REST
        for start in range(0, share, BLOCK):
            columns = slice(start, start + BLOCK)
            up_grad = up_grad_of(columns)
            for chunk in range(chunks):
                piece = up_grad[length * chunk : length * (chunk + 1)]
                inside = min(width - start, BLOCK)
                store_feed(
                    place_ref, held_ref, step, chunk,
                    slice(0, length), slice(start, start + inside), piece[:, :inside],
                )
                if inside < BLOCK:
                    for at in range(width // fold):
                        rows = REST * at
                        store_feed(
                            place_ref, held_ref, step, chunk,
                            slice(length, top), slice(fold * at, fold * (at + 1)),
                            piece[rows : rows + REST, inside:],
                        )
            down_grad = down_grad_of(columns)
            for row in range(start, start + BLOCK, 32):
                chunk, inside = 4 * step + row // (2 * part), row % (2 * part)
                base = top + inside % part
                store_feed(
                    place_ref, held_ref, inside // part, chunk,
                    slice(base, base + 32), slice(0, width), down_grad[row - start : row - start + 32],
                )

    @pl.when(step == steps - 1)
    def _():
        if chunks:
            outs = [
                pltpu.make_async_copy(held_ref.at[:, y_at], targets[y_at], held_sems.at[y_at]) for y_at in (1, 0)
            ]
            for copy in outs:
                copy.start()
            for copy in outs:
                copy.wait()
        for copy in copies:
            copy.wait()


def cross_backward_kernel(
    back_ref, back_other_ref, after_cross_ref, gain_feed_ref, grad_ref, after_self_ref, gain_cross_ref,
    q_ref, k_ref, v_ref, probs_ref, wq_ref, wk_ref, wv_ref, wo_ref,
    in_ref, dq_ref, dk_ref, dv_ref, memory_ref, grad_self_ref,
):
    grad = grad_ref[...].astype(FULL) + norm_backward(
        back_ref[...] + back_other_ref[...].astype(FULL), after_cross_ref[...], gain_feed_ref[...]
    )
    branch = grad.astype(LOW)
    in_ref[...] = branch
    query_grad, key_grad, value_grad = attend_back(
        nt(branch, wo_ref[...]).astype(LOW), q_ref[...], k_ref[...], v_ref[...], probs_ref
    )
    dq_ref[...], dk_ref[...], dv_ref[...] = query_grad, key_grad, value_grad
    memory_ref[...] = (nt(key_grad, wk_ref[...]) + nt(value_grad, wv_ref[...])).astype(LOW)
    grad_self_ref[...] = grad + norm_backward(
        nt(query_grad, wq_ref[...]), after_self_ref[...], gain_cross_ref[...]
    )


def input_grad_kernel(dq_ref, dk_ref, dv_ref, wq_ref, wk_ref, wv_ref, x_ref, gain_ref, grad_ref, out_ref):
    inner = (
        nt(dq_ref[...], wq_ref[...]) + nt(dk_ref[...], wk_ref[...]) + nt(dv_ref[...], wv_ref[...])
    )
    back = norm_backward(inner, x_ref[...].astype(FULL), gain_ref[...])
    out_ref[...] = (grad_ref[...] + back).astype(LOW)


def weight_product(chunks, place_ref, left, right, weight, base, target, held_ref):
    width = right.shape[1]
    for start in range(0, width, BLOCK):
        columns = slice(start, min(start + BLOCK, width))
        grad = tn(left[...], right[:, columns]).astype(LOW)
        if not chunks:
            target[weight, :, columns] = grad
            continue
        length = width // chunks
        for chunk in range(chunks):
            piece = grad[length * chunk : length * (chunk + 1)]
            if weight == 3:
                rest = HEADS * MAIN + REST * chunk
                piece = jnp.concatenate(
                    [grad[MAIN * chunk : MAIN * (chunk + 1)], grad[rest : rest + REST]], axis=0
                )
            store_piece(place_ref, held_ref, weight, chunk, slice(base, base + length), columns, piece)


def self_backward_kernel(
    chunks, place_ref, grad_ref, q_ref, k_ref, v_ref, probs_ref, wo_ref, *refs
):
    sources, (dq_ref, dk_ref, dv_ref, *refs) = refs[:9], refs[9:]
    targets, (left_ref, right_ref, cross_left, cross_right, sems, *held) = refs[:2], refs[2:]
    held_ref, held_sems = held if chunks else (None, None)
    step, steps = pl.program_id(0), pl.num_programs(0)
    places = [left_ref.at[0], left_ref.at[1]]
    places += [cross_left.at[at] for at in range(3)] + [cross_right.at[at] for at in range(4)]
    copies = [
        pltpu.make_async_copy(source, place, sems.at[at])
        for at, (source, place) in enumerate(zip(sources, places))
    ]
    needs = ((2, 5), (3, 6), (7,), (4, 8))

    @pl.when(step == 0)
    def _():
        for at in sum(needs, ()) + (0, 1):
            copies[at].start()

    rows = pl.ds(pl.multiple_of(step * ROW_LEN, ROW_LEN), ROW_LEN)
    branch = grad_ref[...].astype(LOW)
    grads = attend_back(
        nt(branch, wo_ref[...]).astype(LOW), q_ref[...], k_ref[...], v_ref[...], probs_ref
    )
    for at, (ref, grad) in enumerate(zip((dq_ref, dk_ref, dv_ref), grads)):
        ref[...] = grad
        right_ref[at, rows, :] = grad
    right_ref[3, rows, :] = branch
    length = dq_ref.shape[1] // HEADS
    cross_rows, self_rows = slice(0, length), slice(length, 2 * length)

    def region(part):
        return (slice(None), part)

    for weight in range(4):

        @pl.when(step == weight)
        def _():
            for at in needs[weight]:
                copies[at].wait()
            left = cross_left.at[(0, 1, 1, 2)[weight]]
            weight_product(
                chunks, place_ref, left, cross_right.at[weight], weight, cross_rows.start, targets[0], held_ref
            )
            if chunks:
                hand_out(place_ref, held_ref, targets, held_sems.at[0, weight], weight, region(cross_rows))

    @pl.when(step == steps - 1)
    def _():
        for copy in copies[:2]:
            copy.wait()
        for weight in range(4):
            left = left_ref.at[weight // 3]
            weight_product(
                chunks, place_ref, left, right_ref.at[weight], weight, self_rows.start, targets[1], held_ref
            )
            if chunks:
                hand_out(place_ref, held_ref, targets, held_sems.at[1, weight], weight, region(self_rows))
        if chunks:
            for group, part in enumerate((cross_rows, self_rows)):
                for weight in range(4):
                    hand_out_done(held_ref, targets, held_sems.at[group, weight], region(part))


def encoder_grad_kernel(place_ref, hits_ref, *refs):
    out_ref = refs[-1]
    step = pl.program_id(0)
    for turn in range(4):

        @pl.when(step == turn)
        def _():
            tokens = refs[turn].shape[0]
            rows = tokens // ROW_LEN
            owner = lax.bitwise_xor(place_ref[0], turn)
            for row in range(rows):
                here = slice(ROW_LEN * row, ROW_LEN * (row + 1))
                weight = 0.5 * hits_ref[owner * rows + row]
                out_ref[0, here, :] = weight * refs[turn][here, :].astype(FULL)


def gain_grad(place_ref, pairs, gain_ref, target):
    total = sum(
        jnp.sum(weight.astype(FULL) * grad.astype(FULL), axis=1, keepdims=True) for weight, grad in pairs
    )
    length = total.shape[0]
    width = gain_ref.shape[0]
    turned = jnp.broadcast_to(total, (length, 128)).T
    gains = jnp.broadcast_to(gain_ref[...].reshape(1, width), (8, width))
    mine = pltpu.roll(gains, lax.rem(width - length * place_ref[1], width), 1)
    target[0] = turned[:1] / mine[:1, :length]


def feed_final_kernel(place_ref, *refs):
    sources, (up_ref, gain_ref, up_out, down_out, gain_out, half_ref) = refs[:4], refs[4:]
    length = up_out.shape[0]
    part = down_out.shape[0] // 4
    share = up_out.shape[1] // 4
    width = down_out.shape[1]
    fold = share - width
    for turn, piece in enumerate(sources):
        owner = lax.bitwise_xor(place_ref[0], turn)
        x_of, core = lax.shift_right_logical(owner, 1), lax.bitwise_and(owner, 1)
        start = pl.multiple_of(x_of * share, 128)
        half_ref[core, :, pl.ds(start, width)] = piece[:length, :]
        for at in range(width // fold):
            half_ref[
                core, REST * at : REST * (at + 1), pl.ds(pl.multiple_of(start + width, 128), fold)
            ] = piece[length : length + REST, fold * at : fold * (at + 1)]
        rows = pl.ds(pl.multiple_of((2 * core + x_of) * part, 32), part)
        down_out[rows, :] = piece[length + REST :, :].astype(FULL)
    picks = [pick_matrix(core, True) for core in range(2)]
    for pair in range(up_out.shape[1] // (2 * UNITS)):
        columns = slice(UNITS * pair, UNITS * (pair + 1))
        up_out[:, 2 * UNITS * pair : 2 * UNITS * (pair + 1)] = nn(
            half_ref[0, :, columns], picks[0]
        ) + nn(half_ref[1, :, columns], picks[1])
    gain_grad(place_ref, [(up_ref[...], up_out[...])], gain_ref, gain_out)


def weight_final_kernel(place_ref, *refs):
    sources, weights, gains, targets = refs[:4], refs[4:8], refs[8:10], refs[10:-2]
    cross_ref, self_ref = refs[-2:]
    length = cross_ref.shape[1]
    for turn, piece in enumerate(sources):
        owner = lax.bitwise_xor(place_ref[0], turn)
        cross_ref[owner] = piece[:length, :]
        self_ref[owner] = piece[length:, :]
    order = order_matrix(cross_ref.shape[2], True)
    for at in range(3):
        targets[at][...] = nn(self_ref[at], order)
        targets[4 + at][...] = nn(cross_ref[at], order)
    targets[3][...] = self_ref[3].astype(FULL)
    targets[7][...] = cross_ref[3].astype(FULL)
    gain_grad(place_ref, [(weights[at][...], self_ref[at]) for at in range(3)], gains[0], targets[8])
    gain_grad(place_ref, [(weights[3][...], cross_ref[0])], gains[1], targets[9])


def whole(array):
    return pl.BlockSpec(array.shape, lambda *at: (0,) * array.ndim)


def by_row(array, first=0):
    if array.ndim == 2:
        return pl.BlockSpec((ROW_LEN, array.shape[1]), lambda at, *_: (at + first, 0))
    return pl.BlockSpec(
        (1,) + array.shape[1:], lambda at, *_: (at + first,) + (0,) * (array.ndim - 1)
    )


def run(
    body, name, grid, ins, in_specs, outs, out_specs, flops, scratch=(), prefetch=(), after=(), into=()
):
    after = list(into) + list(after)
    outs = list(outs) + [shape_of((1, 1), FULL)]
    out_specs = list(out_specs) + [pl.BlockSpec(memory_space=pltpu.SMEM)]
    moved = sum(array.size * array.dtype.itemsize for array in list(ins) + list(outs))
    first, last = len(prefetch) + len(ins), len(prefetch) + len(ins) + len(after)

    tick_at = last + len(outs) - 1

    def ordered_body(*refs):
        refs[tick_at][0, 0] = 0.0
        body(*refs[:first], *refs[last:tick_at], *refs[tick_at + 1 :])

    return pl.pallas_call(
        ordered_body,
        name=name,
        out_shape=outs,
        grid_spec=pltpu.PrefetchScalarGridSpec(
            num_scalar_prefetch=len(prefetch),
            grid=grid,
            in_specs=list(in_specs) + [pl.BlockSpec(memory_space=pl.ANY)] * len(after),
            out_specs=out_specs,
            scratch_shapes=scratch,
        ),
        input_output_aliases={first + at: at for at in range(len(into))},
        compiler_params=pltpu.CompilerParams(vmem_limit_bytes=VMEM_BYTES),
        cost_estimate=pl.CostEstimate(
            flops=int(flops * WEIGHT), bytes_accessed=int(moved * WEIGHT), transcendentals=0
        ),
    )(*prefetch, *ins, *after)


def pause(flops, after):
    return run(lambda: None, "pause", (1,), [], [], [], [], flops, after=after)[0]


def shape_of(shape, dtype=LOW):
    return jax.ShapeDtypeStruct(tuple(shape), dtype)


def row_call(body, name, rowed, fixed, outs, flops, order, after=(), part=None, into=()):
    first, last = part or (0, outs[0].shape[0] // ROW_LEN)
    ins, specs = [], []
    rowed, fixed = list(rowed), list(fixed)
    for kind in order:
        array = rowed.pop(0) if kind == "r" else fixed.pop(0)
        ins.append(array)
        specs.append(by_row(array, first) if kind == "r" else whole(array))
    return run(
        body,
        name,
        (last - first,),
        ins,
        specs,
        outs,
        [by_row(out, first) for out in outs],
        flops,
        after=after,
        into=into,
    )


def permuted(value, axes, sizes, flip):
    count = math.prod(sizes)
    return lax.ppermute(value, axes, [(at, at ^ flip) for at in range(count)])


def added(parts, tick=None):
    total = parts[0].astype(FULL)
    if tick is not None:
        total = total + tick[0, 0]
    for part in parts[1:]:
        total = total + part.astype(FULL)
    return total.astype(LOW)


def on_device(
    layer_size,
    dp_size,
    inputs,
    encoder_out,
    query_self,
    key_self,
    value_self,
    out_self,
    query_cross,
    key_cross,
    value_cross,
    out_cross,
    feed_up,
    feed_down,
    gain_self,
    gain_cross,
    gain_feed,
    seg_target,
    seg_source,
    subnet_of_row,
    chosen_layers,
    out_grad,
):
    tokens, width = inputs.shape
    rows = tokens // ROW_LEN
    layer_at = lax.axis_index("layer")
    dp_at = lax.axis_index("dp")
    place = jnp.stack([layer_at, dp_at]).astype(jnp.int32)
    axes, sizes = ("dp", "layer"), (dp_size, layer_size)

    def across(value, layer_flip, dp_flip=0):
        return permuted(value, axes, sizes, dp_flip * layer_size + layer_flip)

    picked = jnp.sum(
        (chosen_layers[:, :, None] == jnp.arange(layer_size)[None, None, :]).astype(FULL), axis=1
    )
    row_pick = (subnet_of_row[:, None] == jnp.arange(chosen_layers.shape[0])[None, :]).astype(FULL)
    block_hits = jnp.sum(row_pick[:, :, None] * picked[None], axis=1)
    own_layer = encoder_out.reshape(layer_size, rows, ROW_LEN, width)

    def own_block(flip):
        return lax.dynamic_index_in_dim(own_layer, layer_at ^ flip, 0, keepdims=False)

    def hits_of(flip, layer_flip):
        hits = lax.dynamic_slice_in_dim(block_hits, (layer_at ^ flip) * rows, rows, 0)
        hits = lax.dynamic_slice_in_dim(hits, layer_at ^ layer_flip, 1, 1)
        return 0.5 * hits[:, :, None]

    def chip_sum(flip, arrived):
        total = hits_of(flip, 0) * own_block(flip).astype(FULL)
        total = total + hits_of(flip, 1) * arrived.astype(FULL)
        return total.astype(LOW).reshape(tokens, width)

    far_half = across(own_block(3), 1)
    near_half = across(own_block(1), 1)
    far_memory = across(chip_sum(2, far_half), 2)

    weights = [query_self, key_self, value_self, query_cross, key_cross, value_cross, out_self, out_cross, feed_up]
    order_outs = [shape_of(array.shape) for array in weights[:8]]
    order_outs.append(shape_of((width, feed_up.shape[1] // 2)))
    ordered = run(
        order_kernel,
        "order_weights",
        (1,),
        weights,
        [pl.BlockSpec(memory_space=pl.ANY)] * 9,
        order_outs,
        [pl.BlockSpec(memory_space=pl.ANY)] * 9,
        12 * width**3,
        scratch=[
            pltpu.VMEM(shape, LOW)
            for columns in (feed_up.shape[1], feed_up.shape[1] // 2)
            for shape in ((6, width, width), (2, width, width), (width, columns))
        ]
        + [pltpu.SemaphoreType.DMA((9,))] * 2,
        prefetch=(place,),
    )
    wq_self, wk_self, wv_self, wq_cross, wk_cross, wv_cross, wo_self, wo_cross, up_half, _ = ordered
    g_self, g_cross, g_feed = gain_self, gain_cross, gain_feed
    flat = shape_of((tokens, width))
    wide = shape_of((tokens, width), FULL)
    probs = shape_of((rows, HEADS, ROW_LEN, ROW_LEN))
    dense_flops = 2 * tokens * width * width
    head_flops = 2 * tokens * ROW_LEN * ROW_LEN * HEADS

    normed_self, q_self, k_self, v_self, probs_self, attn_self, after_self, normed_cross, q_cross, _ = row_call(
        self_forward_kernel,
        "self_forward",
        (inputs,),
        (seg_target, g_self, g_cross, wq_self, wk_self, wv_self, wo_self, wq_cross),
        [flat, flat, flat, flat, probs, flat, wide, flat, flat],
        5 * dense_flops + 2 * head_flops,
        "rffffffff",
    )
    my_hits = lax.dynamic_slice_in_dim(block_hits, layer_at * rows, rows, 0)
    pair_hits = jnp.stack(
        [lax.dynamic_index_in_dim(my_hits, layer_at ^ flip, 1, keepdims=False) for flip in (0, 1)]
    )
    memory, k_cross, v_cross, probs_cross, attn_cross, after_cross, normed_feed, _ = run(
        cross_forward_kernel,
        "cross_forward",
        (rows,),
        [
            encoder_out, near_half, far_memory, q_cross, after_self, seg_target, seg_source, g_feed,
            wk_cross, wv_cross, wo_cross,
        ],
        [pl.BlockSpec((1, ROW_LEN, width), lambda at, place, hits: (0, place[0] * rows + at, 0))]
        + [by_row(array) for array in (near_half, far_memory, q_cross, after_self)]
        + [whole(array) for array in (seg_target, seg_source, g_feed, wk_cross, wv_cross, wo_cross)],
        [flat, flat, flat, probs, flat, wide, flat],
        [by_row(out) for out in (flat, flat, flat, probs, flat, wide, flat)],
        3 * dense_flops + 2 * head_flops,
        prefetch=(place, pair_hits),
    )

    chunks = dp_size if dp_size == HEADS and layer_size == 4 else 0
    hidden = feed_up.shape[1]
    share = hidden // 4
    anywhere = pl.BlockSpec(memory_space=pl.ANY)
    length = width // HEADS
    if chunks:
        weight_outs = [shape_of((2, chunks, 2 * length, width))] * 2
        weight_specs = [anywhere] * 2
    else:
        weight_outs = [shape_of((4, width, width))] * 2
        weight_specs = [whole(out) for out in weight_outs]

    def held(outs, sems):
        if not chunks:
            return []
        return [pltpu.VMEM((2,) + outs[0].shape, LOW), pltpu.SemaphoreType.DMA(sems)]

    if chunks:
        piece_rows = length + REST + UNITS // 4
        feed_outs = [shape_of((2, dp_size // 2, piece_rows, width))] * 2
        feed_specs = [anywhere] * 2
        feed_held = [
            pltpu.VMEM((2, 2, dp_size // 2, piece_rows, width), LOW),
            pltpu.SemaphoreType.DMA((2,)),
        ]
    else:
        feed_outs = [shape_of((width, hidden // 2)), shape_of((hidden // 2, width))]
        feed_specs = [
            pl.BlockSpec((width, share), lambda at, *_: (0, at)),
            pl.BlockSpec((share, width), lambda at, *_: (at, 0)),
        ]
        feed_held = []

    def down_spec(at_chunk):
        return pl.BlockSpec(
            (1, UNITS // 2, width), lambda at, place: (2 * (4 * at + at_chunk) + (place[0] & 1), 0, 0)
        )

    normed_other, grad_other = across(normed_feed, 1), across(out_grad, 1)
    down_halves = feed_down.reshape(hidden // (UNITS // 2), UNITS // 2, width)
    acc, back_feed, acc_send, back_send, *feed_grads, _ = run(
        functools.partial(feed_kernel, chunks),
        "feed",
        (2,),
        [normed_feed, normed_other, out_grad, grad_other, up_half] + [down_halves] * 4 + [after_cross],
        [whole(flat)] * 4
        + [pl.BlockSpec((width, share), lambda at, *_: (0, at))]
        + [down_spec(at_chunk) for at_chunk in range(4)]
        + [anywhere],
        [wide, wide, flat, flat] + feed_outs,
        [anywhere] * 4 + feed_specs,
        12 * tokens * width * hidden,
        scratch=[
            pltpu.VMEM((2, tokens, width), FULL),
            pltpu.VMEM((2, tokens, width), FULL),
            pltpu.VMEM((2, tokens, width), LOW),
            pltpu.VMEM((2 * tokens, share), LOW),
            pltpu.VMEM((2 * tokens, share), LOW),
            pltpu.SemaphoreType.DMA((5,)),
        ]
        + feed_held,
        prefetch=(place,),
    )
    layer_out = added([acc, across(acc_send, 1)])

    line_groups = [
        [(z_at * 2 + y_at) * layer_size + at for z_at in range(dp_size // 2)]
        for y_at in range(2)
        for at in range(layer_size)
    ]
    z_at = dp_at // 2

    def from_core(grads):
        keep, send = grads
        return [part.reshape((2, 4, 2) + part.shape[2:]) for part in (keep, across(send, 1))]

    def plane_arrived(sends):
        return [across(sent, 2 * x_flip, y_flip) for sent, (x_flip, y_flip) in zip(sends, PLANE)]

    def exchange(operand):
        return lax.all_to_all(operand, axes, 0, 0, axis_index_groups=line_groups, tiled=True)

    cross_in, dq_cross, dk_cross, dv_cross, memory_grad, grad_after_self, tick = row_call(
        cross_backward_kernel,
        "cross_backward",
        (back_feed, across(back_send, 1), after_cross, out_grad, after_self, q_cross, k_cross, v_cross, probs_cross),
        (g_feed, g_cross, wq_cross, wk_cross, wv_cross, wo_cross),
        [flat, flat, flat, flat, flat, wide],
        4 * dense_flops + 4 * head_flops,
        "rrrfrrfrrrrffff",
    )
    if chunks:
        feed_parts = [feed_grads[0], across(feed_grads[1], 0, 1)]
    moved = [normed_self, attn_self, normed_cross, memory, attn_cross]
    moved += [dq_cross, dk_cross, dv_cross, cross_in]
    dq_self, dk_self, dv_self, *weight_grads, tick = run(
        functools.partial(self_backward_kernel, chunks),
        "self_backward",
        (rows,),
        [grad_after_self, q_self, k_self, v_self, probs_self, wo_self] + moved,
        [by_row(array) for array in (grad_after_self, q_self, k_self, v_self, probs_self)]
        + [whole(wo_self)]
        + [anywhere] * len(moved),
        [flat] * 3 + weight_outs,
        [by_row(flat)] * 3 + weight_specs,
        LIGHT * dense_flops,
        scratch=[
            pltpu.VMEM((2, tokens, width), LOW),
            pltpu.VMEM((4, tokens, width), LOW),
            pltpu.VMEM((3, tokens, width), LOW),
            pltpu.VMEM((4, tokens, width), LOW),
            pltpu.SemaphoreType.DMA((len(moved),)),
        ]
        + held(weight_outs, (2, 4)),
        prefetch=(place,),
        after=[tick],
    )
    from_chip = across(memory_grad, 2)
    waits = [tick]
    if chunks:
        feed_operand = added([jnp.moveaxis(part, 0, 1) for part in feed_parts], tick)
        tick = pause(25e9, [feed_operand, tick])
        feed_line = exchange(feed_operand)
        parts = from_core(weight_grads)
        weight_sends = [added([part[x_to, :, y_to] for part in parts], tick) for x_to, y_to in PLANE]
        weight_plane = plane_arrived(weight_sends)
        waits = [tick] + weight_sends
    input_grad, tick = row_call(
        input_grad_kernel,
        "input_grad",
        (dq_self, dk_self, dv_self, inputs, grad_after_self),
        (wq_self, wk_self, wv_self, g_self),
        [flat],
        LIGHT * dense_flops,
        "rrrfffrfr",
        after=waits,
    )
    waits = [tick, layer_out]

    arrived = [memory_grad, across(memory_grad, 1), from_chip, across(from_chip, 1)]
    own_hits = lax.dynamic_slice_in_dim(block_hits, layer_at, 1, 1)[:, 0]
    encoder_shape = shape_of(encoder_out.shape, FULL)
    encoder_grad, tick = run(
        encoder_grad_kernel,
        "encoder_grad",
        (4,),
        arrived,
        [whole(array) for array in arrived],
        [encoder_shape],
        [pl.BlockSpec((1, tokens, width), lambda at, place, hits: (0, place[0] ^ at, 0))],
        LIGHT * encoder_out.size,
        prefetch=(place, own_hits),
        after=waits,
    )

    if chunks:
        feed_chip = added([feed_line[at] for at in range(dp_size // 2)], tick)
        tick = pause(0, [feed_chip])
        weight_operand = added([part[0, :, 0] for part in parts] + weight_plane, tick)
        weight_line = exchange(weight_operand)
        feed_chip = added([feed_chip, across(feed_chip, 2)[::-1]], tick)
        feed_other = across(feed_chip, 1)
        feed_pieces = [feed_chip[0], feed_other[0], feed_chip[1], feed_other[1]]

        def gathered(piece):
            from_x = across(piece, 2)
            return [piece, across(piece, 1), from_x, across(from_x, 1)]

        def final_call(body, name, pieces, chunk_weights, gains, outs, scratch):
            ins = pieces + chunk_weights + gains
            outs = outs + [shape_of((1, 1, length), FULL)] * len(gains)
            return run(
                body,
                name,
                (1,),
                ins,
                [whole(array) for array in pieces]
                + [
                    pl.BlockSpec((length, array.shape[1]), lambda at, place: (place[1], 0))
                    for array in chunk_weights
                ]
                + [whole(gain) for gain in gains],
                outs,
                [whole(out) for out in outs],
                LIGHT * length * width * width,
                scratch=scratch,
                prefetch=(place,),
                after=list(waits),
            )

        waits = [weight_operand]
        *feed_finals, tick = final_call(
            feed_final_kernel,
            "feed_final",
            feed_pieces,
            [feed_up],
            [gain_feed],
            [shape_of((length, hidden), FULL), shape_of((hidden // chunks, width), FULL)],
            [pltpu.VMEM((2, length, hidden // 2), LOW)],
        )
        waits = []
        weight_piece = added([weight_line[at] for at in range(dp_size // 2)], tick)
        *finals, _ = final_call(
            weight_final_kernel,
            "weight_final",
            gathered(weight_piece),
            [wq_self, wk_self, wv_self, wq_cross],
            [gain_self, gain_cross],
            [shape_of((length, width), FULL)] * 8,
            [pltpu.VMEM((4, length, width), LOW)] * 2,
        )
        weight_grads = finals[:8] + feed_finals[:2]
        gain_grads = [value.reshape(length) for value in finals[8:] + feed_finals[2:]]
    else:
        back_order = order_matrix(width, True)

        def total(grad):
            part = lax.psum_scatter(grad.astype(FULL), "dp", scatter_dimension=0, tiled=True)
            return lax.psum(part.astype(LOW), "layer").astype(FULL)

        def natural(grads):
            back = [nn(grads[at], back_order).astype(LOW) for at in range(3)]
            return [total(grad) for grad in back + [nn(back_order.T, grads[3]).astype(LOW)]]

        grads_cross, grads_self = (natural(grads) for grads in weight_grads)
        core = layer_at % 2
        up_shape, down_shape = (width, -1, 2, UNITS // 2), (-1, 2, UNITS // 2, width)
        up_part = feed_grads[0].reshape(width, -1, 1, UNITS // 2)
        down_part = feed_grads[1].reshape(-1, 1, UNITS // 2, width)
        up_all = jnp.zeros(feed_up.shape, LOW).reshape(up_shape)
        down_all = jnp.zeros(feed_down.shape, LOW).reshape(down_shape)
        up_all = lax.dynamic_update_slice_in_dim(up_all, up_part, core, 2).reshape(feed_up.shape)
        down_all = lax.dynamic_update_slice_in_dim(down_all, down_part, core, 1).reshape(feed_down.shape)
        weight_grads = grads_self + grads_cross + [total(up_all), total(down_all)]
        length = width // dp_size

        def my_rows(array):
            return lax.dynamic_slice_in_dim(array, dp_at * length, length, 0).astype(FULL)

        def gain_total(pairs, gain):
            sums = sum(jnp.sum(my_rows(weight) * grad, axis=1) for weight, grad in pairs)
            return sums / my_rows(gain)

        gain_grads = [
            gain_total(zip((query_self, key_self, value_self), grads_self), gain_self),
            gain_total([(query_cross, grads_cross[0])], gain_cross),
            gain_total([(feed_up, weight_grads[8])], gain_feed),
        ]
    return (layer_out, input_grad, encoder_grad, *weight_grads, *gain_grads)


def solution(mesh):
    in_specs = (
        P(("dp", "layer"), None),
        P("layer", "dp", None),
        *[P()] * 13,
        P(("dp", "layer"), None),
        P(("dp", "layer"), None),
        P("dp"),
        P(),
        P(("dp", "layer"), None),
    )
    out_specs = (
        P(("dp", "layer"), None),
        P(("dp", "layer"), None),
        P("layer", "dp", None),
        *[P("dp", None)] * 10,
        *[P("dp")] * 3,
    )
    body = functools.partial(on_device, mesh.shape["layer"], mesh.shape["dp"])
    return jax.shard_map(
        body, mesh=mesh, in_specs=in_specs, out_specs=out_specs, check_vma=False
    )
```

```python
import functools
import math

import jax
import jax.numpy as jnp
from jax import lax
from jax.experimental import pallas as pl
from jax.experimental.pallas import tpu as pltpu
from jax.sharding import PartitionSpec as P

HEADS = 8
HEAD = 80
MAIN = 64
REST = 16
ROW_LEN = 256
BLOCK = 256
FEED_TOKENS = 256
UNITS = 384
SCALE = 1.0 / math.sqrt(HEAD)
LOW = jnp.bfloat16
FULL = jnp.float32
VMEM_BYTES = 56 * 1024 * 1024
WEIGHT = 1.0
LIGHT = 0.05


def dot(left, right, left_dim, right_dim):
    return lax.dot_general(
        left, right, (((left_dim,), (right_dim,)), ((), ())), preferred_element_type=FULL
    )


def nn(left, right):
    return dot(left, right, 1, 0)


def nt(left, right):
    return dot(left, right, 1, 1)


def tn(left, right):
    return dot(left, right, 0, 0)


def norm_parts(value):
    centred = value - jnp.mean(value, axis=-1, keepdims=True)
    inverse = lax.rsqrt(jnp.mean(centred * centred, axis=-1, keepdims=True) + 1e-05)
    return (centred * inverse, inverse)


def norm_forward(value, gain):
    return (norm_parts(value)[0] * gain).astype(LOW)


def norm_backward(grad, value, gain):
    normed, inverse = norm_parts(value)
    scaled = grad * gain
    inner = (
        scaled
        - jnp.mean(scaled, axis=-1, keepdims=True)
        - normed * jnp.mean(scaled * normed, axis=-1, keepdims=True)
    )
    return inner * inverse


def source_column(position):
    rest = position - HEADS * MAIN
    return jnp.where(
        rest < 0,
        HEAD * (position // MAIN) + position % MAIN,
        HEAD * (rest // REST) + MAIN + rest % REST,
    )


def ones_where_equal(sources, size, source_axis):
    shape = [size, size]
    shape[source_axis] = sources.shape[source_axis]
    index = lax.broadcasted_iota(jnp.int32, tuple(shape), 1 - source_axis)
    return (index == sources).astype(FULL).astype(LOW)


def order_matrix(width, transposed):
    axis = 1 - int(transposed)
    shape = (1, width) if axis else (width, 1)
    return ones_where_equal(source_column(lax.broadcasted_iota(jnp.int32, shape, axis)), width, axis)


def head_groups(array, head):
    pair = head // 2
    return jnp.concatenate(
        [array[:, 2 * MAIN * pair : 2 * MAIN * (pair + 1)], array[:, HEADS * MAIN :]], axis=1
    )


def head_mask(head):
    lane = lax.broadcasted_iota(jnp.int32, (1, 2 * MAIN + HEADS * REST), 1)
    rest = lane - 2 * MAIN
    owner = jnp.where(rest < 0, 2 * (head // 2) + lane // MAIN, rest // REST)
    return (owner == head).astype(FULL).astype(LOW)


def same_segment(key_seg, query_seg):
    shape = (16, key_seg.shape[1])
    number = lax.broadcasted_iota(jnp.int32, shape, 0)
    key_hot = (number == key_seg).astype(FULL).astype(LOW)
    query_hot = (number == query_seg).astype(FULL).astype(LOW)
    return tn(key_hot, query_hot)


def merge_pairs(parts):
    mains = [part[:, : 2 * MAIN] for part in parts]
    rests = [part[:, 2 * MAIN :] for part in parts]
    while len(rests) > 1:
        rests = [rests[i] + rests[i + 1] for i in range(0, len(rests), 2)]
    return jnp.concatenate(mains + rests, axis=1)


def attend(queries, keys, values, bias, probs_ref):
    parts = []
    for pair in range(HEADS // 2):
        pair_probs, pair_values = [], []
        for head in (2 * pair, 2 * pair + 1):
            mask = head_mask(head)
            scores = nt(head_groups(keys, head), head_groups(queries, head) * mask) * SCALE + bias
            raised = jnp.exp(scores - jnp.max(scores, axis=0, keepdims=True))
            probs = (raised * (1.0 / jnp.sum(raised, axis=0, keepdims=True))).astype(LOW)
            probs_ref[0, head] = probs
            pair_probs.append(probs)
            pair_values.append(head_groups(values, head) * mask)
        parts.append(
            tn(jnp.concatenate(pair_probs, axis=0), jnp.concatenate(pair_values, axis=0))
        )
    return merge_pairs(parts).astype(LOW)


def attend_back(grad, queries, keys, values, probs_ref):
    query_parts, key_parts, value_parts = [], [], []
    for pair in range(HEADS // 2):
        pair_probs, pair_slopes, pair_grads, pair_queries, pair_keys = [], [], [], [], []
        for head in (2 * pair, 2 * pair + 1):
            mask = head_mask(head)
            grad_head = head_groups(grad, head) * mask
            probs = probs_ref[0, head]
            wide = probs.astype(FULL)
            prob_grad = nt(head_groups(values, head), grad_head)
            delta = jnp.sum(prob_grad * wide, axis=0, keepdims=True)
            pair_probs.append(probs)
            pair_slopes.append((wide * (prob_grad - delta)).astype(LOW))
            pair_grads.append(grad_head)
            pair_queries.append(head_groups(queries, head) * mask)
            pair_keys.append(head_groups(keys, head) * mask)
        query_parts.append(
            tn(jnp.concatenate(pair_slopes, axis=0), jnp.concatenate(pair_keys, axis=0))
        )
        key_parts.append(
            nn(jnp.concatenate(pair_slopes, axis=1), jnp.concatenate(pair_queries, axis=0))
        )
        value_parts.append(
            nn(jnp.concatenate(pair_probs, axis=1), jnp.concatenate(pair_grads, axis=0))
        )
    return (
        (merge_pairs(query_parts) * SCALE).astype(LOW),
        (merge_pairs(key_parts) * SCALE).astype(LOW),
        merge_pairs(value_parts).astype(LOW),
    )


PLANE = ((1, 1), (1, 0), (0, 1))


def pick_matrix(core, transposed):
    axis = 1 - int(transposed)
    taken = lax.broadcasted_iota(jnp.int32, (1, UNITS) if axis else (UNITS, 1), axis)
    half = UNITS // 2
    return ones_where_equal(UNITS * (taken // half) + half * core + taken % half, 2 * UNITS, axis)


def order_kernel(place_ref, *refs):
    sources, targets, refs = refs[:9], refs[9:18], refs[18:]
    froms, tos, refs = (*refs[:2], refs[2]), (*refs[3:5], refs[5]), refs[6:]
    in_sems, out_sems = refs
    core = lax.bitwise_and(place_ref[0], 1)
    columns_in, rows_in, up_in = froms
    columns_out, rows_out, up_out = tos
    ins = [columns_in.at[at] for at in range(6)] + [rows_in.at[at] for at in range(2)] + [up_in]
    outs = [columns_out.at[at] for at in range(6)] + [rows_out.at[at] for at in range(2)] + [up_out]
    fetches = [pltpu.make_async_copy(*pair, in_sems.at[at]) for at, pair in enumerate(zip(sources, ins))]
    stores = [pltpu.make_async_copy(*pair, out_sems.at[at]) for at, pair in enumerate(zip(outs, targets))]
    for fetch in fetches:
        fetch.start()
    order = order_matrix(columns_in.shape[1], False)
    for at in range(6):
        fetches[at].wait()
        columns_out[at] = nn(columns_in[at], order).astype(LOW)
        stores[at].start()
    for at in range(2):
        fetches[6 + at].wait()
        for head in range(HEADS):
            base = HEAD * head
            rows_out[at, MAIN * head : MAIN * (head + 1)] = rows_in[at, base : base + MAIN]
            rest = HEADS * MAIN + REST * head
            rows_out[at, rest : rest + REST] = rows_in[at, base + MAIN : base + HEAD]
        stores[6 + at].start()
    pick = pick_matrix(core, False)
    fetches[8].wait()
    for pair in range(up_in.shape[1] // (2 * UNITS)):
        columns = slice(2 * UNITS * pair, 2 * UNITS * (pair + 1))
        up_out[:, UNITS * pair : UNITS * (pair + 1)] = nn(up_in[:, columns], pick).astype(LOW)
    stores[8].start()
    for store in stores:
        store.wait()


def self_forward_kernel(
    x_ref, seg_ref, gain_ref, next_gain_ref, wq_ref, wk_ref, wv_ref, wo_ref, next_wq_ref,
    normed_ref, q_ref, k_ref, v_ref, probs_ref, attn_ref, after_ref, next_normed_ref, next_q_ref,
):
    value = x_ref[...].astype(FULL)
    normed = norm_forward(value, gain_ref[...])
    normed_ref[...] = normed
    queries = nn(normed, wq_ref[...]).astype(LOW)
    keys = nn(normed, wk_ref[...]).astype(LOW)
    values = nn(normed, wv_ref[...]).astype(LOW)
    q_ref[...], k_ref[...], v_ref[...] = queries, keys, values
    seg = seg_ref[pl.ds(pl.program_id(0), 1), :]
    key_at = lax.broadcasted_iota(jnp.int32, (ROW_LEN, ROW_LEN), 0)
    query_at = lax.broadcasted_iota(jnp.int32, (ROW_LEN, ROW_LEN), 1)
    allowed = (same_segment(seg, seg) > 0.5) & (key_at <= query_at)
    attn = attend(queries, keys, values, jnp.where(allowed, 0.0, -1e9), probs_ref)
    attn_ref[...] = attn
    after = value + nn(attn, wo_ref[...])
    after_ref[...] = after
    next_normed = norm_forward(after, next_gain_ref[...])
    next_normed_ref[...] = next_normed
    next_q_ref[...] = nn(next_normed, next_wq_ref[...]).astype(LOW)


def cross_forward_kernel(
    place_ref, hits_ref, own_ref, near_ref, far_ref, q_ref, after_ref, seg_target_ref, seg_source_ref, gain_ref,
    wk_ref, wv_ref, wo_ref, memory_ref, k_ref, v_ref, probs_ref, attn_ref, next_after_ref, next_normed_ref,
):
    step = pl.program_id(0)
    own = 0.5 * hits_ref[0, step] * own_ref[0].astype(FULL)
    near = 0.5 * hits_ref[1, step] * near_ref[0].astype(FULL)
    memory = (own + near + far_ref[...].astype(FULL)).astype(LOW)
    memory_ref[...] = memory
    keys = nn(memory, wk_ref[...]).astype(LOW)
    values = nn(memory, wv_ref[...]).astype(LOW)
    k_ref[...], v_ref[...] = keys, values
    row = pl.ds(pl.program_id(0), 1)
    allowed = same_segment(seg_source_ref[row, :], seg_target_ref[row, :]) > 0.5
    attn = attend(q_ref[...], keys, values, jnp.where(allowed, 0.0, -1e9), probs_ref)
    attn_ref[...] = attn
    after = after_ref[...] + nn(attn, wo_ref[...])
    next_after_ref[...] = after
    next_normed_ref[...] = norm_forward(after, gain_ref[...])


def store_piece(place_ref, held_ref, quarter, chunk, rows, columns, piece):
    owner = lax.bitwise_xor(place_ref[0], quarter)
    dp_at = lax.bitwise_xor(chunk, lax.bitwise_and(place_ref[1], 1))
    held_ref[
        lax.bitwise_and(owner, 1), lax.shift_right_logical(owner, 1), dp_at, rows, columns
    ] = piece


def store_feed(place_ref, held_ref, x_of, chunk, rows, columns, piece):
    x_at = lax.bitwise_xor(x_of, lax.shift_right_logical(place_ref[0], 1))
    y_at = lax.bitwise_xor(lax.bitwise_and(chunk, 1), lax.bitwise_and(place_ref[1], 1))
    held_ref[x_at, y_at, lax.shift_right_logical(chunk, 1), rows, columns] = piece


def hand_out(place_ref, held_ref, targets, sem, quarter, region):
    owner = lax.bitwise_xor(place_ref[0], quarter)
    x_at = lax.shift_right_logical(owner, 1)
    for half in range(2):

        @pl.when(lax.bitwise_and(owner, 1) == half)
        def _():
            pltpu.make_async_copy(
                held_ref.at[(half, x_at) + region], targets[half].at[(x_at,) + region], sem
            ).start()


def hand_out_done(held_ref, targets, sem, region):
    pltpu.make_async_copy(held_ref.at[(0, 0) + region], targets[0].at[(0,) + region], sem).wait()


def feed_kernel(chunks, place_ref, *refs):
    normed_refs, grad_refs, (up_ref, down_all, after_ref), refs = refs[:2], refs[2:4], refs[4:7], refs[7:]
    (acc_out, back_out, acc_send, back_send), targets, refs = refs[:4], refs[4:6], refs[6:]
    normed_ref, grad_ref, hidden_ref, pre_ref, down_ref, down_sems, *held = refs
    step, steps = pl.program_id(0), pl.num_programs(0)
    size, width = after_ref.shape
    units = up_ref.shape[1]

    rows = pl.ds(pl.multiple_of(step * size, size), size)
    tokens = normed_refs[1].shape[0]
    others = [
        pltpu.make_async_copy(source, target.at[tokens:], down_sems.at[down_all.shape[0] + at])
        for at, (source, target) in enumerate(((normed_refs[1], normed_ref), (grad_refs[1], grad_ref)))
    ]

    @pl.when(step == 0)
    def _():
        half, core = UNITS // 2, lax.bitwise_and(place_ref[0], 1)
        fetches = [
            pltpu.make_async_copy(
                down_all.at[at, core], down_ref.at[half * at : half * (at + 1)], down_sems.at[at]
            )
            for at in range(down_all.shape[0])
        ]
        for fetch in fetches + others:
            fetch.start()
        for fetch in fetches:
            fetch.wait()

    def tokens_step(normed, grad):
        pre = nn(normed, up_ref[...])
        hidden_grad = nt(grad, down_ref[...])
        square = pre * pre
        slope = math.sqrt(2.0 / math.pi)
        bend = jnp.tanh(pre * (slope + slope * 0.044715 * square))
        half = 0.5 + 0.5 * bend
        hidden = (pre * half).astype(LOW)
        rate = half + pre * half * (1.0 - bend) * (slope + slope * 3 * 0.044715 * square)
        pre_grad = (hidden_grad * rate).astype(LOW)
        hidden_ref[rows, :] = hidden
        pre_ref[rows, :] = pre_grad
        return nn(hidden, down_ref[...]), nt(pre_grad, up_ref[...])

    @pl.when(step < steps // 2)
    def _():
        normed_ref[rows, :] = normed_refs[0][...]
        grad_ref[rows, :] = grad_refs[0][...]
        acc, back = tokens_step(normed_refs[0][...], grad_refs[0][...])
        acc_out[...] = after_ref[...] + acc
        back_out[...] = back

    @pl.when(step == steps // 2)
    def _():
        for fetch in others:
            fetch.wait()

    @pl.when((step >= steps // 2) & (step < steps - 1))
    def _():
        acc, back = tokens_step(normed_ref[rows, :], grad_ref[rows, :])
        acc_send[...] = acc.astype(LOW)
        back_send[...] = back.astype(LOW)

    @pl.when(step == steps - 1)
    def _():
        if not chunks:
            targets[0][...] = tn(normed_ref[...], pre_ref[...]).astype(LOW)
            targets[1][...] = tn(hidden_ref[...], grad_ref[...]).astype(LOW)
            return
        held_ref, held_sems = held
        length = width // chunks
        part = UNITS // 4
        share = units // 2
        fold = share - width
        top = length + REST

        def copies(at, rows):
            return [
                pltpu.make_async_copy(
                    held_ref.at[x_at, y_at, :, rows], targets[y_at].at[:, x_at, rows], held_sems.at[at, y_at, x_at]
                )
                for y_at in (1, 0)
                for x_at in range(2)
            ]

        ups, downs = copies(0, slice(0, top)), copies(1, slice(top, held_ref.shape[3]))
        for start in range(0, units, BLOCK):
            x_of, first = start // share, start % share
            up_grad = tn(normed_ref[...], pre_ref[:, start : start + BLOCK]).astype(LOW)
            for chunk in range(chunks):
                piece = up_grad[length * chunk : length * (chunk + 1)]
                inside = min(width - first, BLOCK)
                store_feed(
                    place_ref, held_ref, x_of, chunk,
                    slice(0, length), slice(first, first + inside), piece[:, :inside],
                )
                if inside < BLOCK:
                    for at in range(width // fold):
                        rows = REST * at
                        store_feed(
                            place_ref, held_ref, x_of, chunk,
                            slice(length, top), slice(fold * at, fold * (at + 1)),
                            piece[rows : rows + REST, inside:],
                        )
        for copy in ups:
            copy.start()
        for start in range(0, units, BLOCK):
            down_grad = tn(hidden_ref[:, start : start + BLOCK], grad_ref[...]).astype(LOW)
            for row in range(start, start + BLOCK, 32):
                chunk, inside = row // (2 * part), row % (2 * part)
                base = top + inside % part
                store_feed(
                    place_ref, held_ref, inside // part, chunk,
                    slice(base, base + 32), slice(0, width), down_grad[row - start : row - start + 32],
                )
        for copy in downs:
            copy.start()
        for copy in ups + downs:
            copy.wait()


def cross_backward_kernel(
    back_ref, back_other_ref, after_cross_ref, gain_feed_ref, grad_ref, after_self_ref, gain_cross_ref,
    q_ref, k_ref, v_ref, probs_ref, wq_ref, wk_ref, wv_ref, wo_ref,
    in_ref, dq_ref, dk_ref, dv_ref, memory_ref, grad_self_ref,
):
    grad = grad_ref[...].astype(FULL) + norm_backward(
        back_ref[...] + back_other_ref[...].astype(FULL), after_cross_ref[...], gain_feed_ref[...]
    )
    branch = grad.astype(LOW)
    in_ref[...] = branch
    query_grad, key_grad, value_grad = attend_back(
        nt(branch, wo_ref[...]).astype(LOW), q_ref[...], k_ref[...], v_ref[...], probs_ref
    )
    dq_ref[...], dk_ref[...], dv_ref[...] = query_grad, key_grad, value_grad
    memory_ref[...] = (nt(key_grad, wk_ref[...]) + nt(value_grad, wv_ref[...])).astype(LOW)
    grad_self_ref[...] = grad + norm_backward(
        nt(query_grad, wq_ref[...]), after_self_ref[...], gain_cross_ref[...]
    )


def input_grad_kernel(dq_ref, dk_ref, dv_ref, wq_ref, wk_ref, wv_ref, x_ref, gain_ref, grad_ref, out_ref):
    inner = (
        nt(dq_ref[...], wq_ref[...]) + nt(dk_ref[...], wk_ref[...]) + nt(dv_ref[...], wv_ref[...])
    )
    back = norm_backward(inner, x_ref[...].astype(FULL), gain_ref[...])
    out_ref[...] = (grad_ref[...] + back).astype(LOW)


def weight_product(chunks, place_ref, left, right, weight, base, target, held_ref):
    width = right.shape[1]
    for start in range(0, width, BLOCK):
        columns = slice(start, min(start + BLOCK, width))
        grad = tn(left[...], right[:, columns]).astype(LOW)
        if not chunks:
            target[weight, :, columns] = grad
            continue
        length = width // chunks
        for chunk in range(chunks):
            piece = grad[length * chunk : length * (chunk + 1)]
            if weight == 3:
                rest = HEADS * MAIN + REST * chunk
                piece = jnp.concatenate(
                    [grad[MAIN * chunk : MAIN * (chunk + 1)], grad[rest : rest + REST]], axis=0
                )
            store_piece(place_ref, held_ref, weight, chunk, slice(base, base + length), columns, piece)


def self_backward_kernel(
    chunks, place_ref, grad_ref, q_ref, k_ref, v_ref, probs_ref, wo_ref, *refs
):
    sources, (dq_ref, dk_ref, dv_ref, *refs) = refs[:9], refs[9:]
    targets, (left_ref, right_ref, cross_left, cross_right, sems, *held) = refs[:2], refs[2:]
    held_ref, held_sems = held if chunks else (None, None)
    step, steps = pl.program_id(0), pl.num_programs(0)
    places = [left_ref.at[0], left_ref.at[1]]
    places += [cross_left.at[at] for at in range(3)] + [cross_right.at[at] for at in range(4)]
    copies = [
        pltpu.make_async_copy(source, place, sems.at[at])
        for at, (source, place) in enumerate(zip(sources, places))
    ]
    needs = ((2, 5), (3, 6), (7,), (4, 8))

    @pl.when(step == 0)
    def _():
        for at in sum(needs, ()) + (0, 1):
            copies[at].start()

    rows = pl.ds(pl.multiple_of(step * ROW_LEN, ROW_LEN), ROW_LEN)
    branch = grad_ref[...].astype(LOW)
    grads = attend_back(
        nt(branch, wo_ref[...]).astype(LOW), q_ref[...], k_ref[...], v_ref[...], probs_ref
    )
    for at, (ref, grad) in enumerate(zip((dq_ref, dk_ref, dv_ref), grads)):
        ref[...] = grad
        right_ref[at, rows, :] = grad
    right_ref[3, rows, :] = branch
    length = dq_ref.shape[1] // HEADS
    cross_rows, self_rows = slice(0, length), slice(length, 2 * length)

    def region(part):
        return (slice(None), part)

    for weight in range(4):

        @pl.when(step == weight)
        def _():
            for at in needs[weight]:
                copies[at].wait()
            left = cross_left.at[(0, 1, 1, 2)[weight]]
            weight_product(
                chunks, place_ref, left, cross_right.at[weight], weight, cross_rows.start, targets[0], held_ref
            )
            if chunks:
                hand_out(place_ref, held_ref, targets, held_sems.at[0, weight], weight, region(cross_rows))

    @pl.when(step == steps - 1)
    def _():
        for copy in copies[:2]:
            copy.wait()
        for weight in range(4):
            left = left_ref.at[weight // 3]
            weight_product(
                chunks, place_ref, left, right_ref.at[weight], weight, self_rows.start, targets[1], held_ref
            )
            if chunks:
                hand_out(place_ref, held_ref, targets, held_sems.at[1, weight], weight, region(self_rows))
        if chunks:
            for group, part in enumerate((cross_rows, self_rows)):
                for weight in range(4):
                    hand_out_done(held_ref, targets, held_sems.at[group, weight], region(part))


def encoder_grad_kernel(place_ref, hits_ref, *refs):
    out_ref = refs[-1]
    step = pl.program_id(0)
    for turn in range(4):

        @pl.when(step == turn)
        def _():
            tokens = refs[turn].shape[0]
            rows = tokens // ROW_LEN
            owner = lax.bitwise_xor(place_ref[0], turn)
            for row in range(rows):
                here = slice(ROW_LEN * row, ROW_LEN * (row + 1))
                weight = 0.5 * hits_ref[owner * rows + row]
                out_ref[0, here, :] = weight * refs[turn][here, :].astype(FULL)


def gain_grad(place_ref, pairs, gain_ref, target):
    total = sum(
        jnp.sum(weight.astype(FULL) * grad.astype(FULL), axis=1, keepdims=True) for weight, grad in pairs
    )
    length = total.shape[0]
    width = gain_ref.shape[0]
    turned = jnp.broadcast_to(total, (length, 128)).T
    gains = jnp.broadcast_to(gain_ref[...].reshape(1, width), (8, width))
    mine = pltpu.roll(gains, lax.rem(width - length * place_ref[1], width), 1)
    target[0] = turned[:1] / mine[:1, :length]


def feed_final_kernel(place_ref, *refs):
    sources, (up_ref, gain_ref, up_out, down_out, gain_out, half_ref) = refs[:4], refs[4:]
    length = up_out.shape[0]
    part = down_out.shape[0] // 4
    share = up_out.shape[1] // 4
    width = down_out.shape[1]
    fold = share - width
    for turn, piece in enumerate(sources):
        owner = lax.bitwise_xor(place_ref[0], turn)
        x_of, core = lax.shift_right_logical(owner, 1), lax.bitwise_and(owner, 1)
        start = pl.multiple_of(x_of * share, 128)
        half_ref[core, :, pl.ds(start, width)] = piece[:length, :]
        for at in range(width // fold):
            half_ref[
                core, REST * at : REST * (at + 1), pl.ds(pl.multiple_of(start + width, 128), fold)
            ] = piece[length : length + REST, fold * at : fold * (at + 1)]
        rows = pl.ds(pl.multiple_of((2 * core + x_of) * part, 32), part)
        down_out[rows, :] = piece[length + REST :, :].astype(FULL)
    picks = [pick_matrix(core, True) for core in range(2)]
    for pair in range(up_out.shape[1] // (2 * UNITS)):
        columns = slice(UNITS * pair, UNITS * (pair + 1))
        up_out[:, 2 * UNITS * pair : 2 * UNITS * (pair + 1)] = nn(
            half_ref[0, :, columns], picks[0]
        ) + nn(half_ref[1, :, columns], picks[1])
    gain_grad(place_ref, [(up_ref[...], up_out[...])], gain_ref, gain_out)


def weight_final_kernel(place_ref, *refs):
    sources, weights, gains, targets = refs[:4], refs[4:8], refs[8:10], refs[10:-2]
    cross_ref, self_ref = refs[-2:]
    length = cross_ref.shape[1]
    for turn, piece in enumerate(sources):
        owner = lax.bitwise_xor(place_ref[0], turn)
        cross_ref[owner] = piece[:length, :]
        self_ref[owner] = piece[length:, :]
    order = order_matrix(cross_ref.shape[2], True)
    for at in range(3):
        targets[at][...] = nn(self_ref[at], order)
        targets[4 + at][...] = nn(cross_ref[at], order)
    targets[3][...] = self_ref[3].astype(FULL)
    targets[7][...] = cross_ref[3].astype(FULL)
    gain_grad(place_ref, [(weights[at][...], self_ref[at]) for at in range(3)], gains[0], targets[8])
    gain_grad(place_ref, [(weights[3][...], cross_ref[0])], gains[1], targets[9])


def whole(array):
    return pl.BlockSpec(array.shape, lambda *at: (0,) * array.ndim)


def by_row(array, first=0):
    if array.ndim == 2:
        return pl.BlockSpec((ROW_LEN, array.shape[1]), lambda at, *_: (at + first, 0))
    return pl.BlockSpec(
        (1,) + array.shape[1:], lambda at, *_: (at + first,) + (0,) * (array.ndim - 1)
    )


def run(
    body, name, grid, ins, in_specs, outs, out_specs, flops, scratch=(), prefetch=(), after=(), into=()
):
    after = list(into) + list(after)
    outs = list(outs) + [shape_of((1, 1), FULL)]
    out_specs = list(out_specs) + [pl.BlockSpec(memory_space=pltpu.SMEM)]
    moved = sum(array.size * array.dtype.itemsize for array in list(ins) + list(outs))
    first, last = len(prefetch) + len(ins), len(prefetch) + len(ins) + len(after)

    tick_at = last + len(outs) - 1

    def ordered_body(*refs):
        refs[tick_at][0, 0] = 0.0
        body(*refs[:first], *refs[last:tick_at], *refs[tick_at + 1 :])

    return pl.pallas_call(
        ordered_body,
        name=name,
        out_shape=outs,
        grid_spec=pltpu.PrefetchScalarGridSpec(
            num_scalar_prefetch=len(prefetch),
            grid=grid,
            in_specs=list(in_specs) + [pl.BlockSpec(memory_space=pl.ANY)] * len(after),
            out_specs=out_specs,
            scratch_shapes=scratch,
        ),
        input_output_aliases={first + at: at for at in range(len(into))},
        compiler_params=pltpu.CompilerParams(vmem_limit_bytes=VMEM_BYTES),
        cost_estimate=pl.CostEstimate(
            flops=int(flops * WEIGHT), bytes_accessed=int(moved * WEIGHT), transcendentals=0
        ),
    )(*prefetch, *ins, *after)


def pause(flops, after):
    return run(lambda: None, "pause", (1,), [], [], [], [], flops, after=after)[0]


def shape_of(shape, dtype=LOW):
    return jax.ShapeDtypeStruct(tuple(shape), dtype)


def row_call(body, name, rowed, fixed, outs, flops, order, after=(), part=None, into=()):
    first, last = part or (0, outs[0].shape[0] // ROW_LEN)
    ins, specs = [], []
    rowed, fixed = list(rowed), list(fixed)
    for kind in order:
        array = rowed.pop(0) if kind == "r" else fixed.pop(0)
        ins.append(array)
        specs.append(by_row(array, first) if kind == "r" else whole(array))
    return run(
        body,
        name,
        (last - first,),
        ins,
        specs,
        outs,
        [by_row(out, first) for out in outs],
        flops,
        after=after,
        into=into,
    )


def permuted(value, axes, sizes, flip):
    count = math.prod(sizes)
    return lax.ppermute(value, axes, [(at, at ^ flip) for at in range(count)])


def added(parts, tick=None):
    total = parts[0].astype(FULL)
    if tick is not None:
        total = total + tick[0, 0]
    for part in parts[1:]:
        total = total + part.astype(FULL)
    return total.astype(LOW)


def on_device(
    layer_size,
    dp_size,
    inputs,
    encoder_out,
    query_self,
    key_self,
    value_self,
    out_self,
    query_cross,
    key_cross,
    value_cross,
    out_cross,
    feed_up,
    feed_down,
    gain_self,
    gain_cross,
    gain_feed,
    seg_target,
    seg_source,
    subnet_of_row,
    chosen_layers,
    out_grad,
):
    tokens, width = inputs.shape
    rows = tokens // ROW_LEN
    layer_at = lax.axis_index("layer")
    dp_at = lax.axis_index("dp")
    place = jnp.stack([layer_at, dp_at]).astype(jnp.int32)
    axes, sizes = ("dp", "layer"), (dp_size, layer_size)

    def across(value, layer_flip, dp_flip=0):
        return permuted(value, axes, sizes, dp_flip * layer_size + layer_flip)

    picked = jnp.sum(
        (chosen_layers[:, :, None] == jnp.arange(layer_size)[None, None, :]).astype(FULL), axis=1
    )
    row_pick = (subnet_of_row[:, None] == jnp.arange(chosen_layers.shape[0])[None, :]).astype(FULL)
    block_hits = jnp.sum(row_pick[:, :, None] * picked[None], axis=1)
    own_layer = encoder_out.reshape(layer_size, rows, ROW_LEN, width)

    def own_block(flip):
        return lax.dynamic_index_in_dim(own_layer, layer_at ^ flip, 0, keepdims=False)

    def hits_of(flip, layer_flip):
        hits = lax.dynamic_slice_in_dim(block_hits, (layer_at ^ flip) * rows, rows, 0)
        hits = lax.dynamic_slice_in_dim(hits, layer_at ^ layer_flip, 1, 1)
        return 0.5 * hits[:, :, None]

    def chip_sum(flip, arrived):
        total = hits_of(flip, 0) * own_block(flip).astype(FULL)
        total = total + hits_of(flip, 1) * arrived.astype(FULL)
        return total.astype(LOW).reshape(tokens, width)

    far_half = across(own_block(3), 1)
    near_half = across(own_block(1), 1)
    far_memory = across(chip_sum(2, far_half), 2)

    weights = [query_self, key_self, value_self, query_cross, key_cross, value_cross, out_self, out_cross, feed_up]
    order_outs = [shape_of(array.shape) for array in weights[:8]]
    order_outs.append(shape_of((width, feed_up.shape[1] // 2)))
    ordered = run(
        order_kernel,
        "order_weights",
        (1,),
        weights,
        [pl.BlockSpec(memory_space=pl.ANY)] * 9,
        order_outs,
        [pl.BlockSpec(memory_space=pl.ANY)] * 9,
        12 * width**3,
        scratch=[
            pltpu.VMEM(shape, LOW)
            for columns in (feed_up.shape[1], feed_up.shape[1] // 2)
            for shape in ((6, width, width), (2, width, width), (width, columns))
        ]
        + [pltpu.SemaphoreType.DMA((9,))] * 2,
        prefetch=(place,),
    )
    wq_self, wk_self, wv_self, wq_cross, wk_cross, wv_cross, wo_self, wo_cross, up_half, _ = ordered
    g_self, g_cross, g_feed = gain_self, gain_cross, gain_feed
    flat = shape_of((tokens, width))
    wide = shape_of((tokens, width), FULL)
    probs = shape_of((rows, HEADS, ROW_LEN, ROW_LEN))
    dense_flops = 2 * tokens * width * width
    head_flops = 2 * tokens * ROW_LEN * ROW_LEN * HEADS

    normed_self, q_self, k_self, v_self, probs_self, attn_self, after_self, normed_cross, q_cross, _ = row_call(
        self_forward_kernel,
        "self_forward",
        (inputs,),
        (seg_target, g_self, g_cross, wq_self, wk_self, wv_self, wo_self, wq_cross),
        [flat, flat, flat, flat, probs, flat, wide, flat, flat],
        5 * dense_flops + 2 * head_flops,
        "rffffffff",
    )
    my_hits = lax.dynamic_slice_in_dim(block_hits, layer_at * rows, rows, 0)
    pair_hits = jnp.stack(
        [lax.dynamic_index_in_dim(my_hits, layer_at ^ flip, 1, keepdims=False) for flip in (0, 1)]
    )
    memory, k_cross, v_cross, probs_cross, attn_cross, after_cross, normed_feed, _ = run(
        cross_forward_kernel,
        "cross_forward",
        (rows,),
        [
            encoder_out, near_half, far_memory, q_cross, after_self, seg_target, seg_source, g_feed,
            wk_cross, wv_cross, wo_cross,
        ],
        [pl.BlockSpec((1, ROW_LEN, width), lambda at, place, hits: (0, place[0] * rows + at, 0))]
        + [by_row(array) for array in (near_half, far_memory, q_cross, after_self)]
        + [whole(array) for array in (seg_target, seg_source, g_feed, wk_cross, wv_cross, wo_cross)],
        [flat, flat, flat, probs, flat, wide, flat],
        [by_row(out) for out in (flat, flat, flat, probs, flat, wide, flat)],
        3 * dense_flops + 2 * head_flops,
        prefetch=(place, pair_hits),
    )

    chunks = dp_size if dp_size == HEADS and layer_size == 4 else 0
    hidden = feed_up.shape[1]
    share = hidden // 4
    anywhere = pl.BlockSpec(memory_space=pl.ANY)
    length = width // HEADS
    if chunks:
        weight_outs = [shape_of((2, chunks, 2 * length, width))] * 2
        weight_specs = [anywhere] * 2
    else:
        weight_outs = [shape_of((4, width, width))] * 2
        weight_specs = [whole(out) for out in weight_outs]

    def held(outs, sems):
        if not chunks:
            return []
        return [pltpu.VMEM((2,) + outs[0].shape, LOW), pltpu.SemaphoreType.DMA(sems)]

    if chunks:
        piece_rows = length + REST + UNITS // 4
        feed_outs = [shape_of((dp_size // 2, 2, piece_rows, width))] * 2
        feed_specs = [anywhere] * 2
        feed_held = [
            pltpu.VMEM((2, 2, dp_size // 2, piece_rows, width), LOW),
            pltpu.SemaphoreType.DMA((2, 2, 2)),
        ]
    else:
        feed_outs = [shape_of((width, hidden // 2)), shape_of((hidden // 2, width))]
        feed_specs = [whole(out) for out in feed_outs]
        feed_held = []

    normed_other, grad_other = across(normed_feed, 1), across(out_grad, 1)
    steps = tokens // FEED_TOKENS

    def own_block():
        return pl.BlockSpec((FEED_TOKENS, width), lambda at, *_: (jnp.clip(at, 0, steps - 1), 0))

    def other_block():
        return pl.BlockSpec((FEED_TOKENS, width), lambda at, *_: (jnp.clip(at - steps, 0, steps - 1), 0))

    down_halves = feed_down.reshape(hidden // UNITS, 2, UNITS // 2, width)
    acc, back_feed, acc_send, back_send, *feed_grads, _ = run(
        functools.partial(feed_kernel, chunks),
        "feed",
        (2 * steps + 1,),
        [normed_feed, normed_other, out_grad, grad_other, up_half, down_halves, after_cross],
        [own_block(), anywhere, own_block(), anywhere, whole(up_half), anywhere, own_block()],
        [wide, wide, flat, flat] + feed_outs,
        [own_block(), own_block(), other_block(), other_block()] + feed_specs,
        12 * tokens * width * hidden,
        scratch=[pltpu.VMEM((2 * tokens, width), LOW)] * 2
        + [pltpu.VMEM((2 * tokens, hidden // 2), LOW)] * 2
        + [pltpu.VMEM((hidden // 2, width), LOW), pltpu.SemaphoreType.DMA((hidden // UNITS + 2,))]
        + feed_held,
        prefetch=(place,),
    )
    layer_out = added([acc, across(acc_send, 1)])

    line_groups = [
        [(z_at * 2 + y_at) * layer_size + at for z_at in range(dp_size // 2)]
        for y_at in range(2)
        for at in range(layer_size)
    ]
    z_at = dp_at // 2

    def from_core(grads):
        keep, send = grads
        return [part.reshape((2, 4, 2) + part.shape[2:]) for part in (keep, across(send, 1))]

    def plane_arrived(sends):
        return [across(sent, 2 * x_flip, y_flip) for sent, (x_flip, y_flip) in zip(sends, PLANE)]

    def exchange(operand):
        return lax.all_to_all(operand, axes, 0, 0, axis_index_groups=line_groups, tiled=True)

    cross_in, dq_cross, dk_cross, dv_cross, memory_grad, grad_after_self, tick = row_call(
        cross_backward_kernel,
        "cross_backward",
        (back_feed, across(back_send, 1), after_cross, out_grad, after_self, q_cross, k_cross, v_cross, probs_cross),
        (g_feed, g_cross, wq_cross, wk_cross, wv_cross, wo_cross),
        [flat, flat, flat, flat, flat, wide],
        4 * dense_flops + 4 * head_flops,
        "rrrfrrfrrrrffff",
    )
    if chunks:
        feed_parts = [feed_grads[0], across(feed_grads[1], 0, 1)]
    moved = [normed_self, attn_self, normed_cross, memory, attn_cross]
    moved += [dq_cross, dk_cross, dv_cross, cross_in]
    dq_self, dk_self, dv_self, *weight_grads, tick = run(
        functools.partial(self_backward_kernel, chunks),
        "self_backward",
        (rows,),
        [grad_after_self, q_self, k_self, v_self, probs_self, wo_self] + moved,
        [by_row(array) for array in (grad_after_self, q_self, k_self, v_self, probs_self)]
        + [whole(wo_self)]
        + [anywhere] * len(moved),
        [flat] * 3 + weight_outs,
        [by_row(flat)] * 3 + weight_specs,
        LIGHT * dense_flops,
        scratch=[
            pltpu.VMEM((2, tokens, width), LOW),
            pltpu.VMEM((4, tokens, width), LOW),
            pltpu.VMEM((3, tokens, width), LOW),
            pltpu.VMEM((4, tokens, width), LOW),
            pltpu.SemaphoreType.DMA((len(moved),)),
        ]
        + held(weight_outs, (2, 4)),
        prefetch=(place,),
        after=[tick],
    )
    from_chip = across(memory_grad, 2)
    waits = [tick]
    if chunks:
        feed_operand = added(feed_parts, tick)
        tick = pause(25e9, [feed_operand, tick])
        feed_line = exchange(feed_operand)
        parts = from_core(weight_grads)
        weight_sends = [added([part[x_to, :, y_to] for part in parts], tick) for x_to, y_to in PLANE]
        weight_plane = plane_arrived(weight_sends)
        waits = [tick] + weight_sends
    input_grad, tick = row_call(
        input_grad_kernel,
        "input_grad",
        (dq_self, dk_self, dv_self, inputs, grad_after_self),
        (wq_self, wk_self, wv_self, g_self),
        [flat],
        LIGHT * dense_flops,
        "rrrfffrfr",
        after=waits,
    )
    waits = [tick, layer_out]

    arrived = [memory_grad, across(memory_grad, 1), from_chip, across(from_chip, 1)]
    own_hits = lax.dynamic_slice_in_dim(block_hits, layer_at, 1, 1)[:, 0]
    encoder_shape = shape_of(encoder_out.shape, FULL)
    encoder_grad, tick = run(
        encoder_grad_kernel,
        "encoder_grad",
        (4,),
        arrived,
        [whole(array) for array in arrived],
        [encoder_shape],
        [pl.BlockSpec((1, tokens, width), lambda at, place, hits: (0, place[0] ^ at, 0))],
        LIGHT * encoder_out.size,
        prefetch=(place, own_hits),
        after=waits,
    )

    if chunks:
        feed_chip = added([feed_line[at] for at in range(dp_size // 2)], tick)
        tick = pause(0, [feed_chip])
        weight_operand = added([part[0, :, 0] for part in parts] + weight_plane, tick)
        weight_line = exchange(weight_operand)
        feed_chip = added([feed_chip, across(feed_chip, 2)[::-1]], tick)
        feed_other = across(feed_chip, 1)
        feed_pieces = [feed_chip[0], feed_other[0], feed_chip[1], feed_other[1]]

        def gathered(piece):
            from_x = across(piece, 2)
            return [piece, across(piece, 1), from_x, across(from_x, 1)]

        def final_call(body, name, pieces, chunk_weights, gains, outs, scratch):
            ins = pieces + chunk_weights + gains
            outs = outs + [shape_of((1, 1, length), FULL)] * len(gains)
            return run(
                body,
                name,
                (1,),
                ins,
                [whole(array) for array in pieces]
                + [
                    pl.BlockSpec((length, array.shape[1]), lambda at, place: (place[1], 0))
                    for array in chunk_weights
                ]
                + [whole(gain) for gain in gains],
                outs,
                [whole(out) for out in outs],
                LIGHT * length * width * width,
                scratch=scratch,
                prefetch=(place,),
                after=list(waits),
            )

        waits = [weight_operand]
        *feed_finals, tick = final_call(
            feed_final_kernel,
            "feed_final",
            feed_pieces,
            [feed_up],
            [gain_feed],
            [shape_of((length, hidden), FULL), shape_of((hidden // chunks, width), FULL)],
            [pltpu.VMEM((2, length, hidden // 2), LOW)],
        )
        waits = []
        weight_piece = added([weight_line[at] for at in range(dp_size // 2)], tick)
        *finals, _ = final_call(
            weight_final_kernel,
            "weight_final",
            gathered(weight_piece),
            [wq_self, wk_self, wv_self, wq_cross],
            [gain_self, gain_cross],
            [shape_of((length, width), FULL)] * 8,
            [pltpu.VMEM((4, length, width), LOW)] * 2,
        )
        weight_grads = finals[:8] + feed_finals[:2]
        gain_grads = [value.reshape(length) for value in finals[8:] + feed_finals[2:]]
    else:
        back_order = order_matrix(width, True)

        def total(grad):
            part = lax.psum_scatter(grad.astype(FULL), "dp", scatter_dimension=0, tiled=True)
            return lax.psum(part.astype(LOW), "layer").astype(FULL)

        def natural(grads):
            back = [nn(grads[at], back_order).astype(LOW) for at in range(3)]
            return [total(grad) for grad in back + [nn(back_order.T, grads[3]).astype(LOW)]]

        grads_cross, grads_self = (natural(grads) for grads in weight_grads)
        core = layer_at % 2
        up_shape, down_shape = (width, -1, 2, UNITS // 2), (-1, 2, UNITS // 2, width)
        up_part = feed_grads[0].reshape(width, -1, 1, UNITS // 2)
        down_part = feed_grads[1].reshape(-1, 1, UNITS // 2, width)
        up_all = jnp.zeros(feed_up.shape, LOW).reshape(up_shape)
        down_all = jnp.zeros(feed_down.shape, LOW).reshape(down_shape)
        up_all = lax.dynamic_update_slice_in_dim(up_all, up_part, core, 2).reshape(feed_up.shape)
        down_all = lax.dynamic_update_slice_in_dim(down_all, down_part, core, 1).reshape(feed_down.shape)
        weight_grads = grads_self + grads_cross + [total(up_all), total(down_all)]
        length = width // dp_size

        def my_rows(array):
            return lax.dynamic_slice_in_dim(array, dp_at * length, length, 0).astype(FULL)

        def gain_total(pairs, gain):
            sums = sum(jnp.sum(my_rows(weight) * grad, axis=1) for weight, grad in pairs)
            return sums / my_rows(gain)

        gain_grads = [
            gain_total(zip((query_self, key_self, value_self), grads_self), gain_self),
            gain_total([(query_cross, grads_cross[0])], gain_cross),
            gain_total([(feed_up, weight_grads[8])], gain_feed),
        ]
    return (layer_out, input_grad, encoder_grad, *weight_grads, *gain_grads)


def solution(mesh):
    in_specs = (
        P(("dp", "layer"), None),
        P("layer", "dp", None),
        *[P()] * 13,
        P(("dp", "layer"), None),
        P(("dp", "layer"), None),
        P("dp"),
        P(),
        P(("dp", "layer"), None),
    )
    out_specs = (
        P(("dp", "layer"), None),
        P(("dp", "layer"), None),
        P("layer", "dp", None),
        *[P("dp", None)] * 10,
        *[P("dp")] * 3,
    )
    body = functools.partial(on_device, mesh.shape["layer"], mesh.shape["dp"])
    return jax.shard_map(
        body, mesh=mesh, in_specs=in_specs, out_specs=out_specs, check_vma=False
    )
```

```python
import functools
import math

import jax
import jax.numpy as jnp
from jax import lax
from jax.experimental import pallas as pl
from jax.experimental.pallas import tpu as pltpu
from jax.sharding import PartitionSpec as P

HEADS = 8
HEAD = 80
MAIN = 64
REST = 16
ROW_LEN = 256
BLOCK = 256
FEED_TOKENS = 256
UNITS = 384
SCALE = 1.0 / math.sqrt(HEAD)
LOW = jnp.bfloat16
FULL = jnp.float32
VMEM_BYTES = 56 * 1024 * 1024
WEIGHT = 1.0
LIGHT = 0.05


def dot(left, right, left_dim, right_dim):
    return lax.dot_general(
        left, right, (((left_dim,), (right_dim,)), ((), ())), preferred_element_type=FULL
    )


def nn(left, right):
    return dot(left, right, 1, 0)


def nt(left, right):
    return dot(left, right, 1, 1)


def tn(left, right):
    return dot(left, right, 0, 0)


def norm_parts(value):
    centred = value - jnp.mean(value, axis=-1, keepdims=True)
    inverse = lax.rsqrt(jnp.mean(centred * centred, axis=-1, keepdims=True) + 1e-05)
    return (centred * inverse, inverse)


def norm_forward(value, gain):
    return (norm_parts(value)[0] * gain).astype(LOW)


def norm_backward(grad, value, gain):
    normed, inverse = norm_parts(value)
    scaled = grad * gain
    inner = (
        scaled
        - jnp.mean(scaled, axis=-1, keepdims=True)
        - normed * jnp.mean(scaled * normed, axis=-1, keepdims=True)
    )
    return inner * inverse


def source_column(position):
    rest = position - HEADS * MAIN
    return jnp.where(
        rest < 0,
        HEAD * (position // MAIN) + position % MAIN,
        HEAD * (rest // REST) + MAIN + rest % REST,
    )


def ones_where_equal(sources, size, source_axis):
    shape = [size, size]
    shape[source_axis] = sources.shape[source_axis]
    index = lax.broadcasted_iota(jnp.int32, tuple(shape), 1 - source_axis)
    return (index == sources).astype(FULL).astype(LOW)


def order_matrix(width, transposed):
    axis = 1 - int(transposed)
    shape = (1, width) if axis else (width, 1)
    return ones_where_equal(source_column(lax.broadcasted_iota(jnp.int32, shape, axis)), width, axis)


def head_groups(array, head):
    pair = head // 2
    return jnp.concatenate(
        [array[:, 2 * MAIN * pair : 2 * MAIN * (pair + 1)], array[:, HEADS * MAIN :]], axis=1
    )


def head_mask(head):
    lane = lax.broadcasted_iota(jnp.int32, (1, 2 * MAIN + HEADS * REST), 1)
    rest = lane - 2 * MAIN
    owner = jnp.where(rest < 0, 2 * (head // 2) + lane // MAIN, rest // REST)
    return (owner == head).astype(FULL).astype(LOW)


def same_segment(key_seg, query_seg):
    shape = (16, key_seg.shape[1])
    number = lax.broadcasted_iota(jnp.int32, shape, 0)
    key_hot = (number == key_seg).astype(FULL).astype(LOW)
    query_hot = (number == query_seg).astype(FULL).astype(LOW)
    return tn(key_hot, query_hot)


def merge_pairs(parts):
    mains = [part[:, : 2 * MAIN] for part in parts]
    rests = [part[:, 2 * MAIN :] for part in parts]
    while len(rests) > 1:
        rests = [rests[i] + rests[i + 1] for i in range(0, len(rests), 2)]
    return jnp.concatenate(mains + rests, axis=1)


def attend(queries, keys, values, bias, probs_ref):
    parts = []
    for pair in range(HEADS // 2):
        pair_probs, pair_values = [], []
        for head in (2 * pair, 2 * pair + 1):
            mask = head_mask(head)
            scores = nt(head_groups(keys, head), head_groups(queries, head) * mask) * SCALE + bias
            raised = jnp.exp(scores - jnp.max(scores, axis=0, keepdims=True))
            probs = (raised * (1.0 / jnp.sum(raised, axis=0, keepdims=True))).astype(LOW)
            probs_ref[0, head] = probs
            pair_probs.append(probs)
            pair_values.append(head_groups(values, head) * mask)
        parts.append(
            tn(jnp.concatenate(pair_probs, axis=0), jnp.concatenate(pair_values, axis=0))
        )
    return merge_pairs(parts).astype(LOW)


def attend_back(grad, queries, keys, values, probs_ref):
    query_parts, key_parts, value_parts = [], [], []
    for pair in range(HEADS // 2):
        pair_probs, pair_slopes, pair_grads, pair_queries, pair_keys = [], [], [], [], []
        for head in (2 * pair, 2 * pair + 1):
            mask = head_mask(head)
            grad_head = head_groups(grad, head) * mask
            probs = probs_ref[0, head]
            wide = probs.astype(FULL)
            prob_grad = nt(head_groups(values, head), grad_head)
            delta = jnp.sum(prob_grad * wide, axis=0, keepdims=True)
            pair_probs.append(probs)
            pair_slopes.append((wide * (prob_grad - delta)).astype(LOW))
            pair_grads.append(grad_head)
            pair_queries.append(head_groups(queries, head) * mask)
            pair_keys.append(head_groups(keys, head) * mask)
        query_parts.append(
            tn(jnp.concatenate(pair_slopes, axis=0), jnp.concatenate(pair_keys, axis=0))
        )
        key_parts.append(
            nn(jnp.concatenate(pair_slopes, axis=1), jnp.concatenate(pair_queries, axis=0))
        )
        value_parts.append(
            nn(jnp.concatenate(pair_probs, axis=1), jnp.concatenate(pair_grads, axis=0))
        )
    return (
        (merge_pairs(query_parts) * SCALE).astype(LOW),
        (merge_pairs(key_parts) * SCALE).astype(LOW),
        merge_pairs(value_parts).astype(LOW),
    )


PLANE = ((1, 1), (1, 0), (0, 1))


def pick_matrix(core, transposed):
    axis = 1 - int(transposed)
    taken = lax.broadcasted_iota(jnp.int32, (1, UNITS) if axis else (UNITS, 1), axis)
    half = UNITS // 2
    return ones_where_equal(UNITS * (taken // half) + half * core + taken % half, 2 * UNITS, axis)


def order_kernel(place_ref, *refs):
    sources, targets, refs = refs[:9], refs[9:18], refs[18:]
    froms, tos, refs = (*refs[:2], refs[2]), (*refs[3:5], refs[5]), refs[6:]
    in_sems, out_sems = refs
    core = lax.bitwise_and(place_ref[0], 1)
    columns_in, rows_in, up_in = froms
    columns_out, rows_out, up_out = tos
    ins = [columns_in.at[at] for at in range(6)] + [rows_in.at[at] for at in range(2)] + [up_in]
    outs = [columns_out.at[at] for at in range(6)] + [rows_out.at[at] for at in range(2)] + [up_out]
    fetches = [pltpu.make_async_copy(*pair, in_sems.at[at]) for at, pair in enumerate(zip(sources, ins))]
    stores = [pltpu.make_async_copy(*pair, out_sems.at[at]) for at, pair in enumerate(zip(outs, targets))]
    for fetch in fetches:
        fetch.start()
    order = order_matrix(columns_in.shape[1], False)
    for at in range(6):
        fetches[at].wait()
        columns_out[at] = nn(columns_in[at], order).astype(LOW)
        stores[at].start()
    for at in range(2):
        fetches[6 + at].wait()
        for head in range(HEADS):
            base = HEAD * head
            rows_out[at, MAIN * head : MAIN * (head + 1)] = rows_in[at, base : base + MAIN]
            rest = HEADS * MAIN + REST * head
            rows_out[at, rest : rest + REST] = rows_in[at, base + MAIN : base + HEAD]
        stores[6 + at].start()
    pick = pick_matrix(core, False)
    fetches[8].wait()
    for pair in range(up_in.shape[1] // (2 * UNITS)):
        columns = slice(2 * UNITS * pair, 2 * UNITS * (pair + 1))
        up_out[:, UNITS * pair : UNITS * (pair + 1)] = nn(up_in[:, columns], pick).astype(LOW)
    stores[8].start()
    for store in stores:
        store.wait()


def self_forward_kernel(
    x_ref, seg_ref, gain_ref, next_gain_ref, wq_ref, wk_ref, wv_ref, wo_ref, next_wq_ref,
    normed_ref, q_ref, k_ref, v_ref, probs_ref, attn_ref, after_ref, next_normed_ref, next_q_ref,
):
    value = x_ref[...].astype(FULL)
    normed = norm_forward(value, gain_ref[...])
    normed_ref[...] = normed
    queries = nn(normed, wq_ref[...]).astype(LOW)
    keys = nn(normed, wk_ref[...]).astype(LOW)
    values = nn(normed, wv_ref[...]).astype(LOW)
    q_ref[...], k_ref[...], v_ref[...] = queries, keys, values
    seg = seg_ref[pl.ds(pl.program_id(0), 1), :]
    key_at = lax.broadcasted_iota(jnp.int32, (ROW_LEN, ROW_LEN), 0)
    query_at = lax.broadcasted_iota(jnp.int32, (ROW_LEN, ROW_LEN), 1)
    allowed = (same_segment(seg, seg) > 0.5) & (key_at <= query_at)
    attn = attend(queries, keys, values, jnp.where(allowed, 0.0, -1e9), probs_ref)
    attn_ref[...] = attn
    after = value + nn(attn, wo_ref[...])
    after_ref[...] = after
    next_normed = norm_forward(after, next_gain_ref[...])
    next_normed_ref[...] = next_normed
    next_q_ref[...] = nn(next_normed, next_wq_ref[...]).astype(LOW)


def cross_forward_kernel(
    place_ref, hits_ref, own_ref, near_ref, far_ref, q_ref, after_ref, seg_target_ref, seg_source_ref, gain_ref,
    wk_ref, wv_ref, wo_ref, memory_ref, k_ref, v_ref, probs_ref, attn_ref, next_after_ref, next_normed_ref,
):
    step = pl.program_id(0)
    row = place_ref[0] * pl.num_programs(0) + step
    own = 0.5 * hits_ref[row, place_ref[0]] * own_ref[0].astype(FULL)
    near = 0.5 * hits_ref[row, lax.bitwise_xor(place_ref[0], 1)] * near_ref[0].astype(FULL)
    memory = (own + near + far_ref[...].astype(FULL)).astype(LOW)
    memory_ref[...] = memory
    keys = nn(memory, wk_ref[...]).astype(LOW)
    values = nn(memory, wv_ref[...]).astype(LOW)
    k_ref[...], v_ref[...] = keys, values
    row = pl.ds(pl.program_id(0), 1)
    allowed = same_segment(seg_source_ref[row, :], seg_target_ref[row, :]) > 0.5
    attn = attend(q_ref[...], keys, values, jnp.where(allowed, 0.0, -1e9), probs_ref)
    attn_ref[...] = attn
    after = after_ref[...] + nn(attn, wo_ref[...])
    next_after_ref[...] = after
    next_normed_ref[...] = norm_forward(after, gain_ref[...])


def store_piece(place_ref, held_ref, quarter, chunk, rows, columns, piece):
    owner = lax.bitwise_xor(place_ref[0], quarter)
    dp_at = lax.bitwise_xor(chunk, lax.bitwise_and(place_ref[1], 1))
    held_ref[
        lax.bitwise_and(owner, 1), lax.shift_right_logical(owner, 1), dp_at, rows, columns
    ] = piece


def store_feed(place_ref, held_ref, x_of, chunk, rows, columns, piece):
    x_at = lax.bitwise_xor(x_of, lax.shift_right_logical(place_ref[0], 1))
    y_at = lax.bitwise_xor(lax.bitwise_and(chunk, 1), lax.bitwise_and(place_ref[1], 1))
    held_ref[x_at, y_at, lax.shift_right_logical(chunk, 1), rows, columns] = piece


def hand_out(place_ref, held_ref, targets, sem, quarter, region):
    owner = lax.bitwise_xor(place_ref[0], quarter)
    x_at = lax.shift_right_logical(owner, 1)
    for half in range(2):

        @pl.when(lax.bitwise_and(owner, 1) == half)
        def _():
            pltpu.make_async_copy(
                held_ref.at[(half, x_at) + region], targets[half].at[(x_at,) + region], sem
            ).start()


def hand_out_done(held_ref, targets, sem, region):
    pltpu.make_async_copy(held_ref.at[(0, 0) + region], targets[0].at[(0,) + region], sem).wait()


def feed_kernel(chunks, place_ref, *refs):
    normed_refs, grad_refs, (up_ref, down_all, after_ref), refs = refs[:2], refs[2:4], refs[4:7], refs[7:]
    (acc_out, back_out, acc_send, back_send), targets, refs = refs[:4], refs[4:6], refs[6:]
    normed_ref, grad_ref, hidden_ref, pre_ref, down_ref, down_sems, *held = refs
    step, steps = pl.program_id(0), pl.num_programs(0)
    size, width = after_ref.shape
    units = up_ref.shape[1]

    rows = pl.ds(pl.multiple_of(step * size, size), size)
    tokens = normed_refs[1].shape[0]
    others = [
        pltpu.make_async_copy(source, target.at[tokens:], down_sems.at[down_all.shape[0] + at])
        for at, (source, target) in enumerate(((normed_refs[1], normed_ref), (grad_refs[1], grad_ref)))
    ]

    @pl.when(step == 0)
    def _():
        half, core = UNITS // 2, lax.bitwise_and(place_ref[0], 1)
        fetches = [
            pltpu.make_async_copy(
                down_all.at[at, core], down_ref.at[half * at : half * (at + 1)], down_sems.at[at]
            )
            for at in range(down_all.shape[0])
        ]
        for fetch in fetches + others:
            fetch.start()
        for fetch in fetches:
            fetch.wait()

    def tokens_step(normed, grad):
        pre = nn(normed, up_ref[...])
        hidden_grad = nt(grad, down_ref[...])
        square = pre * pre
        slope = math.sqrt(2.0 / math.pi)
        bend = jnp.tanh(pre * (slope + slope * 0.044715 * square))
        half = 0.5 + 0.5 * bend
        hidden = (pre * half).astype(LOW)
        rate = half + pre * half * (1.0 - bend) * (slope + slope * 3 * 0.044715 * square)
        pre_grad = (hidden_grad * rate).astype(LOW)
        hidden_ref[rows, :] = hidden
        pre_ref[rows, :] = pre_grad
        return nn(hidden, down_ref[...]), nt(pre_grad, up_ref[...])

    @pl.when(step < steps // 2)
    def _():
        normed_ref[rows, :] = normed_refs[0][...]
        grad_ref[rows, :] = grad_refs[0][...]
        acc, back = tokens_step(normed_refs[0][...], grad_refs[0][...])
        acc_out[...] = after_ref[...] + acc
        back_out[...] = back

    @pl.when(step == steps // 2)
    def _():
        for fetch in others:
            fetch.wait()

    @pl.when((step >= steps // 2) & (step < steps - 1))
    def _():
        acc, back = tokens_step(normed_ref[rows, :], grad_ref[rows, :])
        acc_send[...] = acc.astype(LOW)
        back_send[...] = back.astype(LOW)

    @pl.when(step == steps - 1)
    def _():
        if not chunks:
            targets[0][...] = tn(normed_ref[...], pre_ref[...]).astype(LOW)
            targets[1][...] = tn(hidden_ref[...], grad_ref[...]).astype(LOW)
            return
        held_ref, held_sems = held
        length = width // chunks
        part = UNITS // 4
        share = units // 2
        fold = share - width
        top = length + REST

        def copies(at, rows):
            return [
                pltpu.make_async_copy(
                    held_ref.at[x_at, y_at, :, rows], targets[y_at].at[:, x_at, rows], held_sems.at[at, y_at, x_at]
                )
                for y_at in (1, 0)
                for x_at in range(2)
            ]

        ups, downs = copies(0, slice(0, top)), copies(1, slice(top, held_ref.shape[3]))
        for start in range(0, units, BLOCK):
            x_of, first = start // share, start % share
            up_grad = tn(normed_ref[...], pre_ref[:, start : start + BLOCK]).astype(LOW)
            for chunk in range(chunks):
                piece = up_grad[length * chunk : length * (chunk + 1)]
                inside = min(width - first, BLOCK)
                store_feed(
                    place_ref, held_ref, x_of, chunk,
                    slice(0, length), slice(first, first + inside), piece[:, :inside],
                )
                if inside < BLOCK:
                    for at in range(width // fold):
                        rows = REST * at
                        store_feed(
                            place_ref, held_ref, x_of, chunk,
                            slice(length, top), slice(fold * at, fold * (at + 1)),
                            piece[rows : rows + REST, inside:],
                        )
        for copy in ups:
            copy.start()
        for start in range(0, units, BLOCK):
            down_grad = tn(hidden_ref[:, start : start + BLOCK], grad_ref[...]).astype(LOW)
            for row in range(start, start + BLOCK, 32):
                chunk, inside = row // (2 * part), row % (2 * part)
                base = top + inside % part
                store_feed(
                    place_ref, held_ref, inside // part, chunk,
                    slice(base, base + 32), slice(0, width), down_grad[row - start : row - start + 32],
                )
        for copy in downs:
            copy.start()
        for copy in ups + downs:
            copy.wait()


def cross_backward_kernel(
    back_ref, back_other_ref, after_cross_ref, gain_feed_ref, grad_ref, after_self_ref, gain_cross_ref,
    q_ref, k_ref, v_ref, probs_ref, wq_ref, wk_ref, wv_ref, wo_ref,
    in_ref, dq_ref, dk_ref, dv_ref, memory_ref, grad_self_ref,
):
    grad = grad_ref[...].astype(FULL) + norm_backward(
        back_ref[...] + back_other_ref[...].astype(FULL), after_cross_ref[...], gain_feed_ref[...]
    )
    branch = grad.astype(LOW)
    in_ref[...] = branch
    query_grad, key_grad, value_grad = attend_back(
        nt(branch, wo_ref[...]).astype(LOW), q_ref[...], k_ref[...], v_ref[...], probs_ref
    )
    dq_ref[...], dk_ref[...], dv_ref[...] = query_grad, key_grad, value_grad
    memory_ref[...] = (nt(key_grad, wk_ref[...]) + nt(value_grad, wv_ref[...])).astype(LOW)
    grad_self_ref[...] = grad + norm_backward(
        nt(query_grad, wq_ref[...]), after_self_ref[...], gain_cross_ref[...]
    )


def input_grad_kernel(dq_ref, dk_ref, dv_ref, wq_ref, wk_ref, wv_ref, x_ref, gain_ref, grad_ref, out_ref):
    inner = (
        nt(dq_ref[...], wq_ref[...]) + nt(dk_ref[...], wk_ref[...]) + nt(dv_ref[...], wv_ref[...])
    )
    back = norm_backward(inner, x_ref[...].astype(FULL), gain_ref[...])
    out_ref[...] = (grad_ref[...] + back).astype(LOW)


def weight_product(chunks, place_ref, left, right, weight, base, target, held_ref):
    width = right.shape[1]
    for start in range(0, width, BLOCK):
        columns = slice(start, min(start + BLOCK, width))
        grad = tn(left[...], right[:, columns]).astype(LOW)
        if not chunks:
            target[weight, :, columns] = grad
            continue
        length = width // chunks
        for chunk in range(chunks):
            piece = grad[length * chunk : length * (chunk + 1)]
            if weight == 3:
                rest = HEADS * MAIN + REST * chunk
                piece = jnp.concatenate(
                    [grad[MAIN * chunk : MAIN * (chunk + 1)], grad[rest : rest + REST]], axis=0
                )
            store_piece(place_ref, held_ref, weight, chunk, slice(base, base + length), columns, piece)


def self_backward_kernel(
    chunks, place_ref, grad_ref, q_ref, k_ref, v_ref, probs_ref, wo_ref, *refs
):
    sources, (dq_ref, dk_ref, dv_ref, *refs) = refs[:9], refs[9:]
    targets, (left_ref, right_ref, cross_left, cross_right, sems, *held) = refs[:2], refs[2:]
    held_ref, held_sems = held if chunks else (None, None)
    step, steps = pl.program_id(0), pl.num_programs(0)
    places = [left_ref.at[0], left_ref.at[1]]
    places += [cross_left.at[at] for at in range(3)] + [cross_right.at[at] for at in range(4)]
    copies = [
        pltpu.make_async_copy(source, place, sems.at[at])
        for at, (source, place) in enumerate(zip(sources, places))
    ]
    needs = ((2, 5), (3, 6), (7,), (4, 8))

    @pl.when(step == 0)
    def _():
        for at in sum(needs, ()) + (0, 1):
            copies[at].start()

    rows = pl.ds(pl.multiple_of(step * ROW_LEN, ROW_LEN), ROW_LEN)
    branch = grad_ref[...].astype(LOW)
    grads = attend_back(
        nt(branch, wo_ref[...]).astype(LOW), q_ref[...], k_ref[...], v_ref[...], probs_ref
    )
    for at, (ref, grad) in enumerate(zip((dq_ref, dk_ref, dv_ref), grads)):
        ref[...] = grad
        right_ref[at, rows, :] = grad
    right_ref[3, rows, :] = branch
    length = dq_ref.shape[1] // HEADS
    cross_rows, self_rows = slice(0, length), slice(length, 2 * length)

    def region(part):
        return (slice(None), part)

    for weight in range(4):

        @pl.when(step == weight)
        def _():
            for at in needs[weight]:
                copies[at].wait()
            left = cross_left.at[(0, 1, 1, 2)[weight]]
            weight_product(
                chunks, place_ref, left, cross_right.at[weight], weight, cross_rows.start, targets[0], held_ref
            )
            if chunks:
                hand_out(place_ref, held_ref, targets, held_sems.at[0, weight], weight, region(cross_rows))

    @pl.when(step == steps - 1)
    def _():
        for copy in copies[:2]:
            copy.wait()
        for weight in range(4):
            left = left_ref.at[weight // 3]
            weight_product(
                chunks, place_ref, left, right_ref.at[weight], weight, self_rows.start, targets[1], held_ref
            )
            if chunks:
                hand_out(place_ref, held_ref, targets, held_sems.at[1, weight], weight, region(self_rows))
        if chunks:
            for group, part in enumerate((cross_rows, self_rows)):
                for weight in range(4):
                    hand_out_done(held_ref, targets, held_sems.at[group, weight], region(part))


def encoder_grad_kernel(place_ref, hits_ref, *refs):
    out_ref = refs[-1]
    step = pl.program_id(0)
    for turn in range(4):

        @pl.when(step == turn)
        def _():
            tokens = refs[turn].shape[0]
            rows = tokens // ROW_LEN
            owner = lax.bitwise_xor(place_ref[0], turn)
            for row in range(rows):
                here = slice(ROW_LEN * row, ROW_LEN * (row + 1))
                weight = 0.5 * hits_ref[owner * rows + row, place_ref[0]]
                out_ref[0, here, :] = weight * refs[turn][here, :].astype(FULL)


def gain_grad(place_ref, pairs, gain_ref, target):
    total = sum(
        jnp.sum(weight.astype(FULL) * grad.astype(FULL), axis=1, keepdims=True) for weight, grad in pairs
    )
    length = total.shape[0]
    width = gain_ref.shape[0]
    turned = jnp.broadcast_to(total, (length, 128)).T
    gains = jnp.broadcast_to(gain_ref[...].reshape(1, width), (8, width))
    mine = pltpu.roll(gains, lax.rem(width - length * place_ref[1], width), 1)
    target[0] = turned[:1] / mine[:1, :length]


def feed_final_kernel(place_ref, *refs):
    sources, (up_ref, gain_ref, up_out, down_out, gain_out, half_ref) = refs[:4], refs[4:]
    length = up_out.shape[0]
    part = down_out.shape[0] // 4
    share = up_out.shape[1] // 4
    width = down_out.shape[1]
    fold = share - width
    for turn, piece in enumerate(sources):
        owner = lax.bitwise_xor(place_ref[0], turn)
        x_of, core = lax.shift_right_logical(owner, 1), lax.bitwise_and(owner, 1)
        start = pl.multiple_of(x_of * share, 128)
        half_ref[core, :, pl.ds(start, width)] = piece[:length, :]
        for at in range(width // fold):
            half_ref[
                core, REST * at : REST * (at + 1), pl.ds(pl.multiple_of(start + width, 128), fold)
            ] = piece[length : length + REST, fold * at : fold * (at + 1)]
        rows = pl.ds(pl.multiple_of((2 * core + x_of) * part, 32), part)
        down_out[rows, :] = piece[length + REST :, :].astype(FULL)
    picks = [pick_matrix(core, True) for core in range(2)]
    for pair in range(up_out.shape[1] // (2 * UNITS)):
        columns = slice(UNITS * pair, UNITS * (pair + 1))
        up_out[:, 2 * UNITS * pair : 2 * UNITS * (pair + 1)] = nn(
            half_ref[0, :, columns], picks[0]
        ) + nn(half_ref[1, :, columns], picks[1])
    gain_grad(place_ref, [(up_ref[...], up_out[...])], gain_ref, gain_out)


def weight_final_kernel(place_ref, *refs):
    sources, weights, gains, targets = refs[:4], refs[4:8], refs[8:10], refs[10:-2]
    cross_ref, self_ref = refs[-2:]
    length = cross_ref.shape[1]
    for turn, piece in enumerate(sources):
        owner = lax.bitwise_xor(place_ref[0], turn)
        cross_ref[owner] = piece[:length, :]
        self_ref[owner] = piece[length:, :]
    order = order_matrix(cross_ref.shape[2], True)
    for at in range(3):
        targets[at][...] = nn(self_ref[at], order)
        targets[4 + at][...] = nn(cross_ref[at], order)
    targets[3][...] = self_ref[3].astype(FULL)
    targets[7][...] = cross_ref[3].astype(FULL)
    gain_grad(place_ref, [(weights[at][...], self_ref[at]) for at in range(3)], gains[0], targets[8])
    gain_grad(place_ref, [(weights[3][...], cross_ref[0])], gains[1], targets[9])


def whole(array):
    return pl.BlockSpec(array.shape, lambda *at: (0,) * array.ndim)


def by_row(array, first=0):
    if array.ndim == 2:
        return pl.BlockSpec((ROW_LEN, array.shape[1]), lambda at, *_: (at + first, 0))
    return pl.BlockSpec(
        (1,) + array.shape[1:], lambda at, *_: (at + first,) + (0,) * (array.ndim - 1)
    )


def run(
    body, name, grid, ins, in_specs, outs, out_specs, flops, scratch=(), prefetch=(), after=(), into=()
):
    after = list(into) + list(after)
    outs = list(outs) + [shape_of((1, 1), FULL)]
    out_specs = list(out_specs) + [pl.BlockSpec(memory_space=pltpu.SMEM)]
    moved = sum(array.size * array.dtype.itemsize for array in list(ins) + list(outs))
    first, last = len(prefetch) + len(ins), len(prefetch) + len(ins) + len(after)

    tick_at = last + len(outs) - 1

    def ordered_body(*refs):
        refs[tick_at][0, 0] = 0.0
        body(*refs[:first], *refs[last:tick_at], *refs[tick_at + 1 :])

    return pl.pallas_call(
        ordered_body,
        name=name,
        out_shape=outs,
        grid_spec=pltpu.PrefetchScalarGridSpec(
            num_scalar_prefetch=len(prefetch),
            grid=grid,
            in_specs=list(in_specs) + [pl.BlockSpec(memory_space=pl.ANY)] * len(after),
            out_specs=out_specs,
            scratch_shapes=scratch,
        ),
        input_output_aliases={first + at: at for at in range(len(into))},
        compiler_params=pltpu.CompilerParams(vmem_limit_bytes=VMEM_BYTES),
        cost_estimate=pl.CostEstimate(
            flops=int(flops * WEIGHT), bytes_accessed=int(moved * WEIGHT), transcendentals=0
        ),
    )(*prefetch, *ins, *after)


def pause(flops, after):
    return run(lambda: None, "pause", (1,), [], [], [], [], flops, after=after)[0]


def shape_of(shape, dtype=LOW):
    return jax.ShapeDtypeStruct(tuple(shape), dtype)


def row_call(body, name, rowed, fixed, outs, flops, order, after=(), part=None, into=()):
    first, last = part or (0, outs[0].shape[0] // ROW_LEN)
    ins, specs = [], []
    rowed, fixed = list(rowed), list(fixed)
    for kind in order:
        array = rowed.pop(0) if kind == "r" else fixed.pop(0)
        ins.append(array)
        specs.append(by_row(array, first) if kind == "r" else whole(array))
    return run(
        body,
        name,
        (last - first,),
        ins,
        specs,
        outs,
        [by_row(out, first) for out in outs],
        flops,
        after=after,
        into=into,
    )


def permuted(value, axes, sizes, flip):
    count = math.prod(sizes)
    return lax.ppermute(value, axes, [(at, at ^ flip) for at in range(count)])


def added(parts, tick=None):
    total = parts[0].astype(FULL)
    if tick is not None:
        total = total + tick[0, 0]
    for part in parts[1:]:
        total = total + part.astype(FULL)
    return total.astype(LOW)


def on_device(
    layer_size,
    dp_size,
    inputs,
    encoder_out,
    query_self,
    key_self,
    value_self,
    out_self,
    query_cross,
    key_cross,
    value_cross,
    out_cross,
    feed_up,
    feed_down,
    gain_self,
    gain_cross,
    gain_feed,
    seg_target,
    seg_source,
    subnet_of_row,
    chosen_layers,
    out_grad,
):
    tokens, width = inputs.shape
    rows = tokens // ROW_LEN
    layer_at = lax.axis_index("layer")
    dp_at = lax.axis_index("dp")
    place = jnp.stack([layer_at, dp_at]).astype(jnp.int32)
    axes, sizes = ("dp", "layer"), (dp_size, layer_size)

    def across(value, layer_flip, dp_flip=0):
        return permuted(value, axes, sizes, dp_flip * layer_size + layer_flip)

    picked = jnp.sum(
        (chosen_layers[:, :, None] == jnp.arange(layer_size)[None, None, :]).astype(FULL), axis=1
    )
    row_pick = (subnet_of_row[:, None] == jnp.arange(chosen_layers.shape[0])[None, :]).astype(FULL)
    block_hits = jnp.sum(row_pick[:, :, None] * picked[None], axis=1)
    own_layer = encoder_out.reshape(layer_size, rows, ROW_LEN, width)

    def own_block(flip):
        return lax.dynamic_index_in_dim(own_layer, layer_at ^ flip, 0, keepdims=False)

    def hits_of(flip, layer_flip):
        hits = lax.dynamic_slice_in_dim(block_hits, (layer_at ^ flip) * rows, rows, 0)
        hits = lax.dynamic_slice_in_dim(hits, layer_at ^ layer_flip, 1, 1)
        return 0.5 * hits[:, :, None]

    def chip_sum(flip, arrived):
        total = hits_of(flip, 0) * own_block(flip).astype(FULL)
        total = total + hits_of(flip, 1) * arrived.astype(FULL)
        return total.astype(LOW).reshape(tokens, width)

    far_half = across(own_block(3), 1)
    near_half = across(own_block(1), 1)
    far_memory = across(chip_sum(2, far_half), 2)

    weights = [query_self, key_self, value_self, query_cross, key_cross, value_cross, out_self, out_cross, feed_up]
    order_outs = [shape_of(array.shape) for array in weights[:8]]
    order_outs.append(shape_of((width, feed_up.shape[1] // 2)))
    ordered = run(
        order_kernel,
        "order_weights",
        (1,),
        weights,
        [pl.BlockSpec(memory_space=pl.ANY)] * 9,
        order_outs,
        [pl.BlockSpec(memory_space=pl.ANY)] * 9,
        12 * width**3,
        scratch=[
            pltpu.VMEM(shape, LOW)
            for columns in (feed_up.shape[1], feed_up.shape[1] // 2)
            for shape in ((6, width, width), (2, width, width), (width, columns))
        ]
        + [pltpu.SemaphoreType.DMA((9,))] * 2,
        prefetch=(place,),
    )
    wq_self, wk_self, wv_self, wq_cross, wk_cross, wv_cross, wo_self, wo_cross, up_half, _ = ordered
    g_self, g_cross, g_feed = gain_self, gain_cross, gain_feed
    flat = shape_of((tokens, width))
    wide = shape_of((tokens, width), FULL)
    probs = shape_of((rows, HEADS, ROW_LEN, ROW_LEN))
    dense_flops = 2 * tokens * width * width
    head_flops = 2 * tokens * ROW_LEN * ROW_LEN * HEADS

    normed_self, q_self, k_self, v_self, probs_self, attn_self, after_self, normed_cross, q_cross, _ = row_call(
        self_forward_kernel,
        "self_forward",
        (inputs,),
        (seg_target, g_self, g_cross, wq_self, wk_self, wv_self, wo_self, wq_cross),
        [flat, flat, flat, flat, probs, flat, wide, flat, flat],
        5 * dense_flops + 2 * head_flops,
        "rffffffff",
    )
    memory, k_cross, v_cross, probs_cross, attn_cross, after_cross, normed_feed, _ = run(
        cross_forward_kernel,
        "cross_forward",
        (rows,),
        [
            encoder_out, near_half, far_memory, q_cross, after_self, seg_target, seg_source, g_feed,
            wk_cross, wv_cross, wo_cross,
        ],
        [pl.BlockSpec((1, ROW_LEN, width), lambda at, place, hits: (0, place[0] * rows + at, 0))]
        + [by_row(array) for array in (near_half, far_memory, q_cross, after_self)]
        + [whole(array) for array in (seg_target, seg_source, g_feed, wk_cross, wv_cross, wo_cross)],
        [flat, flat, flat, probs, flat, wide, flat],
        [by_row(out) for out in (flat, flat, flat, probs, flat, wide, flat)],
        3 * dense_flops + 2 * head_flops,
        prefetch=(place, block_hits),
    )

    chunks = dp_size if dp_size == HEADS and layer_size == 4 else 0
    hidden = feed_up.shape[1]
    share = hidden // 4
    anywhere = pl.BlockSpec(memory_space=pl.ANY)
    length = width // HEADS
    if chunks:
        weight_outs = [shape_of((2, chunks, 2 * length, width))] * 2
        weight_specs = [anywhere] * 2
    else:
        weight_outs = [shape_of((4, width, width))] * 2
        weight_specs = [whole(out) for out in weight_outs]

    def held(outs, sems):
        if not chunks:
            return []
        return [pltpu.VMEM((2,) + outs[0].shape, LOW), pltpu.SemaphoreType.DMA(sems)]

    if chunks:
        piece_rows = length + REST + UNITS // 4
        feed_outs = [shape_of((dp_size // 2, 2, piece_rows, width))] * 2
        feed_specs = [anywhere] * 2
        feed_held = [
            pltpu.VMEM((2, 2, dp_size // 2, piece_rows, width), LOW),
            pltpu.SemaphoreType.DMA((2, 2, 2)),
        ]
    else:
        feed_outs = [shape_of((width, hidden // 2)), shape_of((hidden // 2, width))]
        feed_specs = [whole(out) for out in feed_outs]
        feed_held = []

    normed_other, grad_other = across(normed_feed, 1), across(out_grad, 1)
    steps = tokens // FEED_TOKENS

    def own_block():
        return pl.BlockSpec((FEED_TOKENS, width), lambda at, *_: (jnp.clip(at, 0, steps - 1), 0))

    def other_block():
        return pl.BlockSpec((FEED_TOKENS, width), lambda at, *_: (jnp.clip(at - steps, 0, steps - 1), 0))

    down_halves = feed_down.reshape(hidden // UNITS, 2, UNITS // 2, width)
    acc, back_feed, acc_send, back_send, *feed_grads, _ = run(
        functools.partial(feed_kernel, chunks),
        "feed",
        (2 * steps + 1,),
        [normed_feed, normed_other, out_grad, grad_other, up_half, down_halves, after_cross],
        [own_block(), anywhere, own_block(), anywhere, whole(up_half), anywhere, own_block()],
        [wide, wide, flat, flat] + feed_outs,
        [own_block(), own_block(), other_block(), other_block()] + feed_specs,
        12 * tokens * width * hidden,
        scratch=[pltpu.VMEM((2 * tokens, width), LOW)] * 2
        + [pltpu.VMEM((2 * tokens, hidden // 2), LOW)] * 2
        + [pltpu.VMEM((hidden // 2, width), LOW), pltpu.SemaphoreType.DMA((hidden // UNITS + 2,))]
        + feed_held,
        prefetch=(place,),
    )
    layer_out = added([acc, across(acc_send, 1)])

    line_groups = [
        [(z_at * 2 + y_at) * layer_size + at for z_at in range(dp_size // 2)]
        for y_at in range(2)
        for at in range(layer_size)
    ]
    z_at = dp_at // 2

    def from_core(grads):
        keep, send = grads
        return [part.reshape((2, 4, 2) + part.shape[2:]) for part in (keep, across(send, 1))]

    def plane_arrived(sends):
        return [across(sent, 2 * x_flip, y_flip) for sent, (x_flip, y_flip) in zip(sends, PLANE)]

    def exchange(operand):
        return lax.all_to_all(operand, axes, 0, 0, axis_index_groups=line_groups, tiled=True)

    cross_in, dq_cross, dk_cross, dv_cross, memory_grad, grad_after_self, tick = row_call(
        cross_backward_kernel,
        "cross_backward",
        (back_feed, across(back_send, 1), after_cross, out_grad, after_self, q_cross, k_cross, v_cross, probs_cross),
        (g_feed, g_cross, wq_cross, wk_cross, wv_cross, wo_cross),
        [flat, flat, flat, flat, flat, wide],
        4 * dense_flops + 4 * head_flops,
        "rrrfrrfrrrrffff",
    )
    if chunks:
        feed_parts = [feed_grads[0], across(feed_grads[1], 0, 1)]
    moved = [normed_self, attn_self, normed_cross, memory, attn_cross]
    moved += [dq_cross, dk_cross, dv_cross, cross_in]
    dq_self, dk_self, dv_self, *weight_grads, tick = run(
        functools.partial(self_backward_kernel, chunks),
        "self_backward",
        (rows,),
        [grad_after_self, q_self, k_self, v_self, probs_self, wo_self] + moved,
        [by_row(array) for array in (grad_after_self, q_self, k_self, v_self, probs_self)]
        + [whole(wo_self)]
        + [anywhere] * len(moved),
        [flat] * 3 + weight_outs,
        [by_row(flat)] * 3 + weight_specs,
        LIGHT * dense_flops,
        scratch=[
            pltpu.VMEM((2, tokens, width), LOW),
            pltpu.VMEM((4, tokens, width), LOW),
            pltpu.VMEM((3, tokens, width), LOW),
            pltpu.VMEM((4, tokens, width), LOW),
            pltpu.SemaphoreType.DMA((len(moved),)),
        ]
        + held(weight_outs, (2, 4)),
        prefetch=(place,),
        after=[tick],
    )
    from_chip = across(memory_grad, 2)
    waits = [tick]
    if chunks:
        feed_operand = added(feed_parts, tick)
        tick = pause(25e9, [feed_operand, tick])
        feed_line = exchange(feed_operand)
        parts = from_core(weight_grads)
        weight_sends = [added([part[x_to, :, y_to] for part in parts], tick) for x_to, y_to in PLANE]
        weight_plane = plane_arrived(weight_sends)
        waits = [tick] + weight_sends
    input_grad, tick = row_call(
        input_grad_kernel,
        "input_grad",
        (dq_self, dk_self, dv_self, inputs, grad_after_self),
        (wq_self, wk_self, wv_self, g_self),
        [flat],
        LIGHT * dense_flops,
        "rrrfffrfr",
        after=waits,
    )
    waits = [tick, layer_out]

    arrived = [memory_grad, across(memory_grad, 1), from_chip, across(from_chip, 1)]
    encoder_shape = shape_of(encoder_out.shape, FULL)
    encoder_grad, tick = run(
        encoder_grad_kernel,
        "encoder_grad",
        (4,),
        arrived,
        [whole(array) for array in arrived],
        [encoder_shape],
        [pl.BlockSpec((1, tokens, width), lambda at, place, hits: (0, place[0] ^ at, 0))],
        LIGHT * encoder_out.size,
        prefetch=(place, block_hits),
        after=waits,
    )

    if chunks:
        feed_chip = added([feed_line[at] for at in range(dp_size // 2)], tick)
        tick = pause(0, [feed_chip])
        weight_operand = added([part[0, :, 0] for part in parts] + weight_plane, tick)
        weight_line = exchange(weight_operand)
        feed_chip = added([feed_chip, across(feed_chip, 2)[::-1]], tick)
        feed_other = across(feed_chip, 1)
        feed_pieces = [feed_chip[0], feed_other[0], feed_chip[1], feed_other[1]]

        def gathered(piece):
            from_x = across(piece, 2)
            return [piece, across(piece, 1), from_x, across(from_x, 1)]

        def final_call(body, name, pieces, chunk_weights, gains, outs, scratch):
            ins = pieces + chunk_weights + gains
            outs = outs + [shape_of((1, 1, length), FULL)] * len(gains)
            return run(
                body,
                name,
                (1,),
                ins,
                [whole(array) for array in pieces]
                + [
                    pl.BlockSpec((length, array.shape[1]), lambda at, place: (place[1], 0))
                    for array in chunk_weights
                ]
                + [whole(gain) for gain in gains],
                outs,
                [whole(out) for out in outs],
                LIGHT * length * width * width,
                scratch=scratch,
                prefetch=(place,),
                after=list(waits),
            )

        waits = [weight_operand]
        *feed_finals, tick = final_call(
            feed_final_kernel,
            "feed_final",
            feed_pieces,
            [feed_up],
            [gain_feed],
            [shape_of((length, hidden), FULL), shape_of((hidden // chunks, width), FULL)],
            [pltpu.VMEM((2, length, hidden // 2), LOW)],
        )
        waits = []
        weight_piece = added([weight_line[at] for at in range(dp_size // 2)], tick)
        *finals, _ = final_call(
            weight_final_kernel,
            "weight_final",
            gathered(weight_piece),
            [wq_self, wk_self, wv_self, wq_cross],
            [gain_self, gain_cross],
            [shape_of((length, width), FULL)] * 8,
            [pltpu.VMEM((4, length, width), LOW)] * 2,
        )
        weight_grads = finals[:8] + feed_finals[:2]
        gain_grads = [value.reshape(length) for value in finals[8:] + feed_finals[2:]]
    else:
        back_order = order_matrix(width, True)

        def total(grad):
            part = lax.psum_scatter(grad.astype(FULL), "dp", scatter_dimension=0, tiled=True)
            return lax.psum(part.astype(LOW), "layer").astype(FULL)

        def natural(grads):
            back = [nn(grads[at], back_order).astype(LOW) for at in range(3)]
            return [total(grad) for grad in back + [nn(back_order.T, grads[3]).astype(LOW)]]

        grads_cross, grads_self = (natural(grads) for grads in weight_grads)
        core = layer_at % 2
        up_shape, down_shape = (width, -1, 2, UNITS // 2), (-1, 2, UNITS // 2, width)
        up_part = feed_grads[0].reshape(width, -1, 1, UNITS // 2)
        down_part = feed_grads[1].reshape(-1, 1, UNITS // 2, width)
        up_all = jnp.zeros(feed_up.shape, LOW).reshape(up_shape)
        down_all = jnp.zeros(feed_down.shape, LOW).reshape(down_shape)
        up_all = lax.dynamic_update_slice_in_dim(up_all, up_part, core, 2).reshape(feed_up.shape)
        down_all = lax.dynamic_update_slice_in_dim(down_all, down_part, core, 1).reshape(feed_down.shape)
        weight_grads = grads_self + grads_cross + [total(up_all), total(down_all)]
        length = width // dp_size

        def my_rows(array):
            return lax.dynamic_slice_in_dim(array, dp_at * length, length, 0).astype(FULL)

        def gain_total(pairs, gain):
            sums = sum(jnp.sum(my_rows(weight) * grad, axis=1) for weight, grad in pairs)
            return sums / my_rows(gain)

        gain_grads = [
            gain_total(zip((query_self, key_self, value_self), grads_self), gain_self),
            gain_total([(query_cross, grads_cross[0])], gain_cross),
            gain_total([(feed_up, weight_grads[8])], gain_feed),
        ]
    return (layer_out, input_grad, encoder_grad, *weight_grads, *gain_grads)


def solution(mesh):
    in_specs = (
        P(("dp", "layer"), None),
        P("layer", "dp", None),
        *[P()] * 13,
        P(("dp", "layer"), None),
        P(("dp", "layer"), None),
        P("dp"),
        P(),
        P(("dp", "layer"), None),
    )
    out_specs = (
        P(("dp", "layer"), None),
        P(("dp", "layer"), None),
        P("layer", "dp", None),
        *[P("dp", None)] * 10,
        *[P("dp")] * 3,
    )
    body = functools.partial(on_device, mesh.shape["layer"], mesh.shape["dp"])
    return jax.shard_map(
        body, mesh=mesh, in_specs=in_specs, out_specs=out_specs, check_vma=False
    )
```
